32 devices in a mesh: clip: 4 (over y, core), seq: 8 (over z, x).
Axes of the slice: x: 2, y: 2, z: 4, core: 2. Of those that a mesh axis runs over, the one named last changes fastest.
Arguments:
- tokens: bfloat16 [4, 1024, 1536], P('clip', 'seq'), may hold values from -6 to 6
- caption: bfloat16 [4, 128, 4096], P('clip', 'seq'), may hold values from -6 to 6
- condition: bfloat16 [4, 1024], P('clip'), may hold values from -6 to 6
- caption_len: int32 [4], P('clip'), may hold values from 32 to 128, as said below
- frame_shape: int32 [4, 3], P('clip'), may hold values from 2 to 32, as said below
- rope_shift: int32 [4, 3], P('clip'), may hold values from 0 to 64
- w_modulation: bfloat16 [1024, 6144], P(('clip', 'seq')), may hold values from -0.1875 to 0.1875
- mod_bias: bfloat16 [6144], P(('clip', 'seq')), may hold values from -3 to 3
- w_attention: bfloat16 [1536, 4608], P(('clip', 'seq')), may hold values from -0.15625 to 0.15625
- w_output: bfloat16 [1536, 1536], P(('clip', 'seq')), may hold values from -0.15625 to 0.15625
- w_caption: bfloat16 [4096, 3072], P(('clip', 'seq')), may hold values from -0.09375 to 0.09375
- norm_gains: bfloat16 [7, 1536], P(None, ('clip', 'seq')), may hold values from 0.099609375 to 1.8984375
- head_gate: bfloat16 [24], replicated, may hold values from -1.5 to 1.5
- w_gateup: bfloat16 [1536, 8192], P(('clip', 'seq')), may hold values from -0.15625 to 0.15625
- w_down: bfloat16 [4096, 1536], P(('clip', 'seq')), may hold values from -0.09375 to 0.09375
- cotangent: bfloat16 [4, 1024, 1536], P('clip', 'seq'), may hold values from -6 to 6
Outputs:
- block_out: float32 [4, 1024, 1536], P('clip', 'seq')
- grad_tokens: float32 [4, 1024, 1536], P('clip', 'seq')
- grad_caption: float32 [4, 128, 4096], P('clip', 'seq')
- grad_condition: float32 [4, 1024], P('clip')
- grad_w_modulation: float32 [1024, 6144], P(('clip', 'seq'))
- grad_mod_bias: float32 [6144], P(('clip', 'seq'))
- grad_w_attention: float32 [1536, 4608], P(('clip', 'seq'))
- grad_w_output: float32 [1536, 1536], P(('clip', 'seq'))
- grad_w_caption: float32 [4096, 3072], P(('clip', 'seq'))
- grad_norm_gains: float32 [7, 1536], P(None, ('clip', 'seq'))
- grad_head_gate: float32 [24], replicated
- grad_w_gateup: float32 [1536, 8192], P(('clip', 'seq'))
- grad_w_down: float32 [4096, 1536], P(('clip', 'seq'))
The draws below stay inside these ranges and needn't reach their ends.
Inputs may be any that keep to these rules, and one draw needn't show every extreme that they name: `caption_len`: one clip, which one drawn from the seed, uses all 128 caption tokens; every other clip uses fewer. `frame_shape`: per clip (frames, height, width): width + 1 is 8, 16 or 32, height is 4 to 16, and frames is the least number with frames * height * (width + 1) >= 1024; the first clip has width 7 and height 4, the second width 31 and height 16.
All inputs are finite; a program needn't handle non-finite values.
Results may differ from the reference program's by a relative error of at most 0.023.
Values may be sent and summed in bfloat16 or wider, within the bound.
No kernel may reach another device: no remote copies, remote signals or barrier semaphores. Data moves between devices by JAX's collectives and lax.ppermute only.
A program may use at most 448 MiB of HBM per device.

```python
import math
import jax
import jax.numpy as jnp
from jax import lax

D = 1536
H = 24
FF = 4096
TD = 4096
CD = 1024
TXT = 128
LENGTH = 1024
CLIPS = 4


def draw_frame_shape(key, part):
    key = jax.random.fold_in(key, 11)
    first_key, second_key = jax.random.split(key)
    shift_power = jax.random.randint(first_key, (CLIPS,), 3, 6)
    height = jax.random.randint(second_key, (CLIPS,), 4, 17)
    slot_index = jnp.arange(CLIPS, dtype=jnp.int32)
    shift_power = jnp.where(slot_index == 0, 3, jnp.where(slot_index == 1, 5, shift_power))
    height = jnp.where(slot_index == 0, 4, jnp.where(slot_index == 1, 16, height))
    across = jnp.left_shift(jnp.ones((CLIPS,), jnp.int32), shift_power)
    plane_size = height * across
    frames = (LENGTH + plane_size - 1) // plane_size
    return jnp.stack([frames, height, across - 1], axis=1).astype(jnp.int32)


def draw_caption_len(key, part):
    key = jax.random.fold_in(key, 23)
    first_key, second_key = jax.random.split(key)
    lengths = jax.random.randint(first_key, (CLIPS,), TXT // 4, TXT)
    chosen = jax.random.randint(second_key, (), 0, CLIPS)
    slot_index = jnp.arange(CLIPS, dtype=jnp.int32)
    return jnp.where(slot_index == chosen, TXT, lengths).astype(jnp.int32)


def plant(values, rng, least, largest):
    longest = values.shape.index(max(values.shape))
    spots = []
    for shift in (0, 1):
        where = [jax.random.randint(jax.random.fold_in(rng, axis), (), 0, length) for axis, length in enumerate(values.shape)]
        where[longest] = (where[longest] + shift) % values.shape[longest]
        spots.append(tuple(where))
    return values.at[spots[0]].set(least).at[spots[1]].set(largest)


def block_scale(rng, shape, shards, smallest, largest):
    level, own = 1.0, jax.random.fold_in(rng, 6)
    for axis_at, parts in shards:
        heights = jnp.exp(jax.random.uniform(jax.random.fold_in(own, axis_at), (parts,), jnp.float32, smallest / len(shards), largest / len(shards)))
        level = level * jnp.repeat(heights, shape[axis_at] // parts).reshape([-1 if axis == axis_at else 1 for axis in range(len(shape))])
    return level


def normal_values(rng, extent, width, reach, cuts=(), kind=jnp.bfloat16):
    drawn = width * jax.random.normal(rng, extent, jnp.float32)
    if cuts:
        drawn = drawn * block_scale(rng, extent, cuts, -0.22, 0.18)
    return jnp.clip(drawn, -reach, reach).astype(kind)


def setup_inputs(seed: int = 0) -> dict:
    key_list = jax.random.split(jax.random.key(seed), 17)
    return {
        "tokens": normal_values(key_list[0], (CLIPS, LENGTH, D), 1.0, 6.0, ((0, 4), (1, 8))),
        "caption": normal_values(key_list[1], (CLIPS, TXT, TD), 1.0, 6.0, ((0, 4), (1, 8))),
        "condition": normal_values(key_list[2], (CLIPS, CD), 1.0, 6.0, ((0, 4),)),
        "caption_len": draw_caption_len(jax.random.fold_in(key_list[16], 71), 0),
        "frame_shape": draw_frame_shape(jax.random.fold_in(key_list[16], 71), 0),
        "rope_shift": plant(jax.random.randint(key_list[5], (CLIPS, 3), 0, 65), jax.random.fold_in(key_list[5], 1), 0, 64).astype(jnp.int32),
        "w_modulation": normal_values(key_list[6], (CD, 4 * D), CD ** -0.5, 0.1875, ((0, 32),)),
        "mod_bias": normal_values(key_list[7], (4 * D,), 0.5, 3.0, ((0, 32),)),
        "w_attention": normal_values(key_list[8], (D, 3 * D), D ** -0.5, 0.15625, ((0, 32),)),
        "w_output": normal_values(key_list[9], (D, D), D ** -0.5, 0.15625, ((0, 32),)),
        "w_caption": normal_values(key_list[10], (TD, 2 * D), TD ** -0.5, 0.09375, ((0, 32),)),
        "norm_gains": jnp.clip(1.0 + 0.18 * jax.random.normal(key_list[11], (7, D), jnp.float32), 0.099609375, 1.8984375).astype(jnp.bfloat16),
        "head_gate": jnp.clip(jax.random.uniform(key_list[12], (H,), jnp.float32, -1.5, 1.5), -1.5, 1.5).astype(jnp.bfloat16),
        "w_gateup": normal_values(key_list[13], (D, 2 * FF), D ** -0.5, 0.15625, ((0, 32),)),
        "w_down": normal_values(key_list[14], (FF, D), FF ** -0.5, 0.09375, ((0, 32),)),
        "cotangent": normal_values(key_list[15], (CLIPS, LENGTH, D), 1.0, 6.0, ((0, 4), (1, 8))),
    }


@jax.custom_vjp
def low(v):
    return lax.optimization_barrier(v.astype(jnp.bfloat16)).astype(jnp.float32)

@jax.custom_vjp
def low_back(v):
    return v

def low_keep(v):
    return (low(v), None)

def low_pass(kept, grad):
    return (grad,)

def back_keep(v):
    return (v, None)

def back_low(kept, grad):
    return (low(grad),)
low.defvjp(low_keep, low_pass)
low_back.defvjp(back_keep, back_low)
epsilon = 1e-06
theta_base = 10000.0
highest = lax.Precision.HIGHEST

def rms_norm(value):
    return value * lax.rsqrt(lax.optimization_barrier(jnp.mean(value * value, axis=-1, keepdims=True)) + epsilon)

def rope_angles(shape_row, shift_row, position, half_dim):
    across = shape_row[2] + 1
    column_place = position % across + shift_row[2]
    row_place = position // across % shape_row[1] + shift_row[1]
    frame_place = position // (across * shape_row[1]) + shift_row[0]
    frame_count = half_dim // 4
    row_count = 3 * half_dim // 8
    column_count = half_dim - frame_count - row_count
    pieces = []
    for place_index, group_size in ((frame_place, frame_count), (row_place, row_count), (column_place, column_count)):
        frequency = theta_base ** (-jnp.arange(group_size, dtype=jnp.float32) / group_size)
        pieces.append(place_index.astype(jnp.float32)[:, None] * frequency[None, :])
    return jnp.concatenate(pieces, axis=1)

def rotate(value, cosine, sine_table):
    half_dim = value.shape[-1] // 2
    front_half = value[..., :half_dim]
    back_half = value[..., half_dim:]
    return jnp.concatenate([front_half * cosine - back_half * sine_table, back_half * cosine + front_half * sine_table], axis=-1)

def soft_weights(scores):
    shifted = jnp.exp(scores - lax.optimization_barrier(jnp.max(scores, axis=-1, keepdims=True)))
    return shifted / lax.optimization_barrier(jnp.sum(shifted, axis=-1, keepdims=True))

def clip_layer(weights, block_in, caption_in, cond_in, clip_len, clip_shape, clip_shift):
    w_modulation, mod_bias, w_attention, w_output, w_caption, norm_gains, head_gate, w_gateup, w_down = weights
    length, model_width = block_in.shape
    head_count = head_gate.shape[0]
    head_dim = model_width // head_count
    hidden_units = w_down.shape[0]
    score_scale = head_dim ** (-0.5)
    modulation = jnp.dot(low(jax.nn.silu(cond_in))[None, :], w_modulation, precision=highest)[0] + mod_bias
    scale_attn = modulation[:model_width]
    gate_attn = jnp.tanh(modulation[model_width:2 * model_width])
    scale_ffn = modulation[2 * model_width:3 * model_width]
    gate_ffn = jnp.tanh(modulation[3 * model_width:])
    normed = low(rms_norm(block_in) * norm_gains[0] * (1.0 + scale_attn))
    projected = low_back(jnp.dot(normed, w_attention, precision=highest))
    angles = rope_angles(clip_shape, clip_shift, jnp.arange(length, dtype=jnp.int32), head_dim // 2)
    cosine = jnp.cos(angles)[:, None, :]
    sine_table = jnp.sin(angles)[:, None, :]
    split_shape = (length, head_count, head_dim)
    queries = low(rotate((rms_norm(projected[:, :model_width]) * norm_gains[4]).reshape(split_shape), cosine, sine_table))
    key_rows = low(rotate((rms_norm(projected[:, model_width:2 * model_width]) * norm_gains[5]).reshape(split_shape), cosine, sine_table))
    value_rows = low(projected[:, 2 * model_width:]).reshape(split_shape)
    text_proj = low_back(jnp.dot(caption_in, w_caption, precision=highest))
    text_keys = low(rms_norm(text_proj[:, :model_width]) * norm_gains[6]).reshape(-1, head_count, head_dim)
    text_values = low(text_proj[:, model_width:]).reshape(-1, head_count, head_dim)
    usable = jnp.arange(caption_in.shape[0], dtype=jnp.int32) < clip_len
    tanh_gate = jnp.tanh(head_gate)
    block_len = math.gcd(length, 512)

    def attend(query_block):
        scores = low_back(jnp.einsum('qhd,khd->hqk', query_block, key_rows, precision=highest) * score_scale)
        self_out = jnp.einsum('hqk,khd->qhd', low(soft_weights(scores)), value_rows, precision=highest)
        text_scores = low_back(jnp.einsum('qhd,khd->hqk', query_block, text_keys, precision=highest) * score_scale)
        text_scores = jnp.where(usable[None, None, :], text_scores, -1e+30)
        cross_out = jnp.einsum('hqk,khd->qhd', low(soft_weights(text_scores)), text_values, precision=highest)
        return self_out + tanh_gate[None, :, None] * cross_out
    mixed_heads = lax.map(jax.checkpoint(attend), queries.reshape(length // block_len, block_len, head_count, head_dim))
    mixed_heads = low_back(low(mixed_heads.reshape(length, model_width)))
    attn_proj = low_back(jnp.dot(mixed_heads, w_output, precision=highest))
    residual = block_in + gate_attn * rms_norm(attn_proj) * norm_gains[1]
    normed_ffn = low(rms_norm(residual) * norm_gains[2] * (1.0 + scale_ffn))
    gate_up = low_back(jnp.dot(normed_ffn, w_gateup, precision=highest))
    activated = low(jax.nn.silu(gate_up[:, :hidden_units]) * gate_up[:, hidden_units:])
    down_proj = low_back(jnp.dot(activated, w_down, precision=highest))
    return residual + gate_ffn * rms_norm(down_proj) * norm_gains[3]

def reference(tokens, caption, condition, caption_len, frame_shape, rope_shift, w_modulation, mod_bias, w_attention, w_output, w_caption, norm_gains, head_gate, w_gateup, w_down, cotangent):
    params = tuple((weight.astype(jnp.float32) for weight in (w_modulation, mod_bias, w_attention, w_output, w_caption, norm_gains, head_gate, w_gateup, w_down)))

    def one_clip(totals, clip_items):
        clip_tokens, clip_caption, clip_cond, clip_len, clip_shape, clip_shift, clip_cot = clip_items

        def forward(weights, block_in, caption_in, cond_in):
            return clip_layer(weights, block_in, caption_in, cond_in, clip_len, clip_shape, clip_shift)
        result, pullback = jax.vjp(forward, params, clip_tokens.astype(jnp.float32), clip_caption.astype(jnp.float32), clip_cond.astype(jnp.float32))
        gradients = pullback(clip_cot.astype(jnp.float32))
        totals = jax.tree.map(jnp.add, totals, gradients[0])
        return (totals, (result, gradients[1], gradients[2], gradients[3]))
    zero_totals = jax.tree.map(jnp.zeros_like, params)
    totals, per_clip = lax.scan(one_clip, zero_totals, (tokens, caption, condition, caption_len, frame_shape, rope_shift, cotangent))
    return (per_clip[0], per_clip[1], per_clip[2], per_clip[3], totals[0], totals[1], totals[2], totals[3], totals[4], totals[5], totals[6], totals[7], totals[8])
```

```python
import math

import jax
import jax.numpy as jnp
from jax import lax
from jax.sharding import Mesh
from jax.sharding import PartitionSpec as P

epsilon = 1e-06
theta_base = 10000.0
highest = lax.Precision.HIGHEST
bf16 = jnp.bfloat16
f32 = jnp.float32


def rms_norm(value):
    return value * lax.rsqrt(jnp.mean(value * value, axis=-1, keepdims=True) + epsilon)


def rms_back(value, upstream):
    return jax.vjp(rms_norm, value)[1](upstream)[0]


def rope_angles(shape_row, shift_row, position, half_dim):
    across = shape_row[2] + 1
    column_place = position % across + shift_row[2]
    row_place = position // across % shape_row[1] + shift_row[1]
    frame_place = position // (across * shape_row[1]) + shift_row[0]
    frame_count = half_dim // 4
    row_count = 3 * half_dim // 8
    column_count = half_dim - frame_count - row_count
    pieces = []
    for place_index, group_size in (
        (frame_place, frame_count),
        (row_place, row_count),
        (column_place, column_count),
    ):
        frequency = theta_base ** (-jnp.arange(group_size, dtype=jnp.float32) / group_size)
        pieces.append(place_index.astype(jnp.float32)[:, None] * frequency[None, :])
    return jnp.concatenate(pieces, axis=1)


def rotate(value, cosine, sine_table):
    half_dim = value.shape[-1] // 2
    front_half = value[..., :half_dim]
    back_half = value[..., half_dim:]
    return jnp.concatenate(
        [
            front_half * cosine - back_half * sine_table,
            back_half * cosine + front_half * sine_table,
        ],
        axis=-1,
    )


def soft_weights(scores):
    shifted = jnp.exp(scores - jnp.max(scores, axis=-1, keepdims=True))
    return shifted / jnp.sum(shifted, axis=-1, keepdims=True)


def local(
    tokens,
    caption,
    condition,
    caption_len,
    frame_shape,
    rope_shift,
    w_modulation,
    mod_bias,
    w_attention,
    w_output,
    w_caption,
    norm_gains,
    head_gate,
    w_gateup,
    w_down,
    cotangent,
):
    clip_count, local_len, model_width = tokens.shape
    head_count = head_gate.shape[0]
    head_dim = model_width // head_count
    score_scale = head_dim ** (-0.5)
    row_total = clip_count * local_len
    text_local = caption.shape[1]
    text_total = text_local * lax.axis_size("seq")
    gathered = (
        lax.all_gather(w_modulation, ("clip", "seq"), axis=0, tiled=True),
        lax.all_gather(mod_bias, ("clip", "seq"), axis=0, tiled=True),
        lax.all_gather(w_attention, ("clip", "seq"), axis=0, tiled=True),
        lax.all_gather(w_output, ("clip", "seq"), axis=0, tiled=True),
        lax.all_gather(w_caption, ("clip", "seq"), axis=0, tiled=True),
        lax.all_gather(norm_gains, ("clip", "seq"), axis=1, tiled=True),
    )
    full_mod, full_bias, full_attn, full_out, full_caption, full_gains = gathered
    gain_rows = full_gains.astype(jnp.float32)
    tanh_gate = jnp.tanh(head_gate.astype(jnp.float32))
    cond_float = condition.astype(jnp.float32)
    cond_act = jax.nn.silu(cond_float).astype(jnp.bfloat16)
    modulation = jnp.dot(cond_act, full_mod, preferred_element_type=jnp.float32) + full_bias.astype(
        jnp.float32
    )
    scale_attn = modulation[:, None, :model_width]
    gate_attn = jnp.tanh(modulation[:, None, model_width : 2 * model_width])
    scale_ffn = modulation[:, None, 2 * model_width : 3 * model_width]
    gate_ffn = jnp.tanh(modulation[:, None, 3 * model_width :])
    token_float = tokens.astype(jnp.float32)
    token_normed = rms_norm(token_float)
    normed_flat = (
        (token_normed * gain_rows[0] * (1.0 + scale_attn))
        .astype(jnp.bfloat16)
        .reshape(row_total, model_width)
    )
    projected = jnp.dot(normed_flat, full_attn, preferred_element_type=jnp.float32).reshape(
        clip_count, local_len, 3 * model_width
    )
    query_pre = projected[..., :model_width]
    key_pre = projected[..., model_width : 2 * model_width]
    query_normed = rms_norm(query_pre)
    key_normed = rms_norm(key_pre)
    position = lax.axis_index("seq") * local_len + jnp.arange(local_len, dtype=jnp.int32)
    angles = jax.vmap(
        lambda shape_row, shift_row: rope_angles(shape_row, shift_row, position, head_dim // 2)
    )(frame_shape, rope_shift)
    cosine = jnp.cos(angles)[:, :, None, :]
    sine_table = jnp.sin(angles)[:, :, None, :]
    split_shape = (clip_count, local_len, head_count, head_dim)
    queries = rotate((query_normed * gain_rows[4]).reshape(split_shape), cosine, sine_table).astype(
        jnp.bfloat16
    )
    key_rows = rotate((key_normed * gain_rows[5]).reshape(split_shape), cosine, sine_table).astype(
        jnp.bfloat16
    )
    value_rows = projected[..., 2 * model_width :].reshape(split_shape).astype(jnp.bfloat16)
    caption_flat = caption.reshape(clip_count * text_local, caption.shape[2])
    text_proj = jnp.dot(caption_flat, full_caption, preferred_element_type=jnp.float32).reshape(
        clip_count, text_local, 2 * model_width
    )
    text_key_pre = text_proj[..., :model_width]
    text_key_normed = rms_norm(text_key_pre)
    text_shape = (clip_count, text_local, head_count, head_dim)
    text_keys = (text_key_normed * gain_rows[6]).astype(jnp.bfloat16).reshape(text_shape)
    text_values = text_proj[..., model_width:].astype(jnp.bfloat16).reshape(text_shape)
    all_text_keys, all_text_values = (
        lax.all_gather(text_keys, "seq", axis=1, tiled=True),
        lax.all_gather(text_values, "seq", axis=1, tiled=True),
    )
    stat_shape = (clip_count, head_count, local_len)
    start_stats = (jnp.full(stat_shape, -1e30, jnp.float32), jnp.zeros(stat_shape, jnp.float32))
    piece_keys = lax.all_gather(key_rows, "seq", axis=1, tiled=True)
    key_count = piece_keys.shape[1]
    block_len = math.gcd(key_count, 512)

    def stat_one_block(block_index, inner_state):
        row_max, row_sum = inner_state
        block_keys = lax.dynamic_slice_in_dim(piece_keys, block_index * block_len, block_len, 1)
        scores = (
            jnp.einsum("cqhd,ckhd->chqk", queries, block_keys, preferred_element_type=jnp.float32)
            * score_scale
        )
        new_max = jnp.maximum(row_max, jnp.max(scores, axis=-1))
        row_sum = row_sum * jnp.exp(row_max - new_max) + jnp.sum(
            jnp.exp(scores - new_max[..., None]), axis=-1
        )
        return (new_max, row_sum)

    row_max, row_sum = lax.fori_loop(0, key_count // block_len, stat_one_block, start_stats)
    log_sum = row_max + jnp.log(row_sum)
    attend_piece_keys = lax.all_gather(key_rows, "seq", axis=1, tiled=True)
    piece_values = lax.all_gather(value_rows, "seq", axis=1, tiled=True)
    key_count = attend_piece_keys.shape[1]
    attend_block_len = math.gcd(key_count, 512)

    def attend_one_block(block_index, weighted):
        block_keys = lax.dynamic_slice_in_dim(
            attend_piece_keys, block_index * attend_block_len, attend_block_len, 1
        )
        block_values = lax.dynamic_slice_in_dim(
            piece_values, block_index * attend_block_len, attend_block_len, 1
        )
        scores = (
            jnp.einsum("cqhd,ckhd->chqk", queries, block_keys, preferred_element_type=jnp.float32)
            * score_scale
        )
        probs = jnp.exp(scores - log_sum[..., None]).astype(jnp.bfloat16)
        return weighted + jnp.einsum(
            "chqk,ckhd->chqd", probs, block_values, preferred_element_type=jnp.float32
        )

    weighted = lax.fori_loop(
        0,
        key_count // attend_block_len,
        attend_one_block,
        jnp.zeros(stat_shape + (head_dim,), jnp.float32),
    )
    self_out = jnp.transpose(weighted, (0, 2, 1, 3))
    usable = jnp.arange(text_total, dtype=jnp.int32)[None, :] < caption_len[:, None]
    text_scores = (
        jnp.einsum("cqhd,ckhd->chqk", queries, all_text_keys, preferred_element_type=jnp.float32)
        * score_scale
    )
    text_scores = jnp.where(usable[:, None, None, :], text_scores, -1e30)
    text_weights = soft_weights(text_scores)
    text_low = text_weights.astype(jnp.bfloat16)
    cross_out = jnp.einsum(
        "chqk,ckhd->cqhd", text_low, all_text_values, preferred_element_type=jnp.float32
    )
    mixed_heads = self_out + tanh_gate[None, None, :, None] * cross_out
    mixed_flat = mixed_heads.reshape(row_total, model_width).astype(jnp.bfloat16)
    attn_proj = jnp.dot(mixed_flat, full_out, preferred_element_type=jnp.float32).reshape(
        clip_count, local_len, model_width
    )
    attn_normed = rms_norm(attn_proj)
    residual = token_float + gate_attn * attn_normed * gain_rows[1]
    full_gateup, full_down = (
        lax.all_gather(w_gateup, ("clip", "seq"), axis=0, tiled=True),
        lax.all_gather(w_down, ("clip", "seq"), axis=0, tiled=True),
    )
    hidden_units = full_down.shape[0]
    residual_normed = rms_norm(residual)
    normed_ffn = (
        (residual_normed * gain_rows[2] * (1.0 + scale_ffn))
        .astype(jnp.bfloat16)
        .reshape(row_total, model_width)
    )
    gate_up = jnp.dot(normed_ffn, full_gateup, preferred_element_type=jnp.float32)
    gate_part = gate_up[:, :hidden_units]
    up_part = gate_up[:, hidden_units:]
    gate_sigmoid = jax.nn.sigmoid(gate_part)
    activated = (gate_part * gate_sigmoid * up_part).astype(jnp.bfloat16)
    down_proj = jnp.dot(activated, full_down, preferred_element_type=jnp.float32).reshape(
        clip_count, local_len, model_width
    )
    down_normed = rms_norm(down_proj)
    block_out = residual + gate_ffn * down_normed * gain_rows[3]
    upstream = cotangent.astype(jnp.float32)
    gain_three = jnp.sum(upstream * gate_ffn * down_normed, axis=(0, 1))
    grad_gate_ffn = jnp.sum(upstream * down_normed * gain_rows[3], axis=1) * (
        1.0 - gate_ffn[:, 0] * gate_ffn[:, 0]
    )
    grad_down = (
        rms_back(down_proj, upstream * gate_ffn * gain_rows[3])
        .astype(jnp.bfloat16)
        .reshape(row_total, model_width)
    )
    full_gateup, full_down = (
        lax.all_gather(w_gateup, ("clip", "seq"), axis=0, tiled=True),
        lax.all_gather(w_down, ("clip", "seq"), axis=0, tiled=True),
    )
    wgrad_down = jnp.dot(activated.T, grad_down, preferred_element_type=jnp.float32)
    grad_act = jnp.dot(grad_down, full_down.T, preferred_element_type=jnp.float32)
    grad_gate_part = grad_act * up_part * gate_sigmoid * (1.0 + gate_part * (1.0 - gate_sigmoid))
    grad_up_part = grad_act * gate_part * gate_sigmoid
    grad_gate_up = jnp.concatenate([grad_gate_part, grad_up_part], axis=1).astype(jnp.bfloat16)
    wgrad_gateup = jnp.dot(normed_ffn.T, grad_gate_up, preferred_element_type=jnp.float32)
    grad_normed_ffn = jnp.dot(
        grad_gate_up, full_gateup.T, preferred_element_type=jnp.float32
    ).reshape(clip_count, local_len, model_width)
    gain_two = jnp.sum(grad_normed_ffn * residual_normed * (1.0 + scale_ffn), axis=(0, 1))
    grad_scale_ffn = jnp.sum(grad_normed_ffn * residual_normed * gain_rows[2], axis=1)
    grad_residual = upstream + rms_back(
        residual, grad_normed_ffn * gain_rows[2] * (1.0 + scale_ffn)
    )
    gain_one = jnp.sum(grad_residual * gate_attn * attn_normed, axis=(0, 1))
    grad_gate_attn = jnp.sum(grad_residual * attn_normed * gain_rows[1], axis=1) * (
        1.0 - gate_attn[:, 0] * gate_attn[:, 0]
    )
    grad_attn = (
        rms_back(attn_proj, grad_residual * gate_attn * gain_rows[1])
        .astype(jnp.bfloat16)
        .reshape(row_total, model_width)
    )
    full_mod, full_attn, full_out, full_caption = (
        lax.all_gather(w_modulation, ("clip", "seq"), axis=0, tiled=True),
        lax.all_gather(w_attention, ("clip", "seq"), axis=0, tiled=True),
        lax.all_gather(w_output, ("clip", "seq"), axis=0, tiled=True),
        lax.all_gather(w_caption, ("clip", "seq"), axis=0, tiled=True),
    )
    wgrad_output = jnp.dot(mixed_flat.T, grad_attn, preferred_element_type=jnp.float32)
    grad_mixed = (
        jnp.dot(grad_attn, full_out.T, preferred_element_type=jnp.float32)
        .reshape(split_shape)
        .astype(jnp.bfloat16)
    )
    grad_float = grad_mixed.astype(jnp.float32)
    grad_head_gate = jnp.sum(grad_float * cross_out, axis=(0, 1, 3)) * (1.0 - tanh_gate * tanh_gate)
    delta_rows = jnp.sum(grad_float * self_out, axis=-1)
    delta_heads = jnp.transpose(delta_rows, (0, 2, 1))
    lse_rows = jnp.transpose(log_sum, (0, 2, 1))
    text_grad = (
        jnp.einsum(
            "cqhd,ckhd->chqk", grad_mixed, all_text_values, preferred_element_type=jnp.float32
        )
        * tanh_gate[None, :, None, None]
    )
    text_center = jnp.sum(text_weights * text_grad, axis=-1, keepdims=True)
    grad_text_scores = (text_weights * (text_grad - text_center)).astype(jnp.bfloat16)
    grad_queries = (
        jnp.einsum(
            "chqk,ckhd->cqhd", grad_text_scores, all_text_keys, preferred_element_type=jnp.float32
        )
        * score_scale
    )
    grad_text_keys = (
        jnp.einsum("chqk,cqhd->ckhd", grad_text_scores, queries, preferred_element_type=jnp.float32)
        * score_scale
    )
    grad_text_values = (
        jnp.einsum("chqk,cqhd->ckhd", text_low, grad_mixed, preferred_element_type=jnp.float32)
        * tanh_gate[None, None, :, None]
    )
    text_back_keys, text_back_values = (
        lax.psum_scatter(
            grad_text_keys.astype(jnp.bfloat16), "seq", scatter_dimension=1, tiled=True
        ).astype(jnp.float32),
        lax.psum_scatter(
            grad_text_values.astype(jnp.bfloat16), "seq", scatter_dimension=1, tiled=True
        ).astype(jnp.float32),
    )
    query_piece_keys = lax.all_gather(key_rows, "seq", axis=1, tiled=True)
    query_piece_values = lax.all_gather(value_rows, "seq", axis=1, tiled=True)
    key_count = query_piece_keys.shape[1]
    query_block_len = math.gcd(key_count, 512)

    def query_one_block(block_index, inner_state):
        block_keys = lax.dynamic_slice_in_dim(
            query_piece_keys, block_index * query_block_len, query_block_len, 1
        )
        block_values = lax.dynamic_slice_in_dim(
            query_piece_values, block_index * query_block_len, query_block_len, 1
        )
        scores = (
            jnp.einsum("cqhd,ckhd->chqk", queries, block_keys, preferred_element_type=jnp.float32)
            * score_scale
        )
        probs = jnp.exp(scores - log_sum[..., None])
        grad_probs = jnp.einsum(
            "cqhd,ckhd->chqk", grad_mixed, block_values, preferred_element_type=jnp.float32
        )
        grad_scores = (probs * (grad_probs - delta_heads[..., None])).astype(jnp.bfloat16)
        return (
            inner_state
            + jnp.einsum(
                "chqk,ckhd->cqhd", grad_scores, block_keys, preferred_element_type=jnp.float32
            )
            * score_scale
        )

    grad_self_queries = lax.fori_loop(
        0, key_count // query_block_len, query_one_block, jnp.zeros(split_shape, jnp.float32)
    )
    grad_queries = grad_queries + grad_self_queries
    zero_grads = (jnp.zeros(split_shape, jnp.float32), jnp.zeros(split_shape, jnp.float32))
    piece_queries = lax.all_gather(queries.astype(jnp.float32), "seq", axis=1, tiled=True).astype(
        jnp.bfloat16
    )
    piece_grads = lax.all_gather(grad_float, "seq", axis=1, tiled=True).astype(jnp.bfloat16)
    piece_lse = lax.all_gather(lse_rows, "seq", axis=1, tiled=True)
    piece_delta = lax.all_gather(delta_rows, "seq", axis=1, tiled=True)
    query_count = piece_queries.shape[1]
    key_block_len = math.gcd(query_count, 512)

    def key_one_block(block_index, inner_state):
        grad_key_acc, grad_value_acc = inner_state
        block_queries = lax.dynamic_slice_in_dim(
            piece_queries, block_index * key_block_len, key_block_len, 1
        )
        block_grads = lax.dynamic_slice_in_dim(
            piece_grads, block_index * key_block_len, key_block_len, 1
        )
        block_lse = jnp.transpose(
            lax.dynamic_slice_in_dim(piece_lse, block_index * key_block_len, key_block_len, 1),
            (0, 2, 1),
        )
        block_delta = jnp.transpose(
            lax.dynamic_slice_in_dim(piece_delta, block_index * key_block_len, key_block_len, 1),
            (0, 2, 1),
        )
        scores = (
            jnp.einsum(
                "cqhd,ckhd->chqk", block_queries, key_rows, preferred_element_type=jnp.float32
            )
            * score_scale
        )
        probs = jnp.exp(scores - block_lse[..., None])
        grad_value_acc = grad_value_acc + jnp.einsum(
            "chqk,cqhd->ckhd",
            probs.astype(jnp.bfloat16),
            block_grads,
            preferred_element_type=jnp.float32,
        )
        grad_probs = jnp.einsum(
            "cqhd,ckhd->chqk", block_grads, value_rows, preferred_element_type=jnp.float32
        )
        grad_scores = (probs * (grad_probs - block_delta[..., None])).astype(jnp.bfloat16)
        grad_key_acc = (
            grad_key_acc
            + jnp.einsum(
                "chqk,cqhd->ckhd", grad_scores, block_queries, preferred_element_type=jnp.float32
            )
            * score_scale
        )
        return (grad_key_acc, grad_value_acc)

    grad_keys, grad_values = lax.fori_loop(
        0, query_count // key_block_len, key_one_block, zero_grads
    )
    flat_shape = (clip_count, local_len, model_width)
    grad_query_rot = rotate(grad_queries, cosine, -sine_table).reshape(flat_shape)
    grad_key_rot = rotate(grad_keys, cosine, -sine_table).reshape(flat_shape)
    gain_four = jnp.sum(grad_query_rot * query_normed, axis=(0, 1))
    gain_five = jnp.sum(grad_key_rot * key_normed, axis=(0, 1))
    grad_query_pre = rms_back(query_pre, grad_query_rot * gain_rows[4])
    grad_key_pre = rms_back(key_pre, grad_key_rot * gain_rows[5])
    grad_projected = (
        jnp.concatenate([grad_query_pre, grad_key_pre, grad_values.reshape(flat_shape)], axis=-1)
        .astype(jnp.bfloat16)
        .reshape(row_total, 3 * model_width)
    )
    wgrad_attention = jnp.dot(normed_flat.T, grad_projected, preferred_element_type=jnp.float32)
    grad_normed = jnp.dot(grad_projected, full_attn.T, preferred_element_type=jnp.float32).reshape(
        flat_shape
    )
    gain_zero = jnp.sum(grad_normed * token_normed * (1.0 + scale_attn), axis=(0, 1))
    grad_scale_attn = jnp.sum(grad_normed * token_normed * gain_rows[0], axis=1)
    grad_tokens = grad_residual + rms_back(
        token_float, grad_normed * gain_rows[0] * (1.0 + scale_attn)
    )
    grad_text_key_rows = text_back_keys.reshape(clip_count, text_local, model_width)
    gain_six = jnp.sum(grad_text_key_rows * text_key_normed, axis=(0, 1))
    grad_text_pre = rms_back(text_key_pre, grad_text_key_rows * gain_rows[6])
    grad_text_proj = (
        jnp.concatenate(
            [grad_text_pre, text_back_values.reshape(clip_count, text_local, model_width)], axis=-1
        )
        .astype(jnp.bfloat16)
        .reshape(clip_count * text_local, 2 * model_width)
    )
    wgrad_caption = jnp.dot(caption_flat.T, grad_text_proj, preferred_element_type=jnp.float32)
    grad_caption = jnp.dot(
        grad_text_proj, full_caption.T, preferred_element_type=jnp.float32
    ).reshape(clip_count, text_local, caption.shape[2])
    grad_mod_row = jnp.concatenate(
        [grad_scale_attn, grad_gate_attn, grad_scale_ffn, grad_gate_ffn], axis=1
    )
    bias_grad = jnp.sum(grad_mod_row, axis=0)
    wgrad_modulation = jnp.dot(cond_act.astype(jnp.float32).T, grad_mod_row, precision=highest)
    cond_sigmoid = jax.nn.sigmoid(cond_float)
    grad_cond_act = jnp.dot(grad_mod_row, full_mod.astype(jnp.float32).T, precision=highest)
    grad_cond_part = grad_cond_act * cond_sigmoid * (1.0 + cond_float * (1.0 - cond_sigmoid))
    gain_grads = jnp.stack(
        [gain_zero, gain_one, gain_two, gain_three, gain_four, gain_five, gain_six]
    )
    partial_owned = (
        lax.psum_scatter(
            wgrad_modulation.astype(jnp.bfloat16), "clip", scatter_dimension=0, tiled=True
        ).astype(jnp.float32),
        lax.psum_scatter(
            bias_grad.astype(jnp.bfloat16), "clip", scatter_dimension=0, tiled=True
        ).astype(jnp.float32),
        lax.psum_scatter(
            wgrad_attention.astype(jnp.bfloat16), "clip", scatter_dimension=0, tiled=True
        ).astype(jnp.float32),
        lax.psum_scatter(
            wgrad_output.astype(jnp.bfloat16), "clip", scatter_dimension=0, tiled=True
        ).astype(jnp.float32),
        lax.psum_scatter(
            wgrad_caption.astype(jnp.bfloat16), "clip", scatter_dimension=0, tiled=True
        ).astype(jnp.float32),
        lax.psum_scatter(
            gain_grads.astype(jnp.bfloat16), "clip", scatter_dimension=1, tiled=True
        ).astype(jnp.float32),
        lax.psum_scatter(
            wgrad_gateup.astype(jnp.bfloat16), "clip", scatter_dimension=0, tiled=True
        ).astype(jnp.float32),
        lax.psum_scatter(
            wgrad_down.astype(jnp.bfloat16), "clip", scatter_dimension=0, tiled=True
        ).astype(jnp.float32),
    )
    owned = (
        lax.psum_scatter(
            partial_owned[0].astype(jnp.bfloat16), "seq", scatter_dimension=0, tiled=True
        ).astype(jnp.float32),
        lax.psum_scatter(
            partial_owned[1].astype(jnp.bfloat16), "seq", scatter_dimension=0, tiled=True
        ).astype(jnp.float32),
        lax.psum_scatter(
            partial_owned[2].astype(jnp.bfloat16), "seq", scatter_dimension=0, tiled=True
        ).astype(jnp.float32),
        lax.psum_scatter(
            partial_owned[3].astype(jnp.bfloat16), "seq", scatter_dimension=0, tiled=True
        ).astype(jnp.float32),
        lax.psum_scatter(
            partial_owned[4].astype(jnp.bfloat16), "seq", scatter_dimension=0, tiled=True
        ).astype(jnp.float32),
        lax.psum_scatter(
            partial_owned[5].astype(jnp.bfloat16), "seq", scatter_dimension=1, tiled=True
        ).astype(jnp.float32),
        lax.psum_scatter(
            partial_owned[6].astype(jnp.bfloat16), "seq", scatter_dimension=0, tiled=True
        ).astype(jnp.float32),
        lax.psum_scatter(
            partial_owned[7].astype(jnp.bfloat16), "seq", scatter_dimension=0, tiled=True
        ).astype(jnp.float32),
    )
    grad_gate_total = lax.psum(grad_head_gate, ("clip", "seq"))
    grad_condition = lax.psum(grad_cond_part, "seq")
    return (
        block_out,
        grad_tokens,
        grad_caption,
        grad_condition,
        owned[0],
        owned[1],
        owned[2],
        owned[3],
        owned[4],
        owned[5],
        grad_gate_total,
        owned[6],
        owned[7],
    )


def flip(value, axis):
    return lax.ppermute(value, axis, [(0, 1), (1, 0)])


def from_ahead(value, axis, step):
    count = lax.axis_size(axis)
    return lax.ppermute(value, axis, [((i + step) % count, i) for i in range(count)])


def swap_z(value, bit):
    return lax.ppermute(value, "z", [(i, i ^ bit) for i in range(4)])


def sum_seq(value):
    value = value + flip(value, "x")
    value = value + swap_z(value, 1)
    return value + swap_z(value, 2)


def to_relative(value):
    value = jnp.where(lax.axis_index("x") == 0, value, value[:, ::-1])
    return jnp.roll(value, -lax.axis_index("z"), axis=0)


def to_absolute(value):
    value = jnp.where(lax.axis_index("x") == 0, value, value[:, ::-1])
    return jnp.roll(value, lax.axis_index("z"), axis=0)


def clip_relative(value):
    value = jnp.where(lax.axis_index("y") == 0, value, value[::-1])
    return jnp.where(lax.axis_index("core") == 0, value, value[:, ::-1])


def gather_plane(value):
    rows = value.shape[0]
    half = rows // 2
    from_x = flip(value, "x")
    from_y = flip(value, "y")
    far_front = flip(from_y[:half], "x")
    far_back = flip(from_x[half:], "y")
    four = jnp.concatenate([value, from_x, from_y, far_front, far_back], axis=0)
    return jnp.concatenate([four, flip(four, "core")], axis=0)


def scatter_plane(value):
    count = value.shape[0] // 2
    rows = count // 4
    half = rows // 2
    four = value[:count] + flip(value[count:].astype(bf16), "core").astype(f32)
    own, for_x, for_y, far = [four[i * rows : (i + 1) * rows] for i in range(4)]
    by_x = flip(jnp.concatenate([for_x[:half], far[:half]]).astype(bf16), "x").astype(f32)
    by_y = flip(jnp.concatenate([for_y[half:], far[half:]]).astype(bf16), "y").astype(f32)
    own = own + jnp.concatenate([by_x[:half], by_y[:half]])
    last_y = flip((for_y[:half] + by_x[half:]).astype(bf16), "y").astype(f32)
    last_x = flip((for_x[half:] + by_y[half:]).astype(bf16), "x").astype(f32)
    return own + jnp.concatenate([last_y, last_x])


def gather_seq(value):
    rows = value.shape[0]
    early = rows // 4
    rest = rows - early
    ahead = [from_ahead(value[early:], "z", k) for k in (1, 2, 3)]
    other = flip(value, "x")
    both = jnp.concatenate([value[:early], other[:early]], axis=0)
    early_ahead = [from_ahead(both, "z", k) for k in (1, 2, 3)]
    other_ahead = flip(jnp.concatenate(ahead, axis=0), "x")
    pieces = [value, other]
    for k in range(3):
        pieces += [
            early_ahead[k][:early],
            ahead[k],
            early_ahead[k][early:],
            other_ahead[k * rest : (k + 1) * rest],
        ]
    return jnp.concatenate(pieces, axis=0)


def scatter_seq(value):
    rows = value.shape[0] // 8
    early = rows // 4
    parts = value.reshape(4, 2, rows, value.shape[1])
    low = parts.astype(bf16)
    other = flip(low[1:, 1, early:], "x").astype(f32)
    front = [from_ahead(low[(4 - k) % 4, :, :early], "z", k).astype(f32) for k in (1, 2, 3)]
    front_sum = parts[0, :, :early] + front[0] + front[1] + front[2]
    back_sum = (parts[1:, 0, early:] + other).astype(bf16)
    back = [from_ahead(back_sum[3 - k], "z", k).astype(f32) for k in (1, 2, 3)]
    last = flip(jnp.concatenate([front_sum[1].astype(bf16), low[0, 1, early:]]), "x").astype(f32)
    out_front = front_sum[0] + last[:early]
    out_back = parts[0, 0, early:] + last[early:] + back[0] + back[1] + back[2]
    return jnp.concatenate([out_front, out_back])


def scatter_clip(value):
    pair = value[:2] + flip(value[2:], "y")
    return pair[0] + flip(pair[1], "core")


def gather_clip(value):
    pair = jnp.stack([value, flip(value, "core")])
    return jnp.concatenate([pair, flip(pair, "y")])


def rms_scale(square_mean):
    return lax.rsqrt(square_mean + epsilon)


def local_fast(
    tokens,
    caption,
    condition,
    caption_len,
    frame_shape,
    rope_shift,
    w_modulation,
    mod_bias,
    w_attention,
    w_output,
    w_caption,
    norm_gains,
    head_gate,
    w_gateup,
    w_down,
    cotangent,
):
    seq_axes = ("z", "x")
    clip_axes = ("y", "core")
    all_axes = clip_axes + seq_axes
    plane_axes = ("y", "core", "x")
    rows, width = tokens.shape[1:]
    total = rows * 8
    heads = head_gate.shape[0]
    head_dim = width // heads
    own_heads = heads // 8
    cols = own_heads * head_dim
    score_scale = head_dim ** (-0.5)
    text_rows = caption.shape[1]
    text_total = text_rows * 8
    z_at, x_at = lax.axis_index("z"), lax.axis_index("x")
    seq_at = z_at * 2 + x_at
    owner = (lax.axis_index("y") * 2 + lax.axis_index("core")) * 8 + seq_at

    own_tokens = tokens[0]
    token_all = gather_seq(own_tokens)

    attn_piece = jnp.transpose(
        w_attention.reshape(-1, 3, 8, cols), (2, 0, 1, 3)
    ).reshape(8, -1, 3 * cols)
    attn_piece = lax.all_to_all(attn_piece, seq_axes, 0, 0, tiled=True)
    attn_piece = attn_piece.reshape(1, 1, -1, 3 * cols)
    own_attn = gather_clip(attn_piece[0, 0]).reshape(2, 2, -1, 3 * cols)
    own_attn = clip_relative(own_attn).reshape(width, 3 * cols)

    cond_float = condition[0].astype(f32)
    cond_act = jax.nn.silu(cond_float).astype(bf16)
    cond_all = gather_clip(cond_act)
    cond_rows = w_modulation.shape[0]
    cond_own = lax.dynamic_slice_in_dim(cond_all, owner * cond_rows, cond_rows, 1)
    mod_part = jnp.dot(cond_own, w_modulation, preferred_element_type=f32)
    bias_len = mod_bias.shape[0]
    bias_wide = lax.dynamic_update_slice(
        jnp.zeros((4 * width,), f32), mod_bias.astype(f32), (owner * bias_len,)
    )
    mod_part = mod_part + bias_wide[None]
    gain_cols = norm_gains.shape[1]
    gain_wide = lax.dynamic_update_slice(
        jnp.zeros((7, width), f32), norm_gains.astype(f32), (0, owner * gain_cols)
    ).reshape(-1)
    sent = flip(jnp.concatenate([mod_part[2:].reshape(-1), gain_wide]), "y")
    mod_pair = mod_part[:2] + sent[: 8 * width].reshape(2, -1)
    gain_wide = gain_wide + sent[8 * width :]
    sent = flip(jnp.concatenate([mod_pair[1], gain_wide]), "core")
    small = sum_seq(jnp.concatenate([mod_pair[0], gain_wide]) + sent)
    modulation = small[: 4 * width].reshape(4, width)
    gain_rows = small[4 * width :].reshape(7, width)
    scale_attn = modulation[0]
    gate_attn = jnp.tanh(modulation[1])
    scale_ffn = modulation[2]
    gate_ffn = jnp.tanh(modulation[3])
    gain_query = lax.dynamic_slice_in_dim(gain_rows[4], seq_at * cols, cols)
    gain_key = lax.dynamic_slice_in_dim(gain_rows[5], seq_at * cols, cols)
    gain_text = lax.dynamic_slice_in_dim(gain_rows[6], seq_at * cols, cols)
    head_low = lax.dynamic_slice_in_dim(head_gate, seq_at * own_heads, own_heads)
    tanh_gate = jnp.tanh(head_low.astype(f32))

    hidden_own = w_down.shape[0]
    ffn_piece = jnp.transpose(
        w_gateup.reshape(-1, 2, 2, 2, 4, 2, hidden_own), (2, 3, 5, 0, 1, 4, 6)
    ).reshape(8, -1, 8 * hidden_own)
    ffn_piece = lax.all_to_all(ffn_piece, plane_axes, 0, 0, tiled=True)
    block = 2 * ffn_piece.shape[1]
    full_out = lax.all_gather(w_output, all_axes, axis=0, tiled=True)
    own_gateup = lax.all_gather(ffn_piece.reshape(4, block, -1), "z", axis=0)
    own_gateup = jnp.transpose(own_gateup, (1, 0, 2, 3)).reshape(width, -1)
    own_down = lax.all_gather(w_down, "z", axis=0, tiled=True)
    hidden = 4 * hidden_own

    cap_cols = w_caption.shape[0]
    cap_piece = jnp.transpose(caption[0].reshape(text_rows, 32, cap_cols), (1, 0, 2))
    cap_piece = lax.all_to_all(cap_piece, all_axes, 0, 0, tiled=True)
    cap_all = clip_relative(cap_piece.reshape(2, 2, text_total, cap_cols)).reshape(
        4 * text_total, cap_cols
    )
    cap_weight = to_relative(
        jnp.transpose(w_caption.reshape(cap_cols, 2, 4, 2, cols), (2, 3, 0, 1, 4))
    ).reshape(8, cap_cols, 2 * cols)
    text_part = jnp.einsum("tk,skn->tsn", cap_all, cap_weight, preferred_element_type=f32)
    text_part = text_part.reshape(4, text_total, 8, 2 * cols).astype(bf16)
    text_pair = text_part[:2].astype(f32) + flip(text_part[2:], "y").astype(f32)
    text_one = text_pair[0] + flip(text_pair[1].astype(bf16), "core").astype(f32)
    text_proj = scatter_seq(jnp.transpose(text_one, (1, 0, 2)).reshape(8 * text_total, 2 * cols))
    text_key_pre = text_proj[:, :cols]
    text_square = jnp.sum(text_key_pre * text_key_pre, axis=1)

    token_float = token_all.astype(f32)
    normed_all = (rms_norm(token_float) * gain_rows[0] * (1.0 + scale_attn)).astype(bf16)
    projected = jnp.dot(normed_all, own_attn, preferred_element_type=f32)
    projected = to_absolute(projected.reshape(4, 2, rows, 3 * cols)).reshape(total, 3 * cols)
    query_pre = projected[:, :cols]
    key_pre = projected[:, cols : 2 * cols]
    squares = jnp.concatenate(
        [jnp.sum(query_pre * query_pre, axis=1), jnp.sum(key_pre * key_pre, axis=1), text_square]
    )
    squares = sum_seq(squares) / width
    scales = rms_scale(squares)
    query_scale = scales[:total, None]
    key_scale = scales[total : 2 * total, None]
    text_scale = scales[2 * total :, None]
    query_normed = query_pre * query_scale
    key_normed = key_pre * key_scale
    text_key_normed = text_key_pre * text_scale
    position = jnp.arange(total, dtype=jnp.int32)
    angles = rope_angles(frame_shape[0], rope_shift[0], position, head_dim // 2)
    cosine = jnp.cos(angles)[:, None, :]
    sine_table = jnp.sin(angles)[:, None, :]
    split = (total, own_heads, head_dim)
    queries = rotate((query_normed * gain_query).reshape(split), cosine, sine_table).astype(bf16)
    key_rows = rotate((key_normed * gain_key).reshape(split), cosine, sine_table).astype(bf16)
    values = projected[:, 2 * cols :].reshape(split).astype(bf16)
    text_split = (text_total, own_heads, head_dim)
    text_keys = (text_key_normed * gain_text).astype(bf16).reshape(text_split)
    text_values = text_proj[:, cols:].astype(bf16).reshape(text_split)

    scores = jnp.einsum("qhd,khd->hqk", queries, key_rows, preferred_element_type=f32) * score_scale
    row_max = jnp.max(scores, axis=-1)
    log_sum = row_max + jnp.log(jnp.sum(jnp.exp(scores - row_max[..., None]), axis=-1))
    probs = jnp.exp(scores - log_sum[..., None])
    probs_low = probs.astype(bf16)
    self_out = jnp.einsum("hqk,khd->qhd", probs_low, values, preferred_element_type=f32)
    usable = jnp.arange(text_total, dtype=jnp.int32) < caption_len[0]
    text_scores = (
        jnp.einsum("qhd,khd->hqk", queries, text_keys, preferred_element_type=f32) * score_scale
    )
    text_weights = soft_weights(jnp.where(usable[None, None, :], text_scores, -1e30))
    text_low = text_weights.astype(bf16)
    cross_out = jnp.einsum("hqk,khd->qhd", text_low, text_values, preferred_element_type=f32)
    mixed = (self_out + tanh_gate[None, :, None] * cross_out).astype(bf16).reshape(total, cols)

    mixed_own = lax.all_to_all(mixed.reshape(8, rows, cols), seq_axes, 0, 0, tiled=True)
    mixed_own = jnp.transpose(mixed_own, (1, 0, 2)).reshape(rows, width)
    attn_proj = jnp.dot(mixed_own, full_out, preferred_element_type=f32)
    attn_scale = rms_scale(jnp.mean(attn_proj * attn_proj, axis=-1, keepdims=True))
    attn_normed = attn_proj * attn_scale
    own_float = own_tokens.astype(f32)
    token_scale = rms_scale(jnp.mean(own_float * own_float, axis=-1, keepdims=True))
    token_normed = own_float * token_scale
    residual = own_float + gate_attn * attn_normed * gain_rows[1]
    residual_scale = rms_scale(jnp.mean(residual * residual, axis=-1, keepdims=True))
    residual_normed = residual * residual_scale
    normed_ffn = (residual_normed * gain_rows[2] * (1.0 + scale_ffn)).astype(bf16)

    normed_ffn_all = gather_plane(normed_ffn)
    gate_up = jnp.dot(normed_ffn_all, own_gateup, preferred_element_type=f32)
    gate_part = gate_up[:, :hidden]
    up_part = gate_up[:, hidden:]
    gate_sigmoid = jax.nn.sigmoid(gate_part)
    activated = (gate_part * gate_sigmoid * up_part).astype(bf16)
    down_proj = scatter_plane(jnp.dot(activated, own_down, preferred_element_type=f32))
    down_scale = rms_scale(jnp.mean(down_proj * down_proj, axis=-1, keepdims=True))
    down_normed = down_proj * down_scale
    block_out = residual + gate_ffn * down_normed * gain_rows[3]

    upstream = cotangent[0].astype(f32)
    sum_three = jnp.sum(upstream * down_normed, axis=0)
    grad_in = upstream * gate_ffn * gain_rows[3]
    grad_down = (
        (grad_in - down_normed * jnp.mean(grad_in * down_normed, axis=-1, keepdims=True))
        * down_scale
    ).astype(bf16)
    grad_down_all = gather_plane(grad_down)
    wgrad_down = jnp.dot(activated.T, grad_down_all, preferred_element_type=f32)
    grad_act = jnp.dot(grad_down_all, own_down.T, preferred_element_type=f32)
    grad_gate_part = grad_act * up_part * gate_sigmoid * (1.0 + gate_part * (1.0 - gate_sigmoid))
    grad_up_part = grad_act * gate_part * gate_sigmoid
    grad_gate_up = jnp.concatenate([grad_gate_part, grad_up_part], axis=1).astype(bf16)
    grad_normed_ffn = scatter_plane(
        jnp.dot(grad_gate_up, own_gateup.T, preferred_element_type=f32)
    )
    wgrad_gateup = jnp.dot(normed_ffn_all.T, grad_gate_up, preferred_element_type=f32)
    wgrad_down = lax.psum_scatter(
        wgrad_down.astype(bf16), "z", scatter_dimension=0, tiled=True
    ).astype(f32)
    wgrad_gateup = jnp.transpose(
        wgrad_gateup.astype(bf16).reshape(4, 4, block, -1), (1, 0, 2, 3)
    )
    wgrad_gateup = lax.psum_scatter(wgrad_gateup, "z", scatter_dimension=0, tiled=False)
    wgrad_gateup = lax.all_to_all(
        wgrad_gateup.reshape(8, block // 2, -1), plane_axes, 0, 0, tiled=True
    )
    wgrad_gateup = (
        jnp.transpose(
            wgrad_gateup.reshape(2, 2, 2, block // 2, 2, 4, hidden_own), (3, 4, 0, 1, 5, 2, 6)
        )
        .reshape(block // 2, -1)
        .astype(f32)
    )

    sum_two = jnp.sum(grad_normed_ffn * residual_normed, axis=0)
    grad_in = grad_normed_ffn * gain_rows[2] * (1.0 + scale_ffn)
    grad_residual = (
        upstream
        + (grad_in - residual_normed * jnp.mean(grad_in * residual_normed, axis=-1, keepdims=True))
        * residual_scale
    )
    sum_one = jnp.sum(grad_residual * attn_normed, axis=0)
    grad_in = grad_residual * gate_attn * gain_rows[1]
    grad_attn = (
        (grad_in - attn_normed * jnp.mean(grad_in * attn_normed, axis=-1, keepdims=True))
        * attn_scale
    ).astype(bf16)
    grad_mixed_own = jnp.dot(grad_attn, full_out.T, preferred_element_type=f32).astype(bf16)
    grad_mixed = lax.all_to_all(
        jnp.transpose(grad_mixed_own.reshape(rows, 8, cols), (1, 0, 2)), seq_axes, 0, 0, tiled=True
    ).reshape(split)
    grad_attn_all = lax.all_gather(grad_attn, seq_axes, axis=0, tiled=True)
    wgrad_output = jnp.dot(mixed.T, grad_attn_all, preferred_element_type=f32)
    wgrad_output = wgrad_output.reshape(4, -1, width).astype(bf16)
    wgrad_output = scatter_clip_low(clip_relative(wgrad_output.reshape(2, 2, -1, width)))
    wgrad_output = lax.ppermute(
        wgrad_output,
        all_axes,
        [(c * 8 + s, 4 * s + c) for c in range(4) for s in range(8)],
    ).astype(f32)

    grad_float = grad_mixed.astype(f32)
    gate_sum = jnp.sum(grad_float * cross_out, axis=(0, 2)) * (1.0 - tanh_gate * tanh_gate)
    text_grad = (
        jnp.einsum("qhd,khd->hqk", grad_mixed, text_values, preferred_element_type=f32)
        * tanh_gate[:, None, None]
    )
    text_center = jnp.sum(text_weights * text_grad, axis=-1, keepdims=True)
    grad_text_scores = (text_weights * (text_grad - text_center)).astype(bf16)
    grad_text_keys = (
        jnp.einsum("hqk,qhd->khd", grad_text_scores, queries, preferred_element_type=f32)
        * score_scale
    ).reshape(text_total, cols)
    grad_text_values = (
        jnp.einsum("hqk,qhd->khd", text_low, grad_mixed, preferred_element_type=f32)
        * tanh_gate[None, :, None]
    ).reshape(text_total, cols)
    grad_queries = jnp.einsum(
        "hqk,khd->qhd", grad_text_scores, text_keys, preferred_element_type=f32
    )
    sum_six = jnp.sum(grad_text_keys * text_key_normed, axis=0)
    grad_in = grad_text_keys * gain_text
    text_mean = sum_seq(jnp.sum(grad_in * text_key_normed, axis=1)) / width
    grad_text_pre = (grad_in - text_key_normed * text_mean[:, None]) * text_scale
    grad_text_proj = jnp.concatenate([grad_text_pre, grad_text_values], axis=1).astype(bf16)
    text_seq = gather_seq(grad_text_proj).reshape(8, text_total, 2 * cols)
    text_all = jnp.concatenate([text_seq, flip(text_seq, "core")], axis=1)
    text_all = jnp.concatenate([text_all, flip(text_all, "y")], axis=1)
    wgrad_caption = jnp.einsum("tk,stn->skn", cap_all, text_all, preferred_element_type=f32)
    wgrad_caption = jnp.transpose(
        to_absolute(wgrad_caption.reshape(4, 2, cap_cols, 2, cols)), (2, 3, 0, 1, 4)
    ).reshape(cap_cols, 2 * width)
    grad_caption = jnp.einsum("stn,skn->tk", text_all, cap_weight, preferred_element_type=f32)
    grad_caption = clip_relative(grad_caption.reshape(2, 2, text_total, cap_cols))
    grad_caption = lax.all_to_all(
        grad_caption.reshape(32, text_rows, cap_cols), all_axes, 0, 0, tiled=True
    )
    grad_caption = jnp.transpose(grad_caption, (1, 0, 2)).reshape(1, text_rows, 32 * cap_cols)

    delta = jnp.sum(grad_float * self_out, axis=-1).T
    grad_values = jnp.einsum("hqk,qhd->khd", probs_low, grad_mixed, preferred_element_type=f32)
    grad_probs = jnp.einsum("qhd,khd->hqk", grad_mixed, values, preferred_element_type=f32)
    grad_scores = (probs * (grad_probs - delta[..., None])).astype(bf16)
    grad_keys = (
        jnp.einsum("hqk,qhd->khd", grad_scores, queries, preferred_element_type=f32) * score_scale
    )
    grad_queries = (
        grad_queries
        + jnp.einsum("hqk,khd->qhd", grad_scores, key_rows, preferred_element_type=f32)
    ) * score_scale
    grad_query_rot = rotate(grad_queries, cosine, -sine_table).reshape(total, cols)
    grad_key_rot = rotate(grad_keys, cosine, -sine_table).reshape(total, cols)
    sum_four = jnp.sum(grad_query_rot * query_normed, axis=0)
    sum_five = jnp.sum(grad_key_rot * key_normed, axis=0)
    query_in = grad_query_rot * gain_query
    key_in = grad_key_rot * gain_key
    means = sum_seq(
        jnp.concatenate(
            [jnp.sum(query_in * query_normed, axis=1), jnp.sum(key_in * key_normed, axis=1)]
        )
    ) / width
    grad_query_pre = (query_in - query_normed * means[:total, None]) * query_scale
    grad_key_pre = (key_in - key_normed * means[total:, None]) * key_scale
    grad_projected = jnp.concatenate(
        [grad_query_pre, grad_key_pre, grad_values.reshape(total, cols)], axis=1
    ).astype(bf16)
    grad_projected = to_relative(grad_projected.reshape(4, 2, rows, -1)).reshape(total, -1)
    grad_normed = scatter_seq(jnp.dot(grad_projected, own_attn.T, preferred_element_type=f32))
    wgrad_attention = jnp.dot(normed_all.T, grad_projected, preferred_element_type=f32)
    wgrad_attention = scatter_clip_low(
        clip_relative(wgrad_attention.astype(bf16).reshape(2, 2, width // 4, -1))
    )
    wgrad_attention = lax.all_to_all(
        wgrad_attention.reshape(8, -1, 3 * cols), seq_axes, 0, 0, tiled=True
    )
    wgrad_attention = (
        jnp.transpose(wgrad_attention.reshape(8, -1, 3, cols), (1, 2, 0, 3))
        .reshape(-1, 3 * width)
        .astype(f32)
    )
    sum_zero = jnp.sum(grad_normed * token_normed, axis=0)
    grad_in = grad_normed * gain_rows[0] * (1.0 + scale_attn)
    grad_tokens = (
        grad_residual
        + (grad_in - token_normed * jnp.mean(grad_in * token_normed, axis=-1, keepdims=True))
        * token_scale
    )

    wide = lax.dynamic_update_slice(
        jnp.zeros((3, width), f32),
        jnp.stack([sum_four, sum_five, sum_six]),
        (0, seq_at * cols),
    )
    gate_wide = lax.dynamic_update_slice(
        jnp.zeros((128,), f32), gate_sum, (seq_at * own_heads,)
    )
    sums = sum_seq(
        jnp.concatenate([sum_zero, sum_one, sum_two, sum_three, wide.reshape(-1), gate_wide])
    )
    sum_zero, sum_one, sum_two, sum_three = sums[: 4 * width].reshape(4, width)
    grad_mod_own = jnp.concatenate(
        [
            gain_rows[0] * sum_zero,
            gain_rows[1] * sum_one * (1.0 - gate_attn * gate_attn),
            gain_rows[2] * sum_two,
            gain_rows[3] * sum_three * (1.0 - gate_ffn * gate_ffn),
        ]
    )
    shared = jnp.concatenate(
        [
            (1.0 + scale_attn) * sum_zero,
            gate_attn * sum_one,
            (1.0 + scale_ffn) * sum_two,
            gate_ffn * sum_three,
            sums[4 * width :],
        ]
    )
    gathered = gather_clip(jnp.concatenate([grad_mod_own, shared]))
    grad_mod_row = gathered[:, : 4 * width]
    shared = (gathered[0] + gathered[1] + gathered[2] + gathered[3])[4 * width :]
    gain_grads = lax.dynamic_slice(
        shared[: 7 * width].reshape(7, width), (0, owner * gain_cols), (7, gain_cols)
    )
    grad_gate_total = shared[7 * width : 7 * width + heads]
    bias_grad = lax.dynamic_slice(
        jnp.sum(grad_mod_row, axis=0), (owner * bias_len,), (bias_len,)
    )
    wgrad_modulation = jnp.dot(cond_own.astype(f32).T, grad_mod_row, precision=highest)
    cond_back = jnp.dot(grad_mod_row, w_modulation.astype(f32).T, precision=highest)
    cond_wide = lax.dynamic_update_slice(
        jnp.zeros((4, cond_float.shape[0]), f32), cond_back, (0, owner * cond_rows)
    )
    cond_back = sum_seq(scatter_clip(cond_wide))
    cond_sigmoid = jax.nn.sigmoid(cond_float)
    grad_condition = cond_back * cond_sigmoid * (1.0 + cond_float * (1.0 - cond_sigmoid))

    return (
        block_out[None],
        grad_tokens[None],
        grad_caption,
        grad_condition[None],
        wgrad_modulation,
        bias_grad,
        wgrad_attention,
        wgrad_output,
        wgrad_caption,
        gain_grads,
        grad_gate_total,
        wgrad_gateup,
        wgrad_down,
    )


def scatter_clip_low(value):
    pair = value[0].astype(f32) + flip(value[1], "y").astype(f32)
    return (pair[0] + flip(pair[1].astype(bf16), "core").astype(f32)).astype(bf16)


def specs(clip, seq):
    both = clip + seq
    placed = (
        P(clip, seq, None),
        P(clip, seq, None),
        P(clip, None),
        P(clip),
        P(clip, None),
        P(clip, None),
        P(both, None),
        P(both),
        P(both, None),
        P(both, None),
        P(both, None),
        P(None, both),
        P(),
        P(both, None),
        P(both, None),
        P(clip, seq, None),
    )
    given = (
        P(clip, seq, None),
        P(clip, seq, None),
        P(clip, seq, None),
        P(clip, None),
        P(both, None),
        P(both),
        P(both, None),
        P(both, None),
        P(both, None),
        P(None, both),
        P(),
        P(both, None),
        P(both, None),
    )
    return placed, given


def solution(mesh):
    if dict(mesh.shape) == {"clip": 4, "seq": 8}:
        grid = Mesh(mesh.devices.reshape(2, 2, 4, 2), ("y", "core", "z", "x"))
        placed, given = specs(("y", "core"), ("z", "x"))
        return jax.shard_map(
            local_fast, mesh=grid, in_specs=placed, out_specs=given, check_vma=False
        )
    placed, given = specs(("clip",), ("seq",))
    return jax.shard_map(local, mesh=mesh, in_specs=placed, out_specs=given, check_vma=False)
```

```python
import functools
import math

import jax
import jax.numpy as jnp
from jax import lax
from jax.experimental import pallas as pl
from jax.experimental.pallas import tpu as pltpu
from jax.sharding import Mesh
from jax.sharding import PartitionSpec as P

epsilon = 1e-06
theta_base = 10000.0
highest = lax.Precision.HIGHEST
bf16 = jnp.bfloat16
f32 = jnp.float32


def rms_norm(value):
    return value * lax.rsqrt(jnp.mean(value * value, axis=-1, keepdims=True) + epsilon)


def rms_back(value, upstream):
    return jax.vjp(rms_norm, value)[1](upstream)[0]


def rope_angles(shape_row, shift_row, position, half_dim):
    across = shape_row[2] + 1
    column_place = position % across + shift_row[2]
    row_place = position // across % shape_row[1] + shift_row[1]
    frame_place = position // (across * shape_row[1]) + shift_row[0]
    frame_count = half_dim // 4
    row_count = 3 * half_dim // 8
    column_count = half_dim - frame_count - row_count
    pieces = []
    for place_index, group_size in (
        (frame_place, frame_count),
        (row_place, row_count),
        (column_place, column_count),
    ):
        frequency = theta_base ** (-jnp.arange(group_size, dtype=jnp.float32) / group_size)
        pieces.append(place_index.astype(jnp.float32)[:, None] * frequency[None, :])
    return jnp.concatenate(pieces, axis=1)


def rotate(value, cosine, sine_table):
    half_dim = value.shape[-1] // 2
    front_half = value[..., :half_dim]
    back_half = value[..., half_dim:]
    return jnp.concatenate(
        [
            front_half * cosine - back_half * sine_table,
            back_half * cosine + front_half * sine_table,
        ],
        axis=-1,
    )


def soft_weights(scores):
    shifted = jnp.exp(scores - jnp.max(scores, axis=-1, keepdims=True))
    return shifted / jnp.sum(shifted, axis=-1, keepdims=True)


def local(
    tokens,
    caption,
    condition,
    caption_len,
    frame_shape,
    rope_shift,
    w_modulation,
    mod_bias,
    w_attention,
    w_output,
    w_caption,
    norm_gains,
    head_gate,
    w_gateup,
    w_down,
    cotangent,
):
    clip_count, local_len, model_width = tokens.shape
    head_count = head_gate.shape[0]
    head_dim = model_width // head_count
    score_scale = head_dim ** (-0.5)
    row_total = clip_count * local_len
    text_local = caption.shape[1]
    text_total = text_local * lax.axis_size("seq")
    gathered = (
        lax.all_gather(w_modulation, ("clip", "seq"), axis=0, tiled=True),
        lax.all_gather(mod_bias, ("clip", "seq"), axis=0, tiled=True),
        lax.all_gather(w_attention, ("clip", "seq"), axis=0, tiled=True),
        lax.all_gather(w_output, ("clip", "seq"), axis=0, tiled=True),
        lax.all_gather(w_caption, ("clip", "seq"), axis=0, tiled=True),
        lax.all_gather(norm_gains, ("clip", "seq"), axis=1, tiled=True),
    )
    full_mod, full_bias, full_attn, full_out, full_caption, full_gains = gathered
    gain_rows = full_gains.astype(jnp.float32)
    tanh_gate = jnp.tanh(head_gate.astype(jnp.float32))
    cond_float = condition.astype(jnp.float32)
    cond_act = jax.nn.silu(cond_float).astype(jnp.bfloat16)
    modulation = jnp.dot(cond_act, full_mod, preferred_element_type=jnp.float32) + full_bias.astype(
        jnp.float32
    )
    scale_attn = modulation[:, None, :model_width]
    gate_attn = jnp.tanh(modulation[:, None, model_width : 2 * model_width])
    scale_ffn = modulation[:, None, 2 * model_width : 3 * model_width]
    gate_ffn = jnp.tanh(modulation[:, None, 3 * model_width :])
    token_float = tokens.astype(jnp.float32)
    token_normed = rms_norm(token_float)
    normed_flat = (
        (token_normed * gain_rows[0] * (1.0 + scale_attn))
        .astype(jnp.bfloat16)
        .reshape(row_total, model_width)
    )
    projected = jnp.dot(normed_flat, full_attn, preferred_element_type=jnp.float32).reshape(
        clip_count, local_len, 3 * model_width
    )
    query_pre = projected[..., :model_width]
    key_pre = projected[..., model_width : 2 * model_width]
    query_normed = rms_norm(query_pre)
    key_normed = rms_norm(key_pre)
    position = lax.axis_index("seq") * local_len + jnp.arange(local_len, dtype=jnp.int32)
    angles = jax.vmap(
        lambda shape_row, shift_row: rope_angles(shape_row, shift_row, position, head_dim // 2)
    )(frame_shape, rope_shift)
    cosine = jnp.cos(angles)[:, :, None, :]
    sine_table = jnp.sin(angles)[:, :, None, :]
    split_shape = (clip_count, local_len, head_count, head_dim)
    queries = rotate((query_normed * gain_rows[4]).reshape(split_shape), cosine, sine_table).astype(
        jnp.bfloat16
    )
    key_rows = rotate((key_normed * gain_rows[5]).reshape(split_shape), cosine, sine_table).astype(
        jnp.bfloat16
    )
    value_rows = projected[..., 2 * model_width :].reshape(split_shape).astype(jnp.bfloat16)
    caption_flat = caption.reshape(clip_count * text_local, caption.shape[2])
    text_proj = jnp.dot(caption_flat, full_caption, preferred_element_type=jnp.float32).reshape(
        clip_count, text_local, 2 * model_width
    )
    text_key_pre = text_proj[..., :model_width]
    text_key_normed = rms_norm(text_key_pre)
    text_shape = (clip_count, text_local, head_count, head_dim)
    text_keys = (text_key_normed * gain_rows[6]).astype(jnp.bfloat16).reshape(text_shape)
    text_values = text_proj[..., model_width:].astype(jnp.bfloat16).reshape(text_shape)
    all_text_keys, all_text_values = (
        lax.all_gather(text_keys, "seq", axis=1, tiled=True),
        lax.all_gather(text_values, "seq", axis=1, tiled=True),
    )
    stat_shape = (clip_count, head_count, local_len)
    start_stats = (jnp.full(stat_shape, -1e30, jnp.float32), jnp.zeros(stat_shape, jnp.float32))
    piece_keys = lax.all_gather(key_rows, "seq", axis=1, tiled=True)
    key_count = piece_keys.shape[1]
    block_len = math.gcd(key_count, 512)

    def stat_one_block(block_index, inner_state):
        row_max, row_sum = inner_state
        block_keys = lax.dynamic_slice_in_dim(piece_keys, block_index * block_len, block_len, 1)
        scores = (
            jnp.einsum("cqhd,ckhd->chqk", queries, block_keys, preferred_element_type=jnp.float32)
            * score_scale
        )
        new_max = jnp.maximum(row_max, jnp.max(scores, axis=-1))
        row_sum = row_sum * jnp.exp(row_max - new_max) + jnp.sum(
            jnp.exp(scores - new_max[..., None]), axis=-1
        )
        return (new_max, row_sum)

    row_max, row_sum = lax.fori_loop(0, key_count // block_len, stat_one_block, start_stats)
    log_sum = row_max + jnp.log(row_sum)
    attend_piece_keys = lax.all_gather(key_rows, "seq", axis=1, tiled=True)
    piece_values = lax.all_gather(value_rows, "seq", axis=1, tiled=True)
    key_count = attend_piece_keys.shape[1]
    attend_block_len = math.gcd(key_count, 512)

    def attend_one_block(block_index, weighted):
        block_keys = lax.dynamic_slice_in_dim(
            attend_piece_keys, block_index * attend_block_len, attend_block_len, 1
        )
        block_values = lax.dynamic_slice_in_dim(
            piece_values, block_index * attend_block_len, attend_block_len, 1
        )
        scores = (
            jnp.einsum("cqhd,ckhd->chqk", queries, block_keys, preferred_element_type=jnp.float32)
            * score_scale
        )
        probs = jnp.exp(scores - log_sum[..., None]).astype(jnp.bfloat16)
        return weighted + jnp.einsum(
            "chqk,ckhd->chqd", probs, block_values, preferred_element_type=jnp.float32
        )

    weighted = lax.fori_loop(
        0,
        key_count // attend_block_len,
        attend_one_block,
        jnp.zeros(stat_shape + (head_dim,), jnp.float32),
    )
    self_out = jnp.transpose(weighted, (0, 2, 1, 3))
    usable = jnp.arange(text_total, dtype=jnp.int32)[None, :] < caption_len[:, None]
    text_scores = (
        jnp.einsum("cqhd,ckhd->chqk", queries, all_text_keys, preferred_element_type=jnp.float32)
        * score_scale
    )
    text_scores = jnp.where(usable[:, None, None, :], text_scores, -1e30)
    text_weights = soft_weights(text_scores)
    text_low = text_weights.astype(jnp.bfloat16)
    cross_out = jnp.einsum(
        "chqk,ckhd->cqhd", text_low, all_text_values, preferred_element_type=jnp.float32
    )
    mixed_heads = self_out + tanh_gate[None, None, :, None] * cross_out
    mixed_flat = mixed_heads.reshape(row_total, model_width).astype(jnp.bfloat16)
    attn_proj = jnp.dot(mixed_flat, full_out, preferred_element_type=jnp.float32).reshape(
        clip_count, local_len, model_width
    )
    attn_normed = rms_norm(attn_proj)
    residual = token_float + gate_attn * attn_normed * gain_rows[1]
    full_gateup, full_down = (
        lax.all_gather(w_gateup, ("clip", "seq"), axis=0, tiled=True),
        lax.all_gather(w_down, ("clip", "seq"), axis=0, tiled=True),
    )
    hidden_units = full_down.shape[0]
    residual_normed = rms_norm(residual)
    normed_ffn = (
        (residual_normed * gain_rows[2] * (1.0 + scale_ffn))
        .astype(jnp.bfloat16)
        .reshape(row_total, model_width)
    )
    gate_up = jnp.dot(normed_ffn, full_gateup, preferred_element_type=jnp.float32)
    gate_part = gate_up[:, :hidden_units]
    up_part = gate_up[:, hidden_units:]
    gate_sigmoid = jax.nn.sigmoid(gate_part)
    activated = (gate_part * gate_sigmoid * up_part).astype(jnp.bfloat16)
    down_proj = jnp.dot(activated, full_down, preferred_element_type=jnp.float32).reshape(
        clip_count, local_len, model_width
    )
    down_normed = rms_norm(down_proj)
    block_out = residual + gate_ffn * down_normed * gain_rows[3]
    upstream = cotangent.astype(jnp.float32)
    gain_three = jnp.sum(upstream * gate_ffn * down_normed, axis=(0, 1))
    grad_gate_ffn = jnp.sum(upstream * down_normed * gain_rows[3], axis=1) * (
        1.0 - gate_ffn[:, 0] * gate_ffn[:, 0]
    )
    grad_down = (
        rms_back(down_proj, upstream * gate_ffn * gain_rows[3])
        .astype(jnp.bfloat16)
        .reshape(row_total, model_width)
    )
    full_gateup, full_down = (
        lax.all_gather(w_gateup, ("clip", "seq"), axis=0, tiled=True),
        lax.all_gather(w_down, ("clip", "seq"), axis=0, tiled=True),
    )
    wgrad_down = jnp.dot(activated.T, grad_down, preferred_element_type=jnp.float32)
    grad_act = jnp.dot(grad_down, full_down.T, preferred_element_type=jnp.float32)
    grad_gate_part = grad_act * up_part * gate_sigmoid * (1.0 + gate_part * (1.0 - gate_sigmoid))
    grad_up_part = grad_act * gate_part * gate_sigmoid
    grad_gate_up = jnp.concatenate([grad_gate_part, grad_up_part], axis=1).astype(jnp.bfloat16)
    wgrad_gateup = jnp.dot(normed_ffn.T, grad_gate_up, preferred_element_type=jnp.float32)
    grad_normed_ffn = jnp.dot(
        grad_gate_up, full_gateup.T, preferred_element_type=jnp.float32
    ).reshape(clip_count, local_len, model_width)
    gain_two = jnp.sum(grad_normed_ffn * residual_normed * (1.0 + scale_ffn), axis=(0, 1))
    grad_scale_ffn = jnp.sum(grad_normed_ffn * residual_normed * gain_rows[2], axis=1)
    grad_residual = upstream + rms_back(
        residual, grad_normed_ffn * gain_rows[2] * (1.0 + scale_ffn)
    )
    gain_one = jnp.sum(grad_residual * gate_attn * attn_normed, axis=(0, 1))
    grad_gate_attn = jnp.sum(grad_residual * attn_normed * gain_rows[1], axis=1) * (
        1.0 - gate_attn[:, 0] * gate_attn[:, 0]
    )
    grad_attn = (
        rms_back(attn_proj, grad_residual * gate_attn * gain_rows[1])
        .astype(jnp.bfloat16)
        .reshape(row_total, model_width)
    )
    full_mod, full_attn, full_out, full_caption = (
        lax.all_gather(w_modulation, ("clip", "seq"), axis=0, tiled=True),
        lax.all_gather(w_attention, ("clip", "seq"), axis=0, tiled=True),
        lax.all_gather(w_output, ("clip", "seq"), axis=0, tiled=True),
        lax.all_gather(w_caption, ("clip", "seq"), axis=0, tiled=True),
    )
    wgrad_output = jnp.dot(mixed_flat.T, grad_attn, preferred_element_type=jnp.float32)
    grad_mixed = (
        jnp.dot(grad_attn, full_out.T, preferred_element_type=jnp.float32)
        .reshape(split_shape)
        .astype(jnp.bfloat16)
    )
    grad_float = grad_mixed.astype(jnp.float32)
    grad_head_gate = jnp.sum(grad_float * cross_out, axis=(0, 1, 3)) * (1.0 - tanh_gate * tanh_gate)
    delta_rows = jnp.sum(grad_float * self_out, axis=-1)
    delta_heads = jnp.transpose(delta_rows, (0, 2, 1))
    lse_rows = jnp.transpose(log_sum, (0, 2, 1))
    text_grad = (
        jnp.einsum(
            "cqhd,ckhd->chqk", grad_mixed, all_text_values, preferred_element_type=jnp.float32
        )
        * tanh_gate[None, :, None, None]
    )
    text_center = jnp.sum(text_weights * text_grad, axis=-1, keepdims=True)
    grad_text_scores = (text_weights * (text_grad - text_center)).astype(jnp.bfloat16)
    grad_queries = (
        jnp.einsum(
            "chqk,ckhd->cqhd", grad_text_scores, all_text_keys, preferred_element_type=jnp.float32
        )
        * score_scale
    )
    grad_text_keys = (
        jnp.einsum("chqk,cqhd->ckhd", grad_text_scores, queries, preferred_element_type=jnp.float32)
        * score_scale
    )
    grad_text_values = (
        jnp.einsum("chqk,cqhd->ckhd", text_low, grad_mixed, preferred_element_type=jnp.float32)
        * tanh_gate[None, None, :, None]
    )
    text_back_keys, text_back_values = (
        lax.psum_scatter(
            grad_text_keys.astype(jnp.bfloat16), "seq", scatter_dimension=1, tiled=True
        ).astype(jnp.float32),
        lax.psum_scatter(
            grad_text_values.astype(jnp.bfloat16), "seq", scatter_dimension=1, tiled=True
        ).astype(jnp.float32),
    )
    query_piece_keys = lax.all_gather(key_rows, "seq", axis=1, tiled=True)
    query_piece_values = lax.all_gather(value_rows, "seq", axis=1, tiled=True)
    key_count = query_piece_keys.shape[1]
    query_block_len = math.gcd(key_count, 512)

    def query_one_block(block_index, inner_state):
        block_keys = lax.dynamic_slice_in_dim(
            query_piece_keys, block_index * query_block_len, query_block_len, 1
        )
        block_values = lax.dynamic_slice_in_dim(
            query_piece_values, block_index * query_block_len, query_block_len, 1
        )
        scores = (
            jnp.einsum("cqhd,ckhd->chqk", queries, block_keys, preferred_element_type=jnp.float32)
            * score_scale
        )
        probs = jnp.exp(scores - log_sum[..., None])
        grad_probs = jnp.einsum(
            "cqhd,ckhd->chqk", grad_mixed, block_values, preferred_element_type=jnp.float32
        )
        grad_scores = (probs * (grad_probs - delta_heads[..., None])).astype(jnp.bfloat16)
        return (
            inner_state
            + jnp.einsum(
                "chqk,ckhd->cqhd", grad_scores, block_keys, preferred_element_type=jnp.float32
            )
            * score_scale
        )

    grad_self_queries = lax.fori_loop(
        0, key_count // query_block_len, query_one_block, jnp.zeros(split_shape, jnp.float32)
    )
    grad_queries = grad_queries + grad_self_queries
    zero_grads = (jnp.zeros(split_shape, jnp.float32), jnp.zeros(split_shape, jnp.float32))
    piece_queries = lax.all_gather(queries.astype(jnp.float32), "seq", axis=1, tiled=True).astype(
        jnp.bfloat16
    )
    piece_grads = lax.all_gather(grad_float, "seq", axis=1, tiled=True).astype(jnp.bfloat16)
    piece_lse = lax.all_gather(lse_rows, "seq", axis=1, tiled=True)
    piece_delta = lax.all_gather(delta_rows, "seq", axis=1, tiled=True)
    query_count = piece_queries.shape[1]
    key_block_len = math.gcd(query_count, 512)

    def key_one_block(block_index, inner_state):
        grad_key_acc, grad_value_acc = inner_state
        block_queries = lax.dynamic_slice_in_dim(
            piece_queries, block_index * key_block_len, key_block_len, 1
        )
        block_grads = lax.dynamic_slice_in_dim(
            piece_grads, block_index * key_block_len, key_block_len, 1
        )
        block_lse = jnp.transpose(
            lax.dynamic_slice_in_dim(piece_lse, block_index * key_block_len, key_block_len, 1),
            (0, 2, 1),
        )
        block_delta = jnp.transpose(
            lax.dynamic_slice_in_dim(piece_delta, block_index * key_block_len, key_block_len, 1),
            (0, 2, 1),
        )
        scores = (
            jnp.einsum(
                "cqhd,ckhd->chqk", block_queries, key_rows, preferred_element_type=jnp.float32
            )
            * score_scale
        )
        probs = jnp.exp(scores - block_lse[..., None])
        grad_value_acc = grad_value_acc + jnp.einsum(
            "chqk,cqhd->ckhd",
            probs.astype(jnp.bfloat16),
            block_grads,
            preferred_element_type=jnp.float32,
        )
        grad_probs = jnp.einsum(
            "cqhd,ckhd->chqk", block_grads, value_rows, preferred_element_type=jnp.float32
        )
        grad_scores = (probs * (grad_probs - block_delta[..., None])).astype(jnp.bfloat16)
        grad_key_acc = (
            grad_key_acc
            + jnp.einsum(
                "chqk,cqhd->ckhd", grad_scores, block_queries, preferred_element_type=jnp.float32
            )
            * score_scale
        )
        return (grad_key_acc, grad_value_acc)

    grad_keys, grad_values = lax.fori_loop(
        0, query_count // key_block_len, key_one_block, zero_grads
    )
    flat_shape = (clip_count, local_len, model_width)
    grad_query_rot = rotate(grad_queries, cosine, -sine_table).reshape(flat_shape)
    grad_key_rot = rotate(grad_keys, cosine, -sine_table).reshape(flat_shape)
    gain_four = jnp.sum(grad_query_rot * query_normed, axis=(0, 1))
    gain_five = jnp.sum(grad_key_rot * key_normed, axis=(0, 1))
    grad_query_pre = rms_back(query_pre, grad_query_rot * gain_rows[4])
    grad_key_pre = rms_back(key_pre, grad_key_rot * gain_rows[5])
    grad_projected = (
        jnp.concatenate([grad_query_pre, grad_key_pre, grad_values.reshape(flat_shape)], axis=-1)
        .astype(jnp.bfloat16)
        .reshape(row_total, 3 * model_width)
    )
    wgrad_attention = jnp.dot(normed_flat.T, grad_projected, preferred_element_type=jnp.float32)
    grad_normed = jnp.dot(grad_projected, full_attn.T, preferred_element_type=jnp.float32).reshape(
        flat_shape
    )
    gain_zero = jnp.sum(grad_normed * token_normed * (1.0 + scale_attn), axis=(0, 1))
    grad_scale_attn = jnp.sum(grad_normed * token_normed * gain_rows[0], axis=1)
    grad_tokens = grad_residual + rms_back(
        token_float, grad_normed * gain_rows[0] * (1.0 + scale_attn)
    )
    grad_text_key_rows = text_back_keys.reshape(clip_count, text_local, model_width)
    gain_six = jnp.sum(grad_text_key_rows * text_key_normed, axis=(0, 1))
    grad_text_pre = rms_back(text_key_pre, grad_text_key_rows * gain_rows[6])
    grad_text_proj = (
        jnp.concatenate(
            [grad_text_pre, text_back_values.reshape(clip_count, text_local, model_width)], axis=-1
        )
        .astype(jnp.bfloat16)
        .reshape(clip_count * text_local, 2 * model_width)
    )
    wgrad_caption = jnp.dot(caption_flat.T, grad_text_proj, preferred_element_type=jnp.float32)
    grad_caption = jnp.dot(
        grad_text_proj, full_caption.T, preferred_element_type=jnp.float32
    ).reshape(clip_count, text_local, caption.shape[2])
    grad_mod_row = jnp.concatenate(
        [grad_scale_attn, grad_gate_attn, grad_scale_ffn, grad_gate_ffn], axis=1
    )
    bias_grad = jnp.sum(grad_mod_row, axis=0)
    wgrad_modulation = jnp.dot(cond_act.astype(jnp.float32).T, grad_mod_row, precision=highest)
    cond_sigmoid = jax.nn.sigmoid(cond_float)
    grad_cond_act = jnp.dot(grad_mod_row, full_mod.astype(jnp.float32).T, precision=highest)
    grad_cond_part = grad_cond_act * cond_sigmoid * (1.0 + cond_float * (1.0 - cond_sigmoid))
    gain_grads = jnp.stack(
        [gain_zero, gain_one, gain_two, gain_three, gain_four, gain_five, gain_six]
    )
    partial_owned = (
        lax.psum_scatter(
            wgrad_modulation.astype(jnp.bfloat16), "clip", scatter_dimension=0, tiled=True
        ).astype(jnp.float32),
        lax.psum_scatter(
            bias_grad.astype(jnp.bfloat16), "clip", scatter_dimension=0, tiled=True
        ).astype(jnp.float32),
        lax.psum_scatter(
            wgrad_attention.astype(jnp.bfloat16), "clip", scatter_dimension=0, tiled=True
        ).astype(jnp.float32),
        lax.psum_scatter(
            wgrad_output.astype(jnp.bfloat16), "clip", scatter_dimension=0, tiled=True
        ).astype(jnp.float32),
        lax.psum_scatter(
            wgrad_caption.astype(jnp.bfloat16), "clip", scatter_dimension=0, tiled=True
        ).astype(jnp.float32),
        lax.psum_scatter(
            gain_grads.astype(jnp.bfloat16), "clip", scatter_dimension=1, tiled=True
        ).astype(jnp.float32),
        lax.psum_scatter(
            wgrad_gateup.astype(jnp.bfloat16), "clip", scatter_dimension=0, tiled=True
        ).astype(jnp.float32),
        lax.psum_scatter(
            wgrad_down.astype(jnp.bfloat16), "clip", scatter_dimension=0, tiled=True
        ).astype(jnp.float32),
    )
    owned = (
        lax.psum_scatter(
            partial_owned[0].astype(jnp.bfloat16), "seq", scatter_dimension=0, tiled=True
        ).astype(jnp.float32),
        lax.psum_scatter(
            partial_owned[1].astype(jnp.bfloat16), "seq", scatter_dimension=0, tiled=True
        ).astype(jnp.float32),
        lax.psum_scatter(
            partial_owned[2].astype(jnp.bfloat16), "seq", scatter_dimension=0, tiled=True
        ).astype(jnp.float32),
        lax.psum_scatter(
            partial_owned[3].astype(jnp.bfloat16), "seq", scatter_dimension=0, tiled=True
        ).astype(jnp.float32),
        lax.psum_scatter(
            partial_owned[4].astype(jnp.bfloat16), "seq", scatter_dimension=0, tiled=True
        ).astype(jnp.float32),
        lax.psum_scatter(
            partial_owned[5].astype(jnp.bfloat16), "seq", scatter_dimension=1, tiled=True
        ).astype(jnp.float32),
        lax.psum_scatter(
            partial_owned[6].astype(jnp.bfloat16), "seq", scatter_dimension=0, tiled=True
        ).astype(jnp.float32),
        lax.psum_scatter(
            partial_owned[7].astype(jnp.bfloat16), "seq", scatter_dimension=0, tiled=True
        ).astype(jnp.float32),
    )
    grad_gate_total = lax.psum(grad_head_gate, ("clip", "seq"))
    grad_condition = lax.psum(grad_cond_part, "seq")
    return (
        block_out,
        grad_tokens,
        grad_caption,
        grad_condition,
        owned[0],
        owned[1],
        owned[2],
        owned[3],
        owned[4],
        owned[5],
        grad_gate_total,
        owned[6],
        owned[7],
    )


def flip(value, axis):
    return lax.ppermute(value, axis, [(0, 1), (1, 0)])


def from_ahead(value, axis, step):
    count = lax.axis_size(axis)
    return lax.ppermute(value, axis, [((i + step) % count, i) for i in range(count)])


def swap_z(value, bit):
    return lax.ppermute(value, "z", [(i, i ^ bit) for i in range(4)])


def sum_seq(value):
    value = value + flip(value, "x")
    value = value + swap_z(value, 1)
    return value + swap_z(value, 2)


def gather_plane(value):
    half = value.shape[0] // 2
    from_x = flip(value, "x")
    from_y = flip(value, "y")
    far_front = flip(from_y[:half], "x")
    far_back = flip(from_x[half:], "y")
    four = jnp.concatenate([value, from_x, from_y, far_front, far_back], axis=0)
    return jnp.concatenate([four, flip(four, "core")], axis=0)


def scatter_plane(value):
    count = value.shape[0] // 2
    rows = count // 4
    half = rows // 2
    four = value[:count] + flip(value[count:].astype(bf16), "core").astype(f32)
    own, for_x, for_y, far = [four[i * rows : (i + 1) * rows] for i in range(4)]
    by_x = flip(jnp.concatenate([for_x[:half], far[:half]]).astype(bf16), "x").astype(f32)
    by_y = flip(jnp.concatenate([for_y[half:], far[half:]]).astype(bf16), "y").astype(f32)
    own = own + jnp.concatenate([by_x[:half], by_y[:half]])
    last_y = flip((for_y[:half] + by_x[half:]).astype(bf16), "y").astype(f32)
    last_x = flip((for_x[half:] + by_y[half:]).astype(bf16), "x").astype(f32)
    return own + jnp.concatenate([last_y, last_x])


def gather_clip(value):
    pair = jnp.stack([value, flip(value, "core")])
    return jnp.concatenate([pair, flip(pair, "y")])


def scatter_clip(value):
    pair = value[:2] + flip(value[2:], "y")
    return pair[0] + flip(pair[1], "core")


def rms_scale(square_mean):
    return lax.rsqrt(square_mean + epsilon)


def on_chip(body, outs, *operands, scalars=0, scratch=()):
    held = pl.BlockSpec(memory_space=pltpu.SMEM)
    whole = pl.BlockSpec(memory_space=pltpu.VMEM)
    return pl.pallas_call(
        body,
        out_shape=[jax.ShapeDtypeStruct(shape, kind) for shape, kind in outs],
        in_specs=[held] * scalars + [whole] * (len(operands) - scalars),
        out_specs=[whole] * len(outs),
        scratch_shapes=list(scratch),
        compiler_params=pltpu.CompilerParams(vmem_limit_bytes=50 * 2**20),
    )(*operands)


def dot(a, b):
    return jnp.dot(a, b, preferred_element_type=f32)


def dot_rows(a, b):
    return lax.dot_general(a, b, (((1,), (1,)), ((), ())), preferred_element_type=f32)


def dot_cols(a, b):
    return lax.dot_general(a, b, (((0,), (0,)), ((), ())), preferred_element_type=f32)


def round_up(value):
    return -(-value // 128) * 128


def prep_body(attn, gateup, cap, attn_out, ffn_out, cap_out):
    width = attn.shape[1] // 3
    cols = width // 8
    pad = attn_out.shape[2] - 3 * cols
    for s in range(8):
        parts = [attn[:, p * width + s * cols : p * width + (s + 1) * cols] for p in range(3)]
        parts.append(jnp.zeros((attn.shape[0], pad), bf16))
        attn_out[s] = jnp.concatenate(parts, axis=1)
    own = gateup.shape[1] // 64
    for g in range(8):
        for part in range(2):
            for z in range(4):
                source = (part * 32 + (g // 2) * 8 + z * 2 + g % 2) * own
                target = (part * 4 + z) * own
                ffn_out[g, :, target : target + own] = gateup[:, source : source + own]
    own = cap_out.shape[2]
    for o in range(32):
        cap_out[o] = cap[:, o * own : (o + 1) * own]


def caption_slice(weight, s):
    cols = weight.shape[1] // 16
    return jnp.concatenate(
        [weight[:, (p * 8 + s) * cols : (p * 8 + s + 1) * cols] for p in range(2)], axis=1
    )


def caption_body(place, cap, weight, keep_out, send_out):
    for s in range(8):
        own = caption_slice(weight, s)
        for r in range(4):
            part = dot(cap[place[0] ^ r], own).astype(bf16)
            if r % 2:
                send_out[r // 2, s] = part
            else:
                keep_out[r // 2, s] = part


def qkv_body(
    place, token, w0, w1, w2, w3, vectors, text, normed_out, proj_out, text_out, stats_out
):
    total, width = token.shape
    step = total // 4
    block = width // 4
    cols = width // 8
    gain, scale = vectors[0:1], vectors[1:2]
    for b in range(4):
        at = slice(b * step, (b + 1) * step)
        value = token[at].astype(f32)
        inverse = rms_scale(jnp.mean(value * value, axis=1, keepdims=True))
        normed_out[at] = (value * inverse * gain * (1.0 + scale)).astype(bf16)
    for b in range(4):
        at = slice(b * step, (b + 1) * step)
        part = jnp.zeros((step, w0.shape[1]), f32)
        for r, weight in enumerate((w0, w1, w2, w3)):
            from_col = pl.multiple_of((place[0] ^ r) * block, 128)
            part = part + dot(normed_out[at, pl.ds(from_col, block)], weight[...])
        proj_out[:, at] = part.T
    text_sum = text[0].astype(f32)
    for s in range(1, 8):
        text_sum = text_sum + text[s].astype(f32)
    text_out[...] = text_sum.T
    stats_out[...] = jnp.zeros(stats_out.shape, f32)
    query, key, caption_key = proj_out[:cols], proj_out[cols : 2 * cols], text_out[:cols]
    stats_out[0:1, :] = jnp.sum(query * query, axis=0, keepdims=True)
    stats_out[1:2, :] = jnp.sum(key * key, axis=0, keepdims=True)
    stats_out[2:3, : text.shape[1]] = jnp.sum(caption_key * caption_key, axis=0, keepdims=True)


def turn(value, cosine, sine):
    half = value.shape[0] // 2
    front, back = value[:half], value[half:]
    return jnp.concatenate([front * cosine - back * sine, back * cosine + front * sine], axis=0)


def text_softmax(scores, length):
    place = lax.broadcasted_iota(jnp.int32, scores.shape, 0)
    scores = jnp.where(place < length, scores, -1e30)
    shifted = jnp.exp(scores - jnp.max(scores, axis=0, keepdims=True))
    return shifted / jnp.sum(shifted, axis=0, keepdims=True)


def attend_body(
    heads,
    gate,
    length,
    proj,
    stats,
    text,
    gains,
    cosine,
    sine,
    mixed_out,
    query_out,
    key_out,
    value_out,
    self_out,
    cross_out,
    sum_out,
    text_key_out,
    text_value_out,
):
    total = proj.shape[1]
    cols = query_out.shape[0]
    dim = cols // heads
    width = cols * 8
    step = total // 2
    score_scale = dim ** (-0.5)
    scales = rms_scale(stats[0:3, :] / width)
    query_scale, key_scale = scales[0:1], scales[1:2]
    text_scale = scales[2:3, : text.shape[1]]
    text_key_out[...] = (text[:cols] * text_scale * gains[:, 2:3]).astype(bf16)
    text_value_out[...] = text[cols : 2 * cols].astype(bf16)
    value_out[...] = proj[2 * cols : 3 * cols].astype(bf16)
    sum_out[...] = jnp.zeros(sum_out.shape, f32)
    for h in range(heads):
        at = slice(h * dim, (h + 1) * dim)
        query = proj[at] * query_scale * gains[at, 0:1]
        query_out[at] = turn(query, cosine[...], sine[...]).astype(bf16)
        key = proj[cols + h * dim : cols + (h + 1) * dim] * key_scale * gains[at, 1:2]
        key_out[at] = turn(key, cosine[...], sine[...]).astype(bf16)
        key_rows = key_out[at].T
        text_rows = text_key_out[at].T
        for b in range(2):
            to = slice(b * step, (b + 1) * step)
            block = query_out[at, to]
            scores = dot(key_rows, block) * score_scale
            most = jnp.max(scores, axis=0, keepdims=True)
            weights = jnp.exp(scores - most)
            whole = jnp.sum(weights, axis=0, keepdims=True)
            sum_out[h : h + 1, to] = most + jnp.log(whole)
            own = dot(value_out[at], weights.astype(bf16)) * (1.0 / whole)
            text_weights = text_softmax(dot(text_rows, block) * score_scale, length[0])
            cross = dot(text_value_out[at], text_weights.astype(bf16))
            self_out[at, to] = own
            cross_out[at, to] = cross
            mixed = (own + gate[h] * cross).astype(bf16)
            piece = mixed_out.shape[2]
            for s in range(step // piece):
                mixed_out[b * (step // piece) + s, at] = mixed[:, s * piece : (s + 1) * piece]


def text_back_body(
    heads,
    gate,
    length,
    pieces,
    query,
    text_key,
    text_value,
    cross,
    text,
    stats,
    gains,
    grad_out,
    query_out,
    key_out,
    value_out,
    stats_out,
    gain_out,
    gate_out,
):
    cols, total = query.shape
    dim = cols // heads
    width = cols * 8
    step = total // 2
    score_scale = dim ** (-0.5)
    piece = pieces.shape[2]
    for s in range(pieces.shape[0]):
        grad_out[:, s * piece : (s + 1) * piece] = pieces[s]
    gate_out[...] = jnp.zeros(gate_out.shape, f32)
    for h in range(heads):
        at = slice(h * dim, (h + 1) * dim)
        text_rows, value_rows = text_key[at].T, text_value[at].T
        grad = grad_out[at].astype(f32)
        gate_sum = jnp.sum(jnp.sum(grad * cross[at], axis=0, keepdims=True), axis=1, keepdims=True)
        gate_out[h : h + 1, :] = jnp.broadcast_to(
            gate_sum * (1.0 - gate[h] * gate[h]), (1, gate_out.shape[1])
        )
        key_grad = jnp.zeros((dim, text_key.shape[1]), f32)
        value_grad = jnp.zeros((dim, text_key.shape[1]), f32)
        for b in range(2):
            to = slice(b * step, (b + 1) * step)
            block, back = query[at, to], grad_out[at, to]
            weights = text_softmax(dot(text_rows, block) * score_scale, length[0])
            upstream = dot(value_rows, back) * gate[h]
            center = jnp.sum(weights * upstream, axis=0, keepdims=True)
            score_grad = (weights * (upstream - center)).astype(bf16)
            query_out[at, to] = dot(text_key[at], score_grad)
            key_grad = key_grad + dot_rows(block, score_grad)
            value_grad = value_grad + dot_rows(back, weights.astype(bf16))
        key_out[at] = key_grad * score_scale
        value_out[at] = value_grad * gate[h]
    text_scale = rms_scale(stats[2:3, : text.shape[1]] / width)
    normed = text[:cols] * text_scale
    gain_out[...] = jnp.broadcast_to(
        jnp.sum(key_out[...] * normed, axis=1, keepdims=True), gain_out.shape
    )
    key_out[...] = key_out[...] * gains[:, 2:3]
    stats_out[...] = jnp.broadcast_to(
        jnp.sum(key_out[...] * normed, axis=0, keepdims=True), stats_out.shape
    )


def text_proj_back_body(key, value, text, stats, means, grad_out):
    cols = key.shape[0]
    width = cols * 8
    text_scale = rms_scale(stats[2:3, : text.shape[1]] / width)
    normed = text[:cols] * text_scale
    before = (key[...] - normed * (means[0:1, :] / width)) * text_scale
    grad_out[...] = jnp.concatenate([before, value[...]], axis=0).T.astype(bf16)


def caption_back_body(cap, grads, weight, weight_out, cap_out):
    cols = weight.shape[1] // 16
    for s in range(8):
        own = caption_slice(weight, s)
        part = jnp.zeros((cap.shape[2], 2 * cols), f32)
        for c in range(4):
            grad = grads[c, s]
            part = part + dot_cols(cap[c], grad)
            back = dot_rows(grad, own)
            if s == 0:
                cap_out[c] = back
            else:
                cap_out[c] = cap_out[c] + back
        for p in range(2):
            weight_out[:, (p * 8 + s) * cols : (p * 8 + s + 1) * cols] = part[
                :, p * cols : (p + 1) * cols
            ]


def attend_back_body(
    heads,
    grad,
    query,
    key,
    value,
    self_out,
    sums,
    text_query,
    proj,
    stats,
    gains,
    cosine,
    sine,
    query_in_out,
    key_in_out,
    value_grad_out,
    stats_out,
    gain_out,
):
    cols, total = query.shape
    dim = cols // heads
    width = cols * 8
    step = total // 2
    score_scale = dim ** (-0.5)
    scales = rms_scale(stats[0:2, :] / width)
    stats_out[...] = jnp.zeros(stats_out.shape, f32)
    gain_out[...] = jnp.zeros(gain_out.shape, f32)
    query_total = jnp.zeros((1, total), f32)
    key_total = jnp.zeros((1, total), f32)
    for h in range(heads):
        at = slice(h * dim, (h + 1) * dim)
        key_rows, value_rows = key[at].T, value[at].T
        delta = jnp.sum(grad[at].astype(f32) * self_out[at], axis=0, keepdims=True)
        key_grad = jnp.zeros((dim, total), f32)
        value_grad = jnp.zeros((dim, total), f32)
        query_parts = []
        for b in range(2):
            to = slice(b * step, (b + 1) * step)
            block, back = query[at, to], grad[at, to]
            weights = jnp.exp(dot(key_rows, block) * score_scale - sums[h : h + 1, to])
            value_grad = value_grad + dot_rows(back, weights.astype(bf16))
            score_grad = (weights * (dot(value_rows, back) - delta[:, to])).astype(bf16)
            key_grad = key_grad + dot_rows(block, score_grad)
            query_parts.append(dot(key[at], score_grad))
        value_grad_out[at] = value_grad.astype(bf16)
        query_grad = (jnp.concatenate(query_parts, axis=1) + text_query[at]) * score_scale
        query_grad = turn(query_grad, cosine[...], -sine[...])
        key_grad = turn(key_grad * score_scale, cosine[...], -sine[...])
        query_normed = proj[at] * scales[0:1]
        key_normed = proj[cols + h * dim : cols + (h + 1) * dim] * scales[1:2]
        gain_out[at, 0:1] = jnp.sum(query_grad * query_normed, axis=1, keepdims=True)
        gain_out[at, 1:2] = jnp.sum(key_grad * key_normed, axis=1, keepdims=True)
        query_grad = query_grad * gains[at, 0:1]
        key_grad = key_grad * gains[at, 1:2]
        query_in_out[at] = query_grad
        key_in_out[at] = key_grad
        query_total = query_total + jnp.sum(query_grad * query_normed, axis=0, keepdims=True)
        key_total = key_total + jnp.sum(key_grad * key_normed, axis=0, keepdims=True)
    stats_out[0:1, :] = query_total
    stats_out[1:2, :] = key_total


def project_back_body(
    place,
    query_in,
    key_in,
    value_grad,
    proj,
    stats,
    means,
    normed,
    w0,
    w1,
    w2,
    w3,
    own_out,
    keep_out,
    side_out,
    front1_out,
    front2_out,
    front3_out,
    near_out,
    far_out,
    low,
    turned,
):
    cols, total = query_in.shape
    width = normed.shape[1]
    block = width // 4
    rows = total // 8
    early = front1_out.shape[1]
    scales = rms_scale(stats[0:2, :] / width)
    low[...] = jnp.zeros(low.shape, bf16)
    low[:cols] = (
        (query_in[...] - proj[:cols] * scales[0:1] * (means[0:1, :] / width)) * scales[0:1]
    ).astype(bf16)
    low[cols : 2 * cols] = (
        (key_in[...] - proj[cols : 2 * cols] * scales[1:2] * (means[1:2, :] / width)) * scales[1:2]
    ).astype(bf16)
    low[2 * cols : 3 * cols] = value_grad[...]
    turned[...] = low[...].T
    weights = (w0, w1, w2, w3)
    fronts = (front1_out, front2_out, front3_out)
    for k in range(4):
        for j in range(2):
            source = (((place[1] + k) % 4) * 2 + (place[2] ^ j)) * rows
            lines = turned[pl.ds(pl.multiple_of(source, 128), rows), :]
            for r in range(4):
                to_col = pl.ds(pl.multiple_of((place[0] ^ r) * block, 128), block)
                part = dot_rows(lines, weights[r][...]).astype(bf16)
                if k == 0:
                    own_out[j, :, to_col] = part
                else:
                    fronts[k - 1][j, :, to_col] = part[:early]
                    if j == 0:
                        keep_out[k - 1, :, to_col] = part[early:]
                    else:
                        side_out[k - 1, :, to_col] = part[early:]
    for r in range(4):
        from_col = pl.ds(pl.multiple_of((place[0] ^ r) * block, 128), block)
        part = dot(low[...], normed[:, from_col]).T.astype(bf16)
        if r % 2:
            far_out[r // 2] = part
        else:
            near_out[r // 2] = part


def attention_grad_body(pieces, grad_out):
    cols = grad_out.shape[1] // 24
    for s in range(8):
        for p in range(3):
            grad_out[:, (p * 8 + s) * cols : (p * 8 + s + 1) * cols] = pieces[
                s, :, p * cols : (p + 1) * cols
            ].astype(f32)


def gateup_grad_body(pieces, grad_out):
    own = grad_out.shape[1] // 64
    for g in range(8):
        for part in range(2):
            for z in range(4):
                target = (part * 32 + (g // 2) * 8 + z * 2 + g % 2) * own
                source = (part * 4 + z) * own
                grad_out[:, target : target + own] = pieces[g, :, source : source + own].astype(f32)


def caption_grad_body(pieces, grad_out):
    own = pieces.shape[2]
    for o in range(32):
        grad_out[:, o * own : (o + 1) * own] = pieces[o]


def output_grad_body(place, mixed, grad, weight_out):
    rows = mixed.shape[2]
    total = None
    for r in range(8):
        core, y, x = r // 4, (r // 2) % 2, r % 2
        source = ((place[3] ^ y) * 2 + (place[4] ^ core)) * 2 + (place[2] ^ x)
        part = dot(mixed[source], grad[r * rows : (r + 1) * rows])
        total = part if total is None else total + part
    weight_out[...] = total.astype(bf16)


def local_fast(
    tokens,
    caption,
    condition,
    caption_len,
    frame_shape,
    rope_shift,
    w_modulation,
    mod_bias,
    w_attention,
    w_output,
    w_caption,
    norm_gains,
    head_gate,
    w_gateup,
    w_down,
    cotangent,
):
    seq_axes = ("z", "x")
    all_axes = ("y", "core") + seq_axes
    plane_axes = ("y", "core", "x")
    rows, width = tokens.shape[1:]
    total = rows * 8
    heads = head_gate.shape[0]
    head_dim = width // heads
    own_heads = heads // 8
    cols = own_heads * head_dim
    wide_cols = round_up(3 * cols)
    text_rows = caption.shape[1]
    text_total = text_rows * 8
    attn_rows = w_attention.shape[0]
    z_at, x_at = lax.axis_index("z"), lax.axis_index("x")
    y_at, core_at = lax.axis_index("y"), lax.axis_index("core")
    seq_at = z_at * 2 + x_at
    clip_at = y_at * 2 + core_at
    owner = clip_at * 8 + seq_at
    place = jnp.stack([clip_at, z_at, x_at, y_at, core_at]).astype(jnp.int32)

    own_tokens = tokens[0]
    token_all = lax.all_gather(own_tokens, seq_axes, axis=0, tiled=True)
    full_out = lax.all_gather(w_output, all_axes, axis=0, tiled=True)

    cap_cols = w_caption.shape[0]
    hidden_own = w_down.shape[0]
    hidden = 4 * hidden_own
    attn_piece, ffn_piece, cap_piece = on_chip(
        prep_body,
        [
            ((8, attn_rows, wide_cols), bf16),
            ((8, w_gateup.shape[0], 8 * hidden_own), bf16),
            ((32, text_rows, cap_cols), bf16),
        ],
        w_attention,
        w_gateup,
        caption[0],
    )
    cap_all = lax.all_to_all(cap_piece, all_axes, 0, 0, tiled=True).reshape(
        4, text_total, cap_cols
    )
    attn_0 = lax.all_to_all(attn_piece, seq_axes, 0, 0, tiled=True).reshape(-1, wide_cols)
    attn_2 = flip(attn_0, "y")
    attn_1 = flip(attn_0, "core")
    attn_3 = flip(attn_2, "core")
    attn_parts = (attn_0, attn_1, attn_2, attn_3)

    cond_float = condition[0].astype(f32)
    cond_act = jax.nn.silu(cond_float).astype(bf16)
    cond_all = gather_clip(cond_act)
    cond_rows = w_modulation.shape[0]
    cond_own = lax.dynamic_slice_in_dim(cond_all, owner * cond_rows, cond_rows, 1)
    mod_part = jnp.dot(cond_own, w_modulation, preferred_element_type=f32)
    bias_len = mod_bias.shape[0]
    bias_wide = lax.dynamic_update_slice(
        jnp.zeros((4 * width,), f32), mod_bias.astype(f32), (owner * bias_len,)
    )
    mod_part = mod_part + bias_wide[None]
    gain_cols = norm_gains.shape[1]
    gain_wide = lax.dynamic_update_slice(
        jnp.zeros((7, width), f32), norm_gains.astype(f32), (0, owner * gain_cols)
    ).reshape(-1)
    sent = flip(jnp.concatenate([mod_part[2:].reshape(-1), gain_wide]), "y")
    mod_pair = mod_part[:2] + sent[: 8 * width].reshape(2, -1)
    gain_wide = gain_wide + sent[8 * width :]
    sent = flip(jnp.concatenate([mod_pair[1], gain_wide]), "core")
    small = sum_seq(jnp.concatenate([mod_pair[0], gain_wide]) + sent)
    modulation = small[: 4 * width].reshape(4, width)
    gain_rows = small[4 * width :].reshape(7, width)
    scale_attn = modulation[0]
    gate_attn = jnp.tanh(modulation[1])
    scale_ffn = modulation[2]
    gate_ffn = jnp.tanh(modulation[3])
    own_gains = lax.dynamic_slice_in_dim(gain_rows[4:], seq_at * cols, cols, 1).T
    head_low = lax.dynamic_slice_in_dim(head_gate, seq_at * own_heads, own_heads)
    tanh_gate = jnp.tanh(head_low.astype(f32))

    ffn_piece = lax.all_to_all(ffn_piece, plane_axes, 0, 0, tiled=True)
    block = 2 * ffn_piece.shape[1]
    own_gateup = lax.all_gather(ffn_piece.reshape(4, block, -1), "z", axis=0)
    own_gateup = jnp.transpose(own_gateup, (1, 0, 2, 3)).reshape(width, -1)
    own_down = lax.all_gather(w_down, "z", axis=0, tiled=True)

    cap_keep, cap_send = on_chip(
        caption_body,
        [((2, 8, text_total, 2 * cols), bf16)] * 2,
        place,
        cap_all,
        w_caption,
        scalars=1,
    )
    cap_pair = cap_keep.astype(f32) + flip(cap_send, "core").astype(f32)
    cap_one = cap_pair[0] + flip(cap_pair[1].astype(bf16), "y").astype(f32)
    text_pieces = lax.all_to_all(cap_one.astype(bf16), seq_axes, 0, 0, tiled=True)

    normed_all, projected, text_proj, squares = on_chip(
        qkv_body,
        [
            ((total, width), bf16),
            ((wide_cols, total), f32),
            ((2 * cols, text_total), f32),
            ((8, total), f32),
        ],
        place,
        token_all,
        *attn_parts,
        jnp.stack([gain_rows[0], scale_attn]),
        text_pieces,
        scalars=1,
    )
    squares = sum_seq(squares)
    position = jnp.arange(total, dtype=jnp.int32)
    angles = rope_angles(frame_shape[0], rope_shift[0], position, head_dim // 2).T
    cosine = jnp.cos(angles)
    sine = jnp.sin(angles)
    flat = (cols, total)
    (
        mixed_pieces,
        queries,
        key_rows,
        values,
        self_out,
        cross_out,
        log_sum,
        text_keys,
        text_values,
    ) = on_chip(
        functools.partial(attend_body, own_heads),
        [
            ((8, cols, rows), bf16),
            (flat, bf16),
            (flat, bf16),
            (flat, bf16),
            (flat, f32),
            (flat, f32),
            ((8, total), f32),
            ((cols, text_total), bf16),
            ((cols, text_total), bf16),
        ],
        tanh_gate,
        caption_len,
        projected,
        squares,
        text_proj,
        own_gains,
        cosine,
        sine,
        scalars=2,
    )

    mixed_own = lax.all_to_all(mixed_pieces, seq_axes, 0, 0, tiled=True).reshape(width, rows)
    attn_proj = lax.dot_general(
        mixed_own, full_out, (((0,), (0,)), ((), ())), preferred_element_type=f32
    )
    attn_scale = rms_scale(jnp.mean(attn_proj * attn_proj, axis=-1, keepdims=True))
    attn_normed = attn_proj * attn_scale
    own_float = own_tokens.astype(f32)
    token_scale = rms_scale(jnp.mean(own_float * own_float, axis=-1, keepdims=True))
    token_normed = own_float * token_scale
    residual = own_float + gate_attn * attn_normed * gain_rows[1]
    residual_scale = rms_scale(jnp.mean(residual * residual, axis=-1, keepdims=True))
    residual_normed = residual * residual_scale
    normed_ffn = (residual_normed * gain_rows[2] * (1.0 + scale_ffn)).astype(bf16)

    normed_ffn_all = gather_plane(normed_ffn)
    gate_up = jnp.dot(normed_ffn_all, own_gateup, preferred_element_type=f32)
    gate_part = gate_up[:, :hidden]
    up_part = gate_up[:, hidden:]
    gate_sigmoid = jax.nn.sigmoid(gate_part)
    activated = (gate_part * gate_sigmoid * up_part).astype(bf16)
    down_proj = scatter_plane(jnp.dot(activated, own_down, preferred_element_type=f32))
    down_scale = rms_scale(jnp.mean(down_proj * down_proj, axis=-1, keepdims=True))
    down_normed = down_proj * down_scale
    block_out = residual + gate_ffn * down_normed * gain_rows[3]

    upstream = cotangent[0].astype(f32)
    sum_three = jnp.sum(upstream * down_normed, axis=0)
    grad_in = upstream * gate_ffn * gain_rows[3]
    grad_down = (
        (grad_in - down_normed * jnp.mean(grad_in * down_normed, axis=-1, keepdims=True))
        * down_scale
    ).astype(bf16)
    grad_down_all = gather_plane(grad_down)
    wgrad_down = jnp.dot(activated.T, grad_down_all, preferred_element_type=f32)
    grad_act = jnp.dot(grad_down_all, own_down.T, preferred_element_type=f32)
    grad_gate_part = grad_act * up_part * gate_sigmoid * (1.0 + gate_part * (1.0 - gate_sigmoid))
    grad_up_part = grad_act * gate_part * gate_sigmoid
    grad_gate_up = jnp.concatenate([grad_gate_part, grad_up_part], axis=1).astype(bf16)
    grad_normed_ffn = scatter_plane(
        jnp.dot(grad_gate_up, own_gateup.T, preferred_element_type=f32)
    )
    wgrad_gateup = jnp.dot(normed_ffn_all.T, grad_gate_up, preferred_element_type=f32)
    wgrad_gateup = jnp.transpose(
        wgrad_gateup.astype(bf16).reshape(4, 4, block, -1), (1, 0, 2, 3)
    )
    wgrad_gateup = lax.psum_scatter(wgrad_gateup, "z", scatter_dimension=0, tiled=False)
    wgrad_gateup = lax.all_to_all(
        wgrad_gateup.reshape(8, block // 2, -1), plane_axes, 0, 0, tiled=True
    )
    (wgrad_gateup,) = on_chip(gateup_grad_body, [(w_gateup.shape, f32)], wgrad_gateup)
    wgrad_down = lax.psum_scatter(
        wgrad_down.astype(bf16), "z", scatter_dimension=0, tiled=True
    ).astype(f32)

    sum_two = jnp.sum(grad_normed_ffn * residual_normed, axis=0)
    grad_in = grad_normed_ffn * gain_rows[2] * (1.0 + scale_ffn)
    grad_residual = (
        upstream
        + (grad_in - residual_normed * jnp.mean(grad_in * residual_normed, axis=-1, keepdims=True))
        * residual_scale
    )
    sum_one = jnp.sum(grad_residual * attn_normed, axis=0)
    grad_in = grad_residual * gate_attn * gain_rows[1]
    grad_attn = (
        (grad_in - attn_normed * jnp.mean(grad_in * attn_normed, axis=-1, keepdims=True))
        * attn_scale
    ).astype(bf16)
    grad_mixed = lax.dot_general(
        full_out, grad_attn, (((1,), (1,)), ((), ())), preferred_element_type=f32
    ).astype(bf16)
    grad_pieces = lax.all_to_all(grad_mixed.reshape(8, cols, rows), seq_axes, 0, 0, tiled=True)

    (
        grad_mixed,
        text_query,
        text_key_in,
        text_value_grad,
        text_stats,
        text_gain,
        gate_sum,
    ) = on_chip(
        functools.partial(text_back_body, own_heads),
        [
            (flat, bf16),
            (flat, f32),
            ((cols, text_total), f32),
            ((cols, text_total), f32),
            ((8, text_total), f32),
            ((cols, 128), f32),
            ((8, 128), f32),
        ],
        tanh_gate,
        caption_len,
        grad_pieces,
        queries,
        text_keys,
        text_values,
        cross_out,
        text_proj,
        squares,
        own_gains,
        scalars=2,
    )
    text_stats = sum_seq(text_stats)
    (grad_text_proj,) = on_chip(
        text_proj_back_body,
        [((text_total, 2 * cols), bf16)],
        text_key_in,
        text_value_grad,
        text_proj,
        squares,
        text_stats,
    )
    text_all = lax.all_gather(grad_text_proj, all_axes, axis=0)
    wgrad_caption, grad_caption = on_chip(
        caption_back_body,
        [(w_caption.shape, f32), ((4, text_total, cap_cols), f32)],
        cap_all,
        text_all.reshape(4, 8, text_total, 2 * cols),
        w_caption,
    )
    grad_caption = lax.all_to_all(
        grad_caption.reshape(32, text_rows, cap_cols), all_axes, 0, 0, tiled=True
    )
    (grad_caption,) = on_chip(caption_grad_body, [((text_rows, 32 * cap_cols), f32)], grad_caption)

    query_in, key_in, value_grad, means, own_gain_sums = on_chip(
        functools.partial(attend_back_body, own_heads),
        [
            (flat, f32),
            (flat, f32),
            (flat, bf16),
            ((8, total), f32),
            ((cols, 128), f32),
        ],
        grad_mixed,
        queries,
        key_rows,
        values,
        self_out,
        log_sum,
        text_query,
        projected,
        squares,
        own_gains,
        cosine,
        sine,
    )
    means = sum_seq(means)
    early = rows // 4
    rest = rows - early
    quarter = width // 4
    own_part, keep_part, side_part, front_1, front_2, front_3, near_part, far_part = on_chip(
        project_back_body,
        [
            ((2, rows, width), bf16),
            ((3, rest, width), bf16),
            ((3, rest, width), bf16),
            ((2, early, width), bf16),
            ((2, early, width), bf16),
            ((2, early, width), bf16),
            ((2, quarter, wide_cols), bf16),
            ((2, quarter, wide_cols), bf16),
        ],
        place,
        query_in,
        key_in,
        value_grad,
        projected,
        squares,
        means,
        normed_all,
        *attn_parts,
        scalars=1,
        scratch=[
            pltpu.VMEM((wide_cols, total), bf16),
            pltpu.VMEM((total, wide_cols), bf16),
        ],
    )
    side = flip(side_part, "x")
    fronts = [from_ahead((front_3, front_2, front_1)[k - 1], "z", k) for k in (1, 2, 3)]
    back_sum = keep_part.astype(f32) + side.astype(f32)
    backs = [from_ahead(back_sum[3 - k].astype(bf16), "z", k) for k in (1, 2, 3)]
    front_sum = own_part[:, :early].astype(f32)
    for front in fronts:
        front_sum = front_sum + front.astype(f32)
    last = flip(jnp.concatenate([front_sum[1].astype(bf16), own_part[1, early:]]), "x").astype(f32)
    back_total = own_part[0, early:].astype(f32) + last[early:]
    for back in backs:
        back_total = back_total + back.astype(f32)
    grad_normed = jnp.concatenate([front_sum[0] + last[:early], back_total])

    wgrad_pair = near_part.astype(f32) + flip(far_part, "core").astype(f32)
    wgrad_one = wgrad_pair[0] + flip(wgrad_pair[1].astype(bf16), "y").astype(f32)
    wgrad_attention = lax.all_to_all(
        wgrad_one.astype(bf16).reshape(8, attn_rows, wide_cols), seq_axes, 0, 0, tiled=True
    )
    (wgrad_attention,) = on_chip(attention_grad_body, [(w_attention.shape, f32)], wgrad_attention)

    mixed_plane = jnp.transpose(
        mixed_own.reshape(2, 2, 4, 2, attn_rows, rows), (0, 1, 3, 2, 4, 5)
    ).reshape(8, 4 * attn_rows, rows)
    mixed_plane = lax.all_to_all(mixed_plane, plane_axes, 0, 0, tiled=True)
    grad_attn_plane = gather_plane(grad_attn)
    (wgrad_output,) = on_chip(
        output_grad_body,
        [((4 * attn_rows, width), bf16)],
        place,
        mixed_plane,
        grad_attn_plane,
        scalars=1,
    )
    wgrad_output = lax.psum_scatter(
        wgrad_output, "z", scatter_dimension=0, tiled=True
    ).astype(f32)

    sum_zero = jnp.sum(grad_normed * token_normed, axis=0)
    grad_in = grad_normed * gain_rows[0] * (1.0 + scale_attn)
    grad_tokens = (
        grad_residual
        + (grad_in - token_normed * jnp.mean(grad_in * token_normed, axis=-1, keepdims=True))
        * token_scale
    )

    wide = lax.dynamic_update_slice(
        jnp.zeros((3, width), f32),
        jnp.stack([own_gain_sums[:, 0], own_gain_sums[:, 1], text_gain[:, 0]]),
        (0, seq_at * cols),
    )
    gate_wide = lax.dynamic_update_slice(
        jnp.zeros((128,), f32), gate_sum[:own_heads, 0], (seq_at * own_heads,)
    )
    sums = sum_seq(
        jnp.concatenate([sum_zero, sum_one, sum_two, sum_three, wide.reshape(-1), gate_wide])
    )
    sum_zero, sum_one, sum_two, sum_three = sums[: 4 * width].reshape(4, width)
    grad_mod_own = jnp.concatenate(
        [
            gain_rows[0] * sum_zero,
            gain_rows[1] * sum_one * (1.0 - gate_attn * gate_attn),
            gain_rows[2] * sum_two,
            gain_rows[3] * sum_three * (1.0 - gate_ffn * gate_ffn),
        ]
    )
    shared = jnp.concatenate(
        [
            (1.0 + scale_attn) * sum_zero,
            gate_attn * sum_one,
            (1.0 + scale_ffn) * sum_two,
            gate_ffn * sum_three,
            sums[4 * width :],
        ]
    )
    gathered = gather_clip(jnp.concatenate([grad_mod_own, shared]))
    grad_mod_row = gathered[:, : 4 * width]
    shared = (gathered[0] + gathered[1] + gathered[2] + gathered[3])[4 * width :]
    gain_grads = lax.dynamic_slice(
        shared[: 7 * width].reshape(7, width), (0, owner * gain_cols), (7, gain_cols)
    )
    grad_gate_total = shared[7 * width : 7 * width + heads]
    bias_grad = lax.dynamic_slice(
        jnp.sum(grad_mod_row, axis=0), (owner * bias_len,), (bias_len,)
    )
    wgrad_modulation = jnp.dot(cond_own.astype(f32).T, grad_mod_row, precision=highest)
    cond_back = jnp.dot(grad_mod_row, w_modulation.astype(f32).T, precision=highest)
    cond_wide = lax.dynamic_update_slice(
        jnp.zeros((4, cond_float.shape[0]), f32), cond_back, (0, owner * cond_rows)
    )
    cond_back = sum_seq(scatter_clip(cond_wide))
    cond_sigmoid = jax.nn.sigmoid(cond_float)
    grad_condition = cond_back * cond_sigmoid * (1.0 + cond_float * (1.0 - cond_sigmoid))

    return (
        block_out[None],
        grad_tokens[None],
        grad_caption[None],
        grad_condition[None],
        wgrad_modulation,
        bias_grad,
        wgrad_attention,
        wgrad_output,
        wgrad_caption,
        gain_grads,
        grad_gate_total,
        wgrad_gateup,
        wgrad_down,
    )


def specs(clip, seq):
    both = clip + seq
    placed = (
        P(clip, seq, None),
        P(clip, seq, None),
        P(clip, None),
        P(clip),
        P(clip, None),
        P(clip, None),
        P(both, None),
        P(both),
        P(both, None),
        P(both, None),
        P(both, None),
        P(None, both),
        P(),
        P(both, None),
        P(both, None),
        P(clip, seq, None),
    )
    given = (
        P(clip, seq, None),
        P(clip, seq, None),
        P(clip, seq, None),
        P(clip, None),
        P(both, None),
        P(both),
        P(both, None),
        P(both, None),
        P(both, None),
        P(None, both),
        P(),
        P(both, None),
        P(both, None),
    )
    return placed, given


def solution(mesh):
    if dict(mesh.shape) == {"clip": 4, "seq": 8}:
        grid = Mesh(mesh.devices.reshape(2, 2, 4, 2), ("y", "core", "z", "x"))
        placed, given = specs(("y", "core"), ("z", "x"))
        return jax.shard_map(
            local_fast, mesh=grid, in_specs=placed, out_specs=given, check_vma=False
        )
    placed, given = specs(("clip",), ("seq",))
    return jax.shard_map(local, mesh=mesh, in_specs=placed, out_specs=given, check_vma=False)
```

```python
import functools
import math

import jax
import jax.numpy as jnp
from jax import lax
from jax.experimental import pallas as pl
from jax.experimental.pallas import tpu as pltpu
from jax.sharding import Mesh
from jax.sharding import PartitionSpec as P

epsilon = 1e-06
theta_base = 10000.0
highest = lax.Precision.HIGHEST
bf16 = jnp.bfloat16
f32 = jnp.float32


def rms_norm(value):
    return value * lax.rsqrt(jnp.mean(value * value, axis=-1, keepdims=True) + epsilon)


def rms_back(value, upstream):
    return jax.vjp(rms_norm, value)[1](upstream)[0]


def rope_angles(shape_row, shift_row, position, half_dim):
    across = shape_row[2] + 1
    column_place = position % across + shift_row[2]
    row_place = position // across % shape_row[1] + shift_row[1]
    frame_place = position // (across * shape_row[1]) + shift_row[0]
    frame_count = half_dim // 4
    row_count = 3 * half_dim // 8
    column_count = half_dim - frame_count - row_count
    pieces = []
    for place_index, group_size in (
        (frame_place, frame_count),
        (row_place, row_count),
        (column_place, column_count),
    ):
        frequency = theta_base ** (-jnp.arange(group_size, dtype=jnp.float32) / group_size)
        pieces.append(place_index.astype(jnp.float32)[:, None] * frequency[None, :])
    return jnp.concatenate(pieces, axis=1)


def rotate(value, cosine, sine_table):
    half_dim = value.shape[-1] // 2
    front_half = value[..., :half_dim]
    back_half = value[..., half_dim:]
    return jnp.concatenate(
        [
            front_half * cosine - back_half * sine_table,
            back_half * cosine + front_half * sine_table,
        ],
        axis=-1,
    )


def soft_weights(scores):
    shifted = jnp.exp(scores - jnp.max(scores, axis=-1, keepdims=True))
    return shifted / jnp.sum(shifted, axis=-1, keepdims=True)


def local(
    tokens,
    caption,
    condition,
    caption_len,
    frame_shape,
    rope_shift,
    w_modulation,
    mod_bias,
    w_attention,
    w_output,
    w_caption,
    norm_gains,
    head_gate,
    w_gateup,
    w_down,
    cotangent,
):
    clip_count, local_len, model_width = tokens.shape
    head_count = head_gate.shape[0]
    head_dim = model_width // head_count
    score_scale = head_dim ** (-0.5)
    row_total = clip_count * local_len
    text_local = caption.shape[1]
    text_total = text_local * lax.axis_size("seq")
    gathered = (
        lax.all_gather(w_modulation, ("clip", "seq"), axis=0, tiled=True),
        lax.all_gather(mod_bias, ("clip", "seq"), axis=0, tiled=True),
        lax.all_gather(w_attention, ("clip", "seq"), axis=0, tiled=True),
        lax.all_gather(w_output, ("clip", "seq"), axis=0, tiled=True),
        lax.all_gather(w_caption, ("clip", "seq"), axis=0, tiled=True),
        lax.all_gather(norm_gains, ("clip", "seq"), axis=1, tiled=True),
    )
    full_mod, full_bias, full_attn, full_out, full_caption, full_gains = gathered
    gain_rows = full_gains.astype(jnp.float32)
    tanh_gate = jnp.tanh(head_gate.astype(jnp.float32))
    cond_float = condition.astype(jnp.float32)
    cond_act = jax.nn.silu(cond_float).astype(jnp.bfloat16)
    modulation = jnp.dot(cond_act, full_mod, preferred_element_type=jnp.float32) + full_bias.astype(
        jnp.float32
    )
    scale_attn = modulation[:, None, :model_width]
    gate_attn = jnp.tanh(modulation[:, None, model_width : 2 * model_width])
    scale_ffn = modulation[:, None, 2 * model_width : 3 * model_width]
    gate_ffn = jnp.tanh(modulation[:, None, 3 * model_width :])
    token_float = tokens.astype(jnp.float32)
    token_normed = rms_norm(token_float)
    normed_flat = (
        (token_normed * gain_rows[0] * (1.0 + scale_attn))
        .astype(jnp.bfloat16)
        .reshape(row_total, model_width)
    )
    projected = jnp.dot(normed_flat, full_attn, preferred_element_type=jnp.float32).reshape(
        clip_count, local_len, 3 * model_width
    )
    query_pre = projected[..., :model_width]
    key_pre = projected[..., model_width : 2 * model_width]
    query_normed = rms_norm(query_pre)
    key_normed = rms_norm(key_pre)
    position = lax.axis_index("seq") * local_len + jnp.arange(local_len, dtype=jnp.int32)
    angles = jax.vmap(
        lambda shape_row, shift_row: rope_angles(shape_row, shift_row, position, head_dim // 2)
    )(frame_shape, rope_shift)
    cosine = jnp.cos(angles)[:, :, None, :]
    sine_table = jnp.sin(angles)[:, :, None, :]
    split_shape = (clip_count, local_len, head_count, head_dim)
    queries = rotate((query_normed * gain_rows[4]).reshape(split_shape), cosine, sine_table).astype(
        jnp.bfloat16
    )
    key_rows = rotate((key_normed * gain_rows[5]).reshape(split_shape), cosine, sine_table).astype(
        jnp.bfloat16
    )
    value_rows = projected[..., 2 * model_width :].reshape(split_shape).astype(jnp.bfloat16)
    caption_flat = caption.reshape(clip_count * text_local, caption.shape[2])
    text_proj = jnp.dot(caption_flat, full_caption, preferred_element_type=jnp.float32).reshape(
        clip_count, text_local, 2 * model_width
    )
    text_key_pre = text_proj[..., :model_width]
    text_key_normed = rms_norm(text_key_pre)
    text_shape = (clip_count, text_local, head_count, head_dim)
    text_keys = (text_key_normed * gain_rows[6]).astype(jnp.bfloat16).reshape(text_shape)
    text_values = text_proj[..., model_width:].astype(jnp.bfloat16).reshape(text_shape)
    all_text_keys, all_text_values = (
        lax.all_gather(text_keys, "seq", axis=1, tiled=True),
        lax.all_gather(text_values, "seq", axis=1, tiled=True),
    )
    stat_shape = (clip_count, head_count, local_len)
    start_stats = (jnp.full(stat_shape, -1e30, jnp.float32), jnp.zeros(stat_shape, jnp.float32))
    piece_keys = lax.all_gather(key_rows, "seq", axis=1, tiled=True)
    key_count = piece_keys.shape[1]
    block_len = math.gcd(key_count, 512)

    def stat_one_block(block_index, inner_state):
        row_max, row_sum = inner_state
        block_keys = lax.dynamic_slice_in_dim(piece_keys, block_index * block_len, block_len, 1)
        scores = (
            jnp.einsum("cqhd,ckhd->chqk", queries, block_keys, preferred_element_type=jnp.float32)
            * score_scale
        )
        new_max = jnp.maximum(row_max, jnp.max(scores, axis=-1))
        row_sum = row_sum * jnp.exp(row_max - new_max) + jnp.sum(
            jnp.exp(scores - new_max[..., None]), axis=-1
        )
        return (new_max, row_sum)

    row_max, row_sum = lax.fori_loop(0, key_count // block_len, stat_one_block, start_stats)
    log_sum = row_max + jnp.log(row_sum)
    attend_piece_keys = lax.all_gather(key_rows, "seq", axis=1, tiled=True)
    piece_values = lax.all_gather(value_rows, "seq", axis=1, tiled=True)
    key_count = attend_piece_keys.shape[1]
    attend_block_len = math.gcd(key_count, 512)

    def attend_one_block(block_index, weighted):
        block_keys = lax.dynamic_slice_in_dim(
            attend_piece_keys, block_index * attend_block_len, attend_block_len, 1
        )
        block_values = lax.dynamic_slice_in_dim(
            piece_values, block_index * attend_block_len, attend_block_len, 1
        )
        scores = (
            jnp.einsum("cqhd,ckhd->chqk", queries, block_keys, preferred_element_type=jnp.float32)
            * score_scale
        )
        probs = jnp.exp(scores - log_sum[..., None]).astype(jnp.bfloat16)
        return weighted + jnp.einsum(
            "chqk,ckhd->chqd", probs, block_values, preferred_element_type=jnp.float32
        )

    weighted = lax.fori_loop(
        0,
        key_count // attend_block_len,
        attend_one_block,
        jnp.zeros(stat_shape + (head_dim,), jnp.float32),
    )
    self_out = jnp.transpose(weighted, (0, 2, 1, 3))
    usable = jnp.arange(text_total, dtype=jnp.int32)[None, :] < caption_len[:, None]
    text_scores = (
        jnp.einsum("cqhd,ckhd->chqk", queries, all_text_keys, preferred_element_type=jnp.float32)
        * score_scale
    )
    text_scores = jnp.where(usable[:, None, None, :], text_scores, -1e30)
    text_weights = soft_weights(text_scores)
    text_low = text_weights.astype(jnp.bfloat16)
    cross_out = jnp.einsum(
        "chqk,ckhd->cqhd", text_low, all_text_values, preferred_element_type=jnp.float32
    )
    mixed_heads = self_out + tanh_gate[None, None, :, None] * cross_out
    mixed_flat = mixed_heads.reshape(row_total, model_width).astype(jnp.bfloat16)
    attn_proj = jnp.dot(mixed_flat, full_out, preferred_element_type=jnp.float32).reshape(
        clip_count, local_len, model_width
    )
    attn_normed = rms_norm(attn_proj)
    residual = token_float + gate_attn * attn_normed * gain_rows[1]
    full_gateup, full_down = (
        lax.all_gather(w_gateup, ("clip", "seq"), axis=0, tiled=True),
        lax.all_gather(w_down, ("clip", "seq"), axis=0, tiled=True),
    )
    hidden_units = full_down.shape[0]
    residual_normed = rms_norm(residual)
    normed_ffn = (
        (residual_normed * gain_rows[2] * (1.0 + scale_ffn))
        .astype(jnp.bfloat16)
        .reshape(row_total, model_width)
    )
    gate_up = jnp.dot(normed_ffn, full_gateup, preferred_element_type=jnp.float32)
    gate_part = gate_up[:, :hidden_units]
    up_part = gate_up[:, hidden_units:]
    gate_sigmoid = jax.nn.sigmoid(gate_part)
    activated = (gate_part * gate_sigmoid * up_part).astype(jnp.bfloat16)
    down_proj = jnp.dot(activated, full_down, preferred_element_type=jnp.float32).reshape(
        clip_count, local_len, model_width
    )
    down_normed = rms_norm(down_proj)
    block_out = residual + gate_ffn * down_normed * gain_rows[3]
    upstream = cotangent.astype(jnp.float32)
    gain_three = jnp.sum(upstream * gate_ffn * down_normed, axis=(0, 1))
    grad_gate_ffn = jnp.sum(upstream * down_normed * gain_rows[3], axis=1) * (
        1.0 - gate_ffn[:, 0] * gate_ffn[:, 0]
    )
    grad_down = (
        rms_back(down_proj, upstream * gate_ffn * gain_rows[3])
        .astype(jnp.bfloat16)
        .reshape(row_total, model_width)
    )
    full_gateup, full_down = (
        lax.all_gather(w_gateup, ("clip", "seq"), axis=0, tiled=True),
        lax.all_gather(w_down, ("clip", "seq"), axis=0, tiled=True),
    )
    wgrad_down = jnp.dot(activated.T, grad_down, preferred_element_type=jnp.float32)
    grad_act = jnp.dot(grad_down, full_down.T, preferred_element_type=jnp.float32)
    grad_gate_part = grad_act * up_part * gate_sigmoid * (1.0 + gate_part * (1.0 - gate_sigmoid))
    grad_up_part = grad_act * gate_part * gate_sigmoid
    grad_gate_up = jnp.concatenate([grad_gate_part, grad_up_part], axis=1).astype(jnp.bfloat16)
    wgrad_gateup = jnp.dot(normed_ffn.T, grad_gate_up, preferred_element_type=jnp.float32)
    grad_normed_ffn = jnp.dot(
        grad_gate_up, full_gateup.T, preferred_element_type=jnp.float32
    ).reshape(clip_count, local_len, model_width)
    gain_two = jnp.sum(grad_normed_ffn * residual_normed * (1.0 + scale_ffn), axis=(0, 1))
    grad_scale_ffn = jnp.sum(grad_normed_ffn * residual_normed * gain_rows[2], axis=1)
    grad_residual = upstream + rms_back(
        residual, grad_normed_ffn * gain_rows[2] * (1.0 + scale_ffn)
    )
    gain_one = jnp.sum(grad_residual * gate_attn * attn_normed, axis=(0, 1))
    grad_gate_attn = jnp.sum(grad_residual * attn_normed * gain_rows[1], axis=1) * (
        1.0 - gate_attn[:, 0] * gate_attn[:, 0]
    )
    grad_attn = (
        rms_back(attn_proj, grad_residual * gate_attn * gain_rows[1])
        .astype(jnp.bfloat16)
        .reshape(row_total, model_width)
    )
    full_mod, full_attn, full_out, full_caption = (
        lax.all_gather(w_modulation, ("clip", "seq"), axis=0, tiled=True),
        lax.all_gather(w_attention, ("clip", "seq"), axis=0, tiled=True),
        lax.all_gather(w_output, ("clip", "seq"), axis=0, tiled=True),
        lax.all_gather(w_caption, ("clip", "seq"), axis=0, tiled=True),
    )
    wgrad_output = jnp.dot(mixed_flat.T, grad_attn, preferred_element_type=jnp.float32)
    grad_mixed = (
        jnp.dot(grad_attn, full_out.T, preferred_element_type=jnp.float32)
        .reshape(split_shape)
        .astype(jnp.bfloat16)
    )
    grad_float = grad_mixed.astype(jnp.float32)
    grad_head_gate = jnp.sum(grad_float * cross_out, axis=(0, 1, 3)) * (1.0 - tanh_gate * tanh_gate)
    delta_rows = jnp.sum(grad_float * self_out, axis=-1)
    delta_heads = jnp.transpose(delta_rows, (0, 2, 1))
    lse_rows = jnp.transpose(log_sum, (0, 2, 1))
    text_grad = (
        jnp.einsum(
            "cqhd,ckhd->chqk", grad_mixed, all_text_values, preferred_element_type=jnp.float32
        )
        * tanh_gate[None, :, None, None]
    )
    text_center = jnp.sum(text_weights * text_grad, axis=-1, keepdims=True)
    grad_text_scores = (text_weights * (text_grad - text_center)).astype(jnp.bfloat16)
    grad_queries = (
        jnp.einsum(
            "chqk,ckhd->cqhd", grad_text_scores, all_text_keys, preferred_element_type=jnp.float32
        )
        * score_scale
    )
    grad_text_keys = (
        jnp.einsum("chqk,cqhd->ckhd", grad_text_scores, queries, preferred_element_type=jnp.float32)
        * score_scale
    )
    grad_text_values = (
        jnp.einsum("chqk,cqhd->ckhd", text_low, grad_mixed, preferred_element_type=jnp.float32)
        * tanh_gate[None, None, :, None]
    )
    text_back_keys, text_back_values = (
        lax.psum_scatter(
            grad_text_keys.astype(jnp.bfloat16), "seq", scatter_dimension=1, tiled=True
        ).astype(jnp.float32),
        lax.psum_scatter(
            grad_text_values.astype(jnp.bfloat16), "seq", scatter_dimension=1, tiled=True
        ).astype(jnp.float32),
    )
    query_piece_keys = lax.all_gather(key_rows, "seq", axis=1, tiled=True)
    query_piece_values = lax.all_gather(value_rows, "seq", axis=1, tiled=True)
    key_count = query_piece_keys.shape[1]
    query_block_len = math.gcd(key_count, 512)

    def query_one_block(block_index, inner_state):
        block_keys = lax.dynamic_slice_in_dim(
            query_piece_keys, block_index * query_block_len, query_block_len, 1
        )
        block_values = lax.dynamic_slice_in_dim(
            query_piece_values, block_index * query_block_len, query_block_len, 1
        )
        scores = (
            jnp.einsum("cqhd,ckhd->chqk", queries, block_keys, preferred_element_type=jnp.float32)
            * score_scale
        )
        probs = jnp.exp(scores - log_sum[..., None])
        grad_probs = jnp.einsum(
            "cqhd,ckhd->chqk", grad_mixed, block_values, preferred_element_type=jnp.float32
        )
        grad_scores = (probs * (grad_probs - delta_heads[..., None])).astype(jnp.bfloat16)
        return (
            inner_state
            + jnp.einsum(
                "chqk,ckhd->cqhd", grad_scores, block_keys, preferred_element_type=jnp.float32
            )
            * score_scale
        )

    grad_self_queries = lax.fori_loop(
        0, key_count // query_block_len, query_one_block, jnp.zeros(split_shape, jnp.float32)
    )
    grad_queries = grad_queries + grad_self_queries
    zero_grads = (jnp.zeros(split_shape, jnp.float32), jnp.zeros(split_shape, jnp.float32))
    piece_queries = lax.all_gather(queries.astype(jnp.float32), "seq", axis=1, tiled=True).astype(
        jnp.bfloat16
    )
    piece_grads = lax.all_gather(grad_float, "seq", axis=1, tiled=True).astype(jnp.bfloat16)
    piece_lse = lax.all_gather(lse_rows, "seq", axis=1, tiled=True)
    piece_delta = lax.all_gather(delta_rows, "seq", axis=1, tiled=True)
    query_count = piece_queries.shape[1]
    key_block_len = math.gcd(query_count, 512)

    def key_one_block(block_index, inner_state):
        grad_key_acc, grad_value_acc = inner_state
        block_queries = lax.dynamic_slice_in_dim(
            piece_queries, block_index * key_block_len, key_block_len, 1
        )
        block_grads = lax.dynamic_slice_in_dim(
            piece_grads, block_index * key_block_len, key_block_len, 1
        )
        block_lse = jnp.transpose(
            lax.dynamic_slice_in_dim(piece_lse, block_index * key_block_len, key_block_len, 1),
            (0, 2, 1),
        )
        block_delta = jnp.transpose(
            lax.dynamic_slice_in_dim(piece_delta, block_index * key_block_len, key_block_len, 1),
            (0, 2, 1),
        )
        scores = (
            jnp.einsum(
                "cqhd,ckhd->chqk", block_queries, key_rows, preferred_element_type=jnp.float32
            )
            * score_scale
        )
        probs = jnp.exp(scores - block_lse[..., None])
        grad_value_acc = grad_value_acc + jnp.einsum(
            "chqk,cqhd->ckhd",
            probs.astype(jnp.bfloat16),
            block_grads,
            preferred_element_type=jnp.float32,
        )
        grad_probs = jnp.einsum(
            "cqhd,ckhd->chqk", block_grads, value_rows, preferred_element_type=jnp.float32
        )
        grad_scores = (probs * (grad_probs - block_delta[..., None])).astype(jnp.bfloat16)
        grad_key_acc = (
            grad_key_acc
            + jnp.einsum(
                "chqk,cqhd->ckhd", grad_scores, block_queries, preferred_element_type=jnp.float32
            )
            * score_scale
        )
        return (grad_key_acc, grad_value_acc)

    grad_keys, grad_values = lax.fori_loop(
        0, query_count // key_block_len, key_one_block, zero_grads
    )
    flat_shape = (clip_count, local_len, model_width)
    grad_query_rot = rotate(grad_queries, cosine, -sine_table).reshape(flat_shape)
    grad_key_rot = rotate(grad_keys, cosine, -sine_table).reshape(flat_shape)
    gain_four = jnp.sum(grad_query_rot * query_normed, axis=(0, 1))
    gain_five = jnp.sum(grad_key_rot * key_normed, axis=(0, 1))
    grad_query_pre = rms_back(query_pre, grad_query_rot * gain_rows[4])
    grad_key_pre = rms_back(key_pre, grad_key_rot * gain_rows[5])
    grad_projected = (
        jnp.concatenate([grad_query_pre, grad_key_pre, grad_values.reshape(flat_shape)], axis=-1)
        .astype(jnp.bfloat16)
        .reshape(row_total, 3 * model_width)
    )
    wgrad_attention = jnp.dot(normed_flat.T, grad_projected, preferred_element_type=jnp.float32)
    grad_normed = jnp.dot(grad_projected, full_attn.T, preferred_element_type=jnp.float32).reshape(
        flat_shape
    )
    gain_zero = jnp.sum(grad_normed * token_normed * (1.0 + scale_attn), axis=(0, 1))
    grad_scale_attn = jnp.sum(grad_normed * token_normed * gain_rows[0], axis=1)
    grad_tokens = grad_residual + rms_back(
        token_float, grad_normed * gain_rows[0] * (1.0 + scale_attn)
    )
    grad_text_key_rows = text_back_keys.reshape(clip_count, text_local, model_width)
    gain_six = jnp.sum(grad_text_key_rows * text_key_normed, axis=(0, 1))
    grad_text_pre = rms_back(text_key_pre, grad_text_key_rows * gain_rows[6])
    grad_text_proj = (
        jnp.concatenate(
            [grad_text_pre, text_back_values.reshape(clip_count, text_local, model_width)], axis=-1
        )
        .astype(jnp.bfloat16)
        .reshape(clip_count * text_local, 2 * model_width)
    )
    wgrad_caption = jnp.dot(caption_flat.T, grad_text_proj, preferred_element_type=jnp.float32)
    grad_caption = jnp.dot(
        grad_text_proj, full_caption.T, preferred_element_type=jnp.float32
    ).reshape(clip_count, text_local, caption.shape[2])
    grad_mod_row = jnp.concatenate(
        [grad_scale_attn, grad_gate_attn, grad_scale_ffn, grad_gate_ffn], axis=1
    )
    bias_grad = jnp.sum(grad_mod_row, axis=0)
    wgrad_modulation = jnp.dot(cond_act.astype(jnp.float32).T, grad_mod_row, precision=highest)
    cond_sigmoid = jax.nn.sigmoid(cond_float)
    grad_cond_act = jnp.dot(grad_mod_row, full_mod.astype(jnp.float32).T, precision=highest)
    grad_cond_part = grad_cond_act * cond_sigmoid * (1.0 + cond_float * (1.0 - cond_sigmoid))
    gain_grads = jnp.stack(
        [gain_zero, gain_one, gain_two, gain_three, gain_four, gain_five, gain_six]
    )
    partial_owned = (
        lax.psum_scatter(
            wgrad_modulation.astype(jnp.bfloat16), "clip", scatter_dimension=0, tiled=True
        ).astype(jnp.float32),
        lax.psum_scatter(
            bias_grad.astype(jnp.bfloat16), "clip", scatter_dimension=0, tiled=True
        ).astype(jnp.float32),
        lax.psum_scatter(
            wgrad_attention.astype(jnp.bfloat16), "clip", scatter_dimension=0, tiled=True
        ).astype(jnp.float32),
        lax.psum_scatter(
            wgrad_output.astype(jnp.bfloat16), "clip", scatter_dimension=0, tiled=True
        ).astype(jnp.float32),
        lax.psum_scatter(
            wgrad_caption.astype(jnp.bfloat16), "clip", scatter_dimension=0, tiled=True
        ).astype(jnp.float32),
        lax.psum_scatter(
            gain_grads.astype(jnp.bfloat16), "clip", scatter_dimension=1, tiled=True
        ).astype(jnp.float32),
        lax.psum_scatter(
            wgrad_gateup.astype(jnp.bfloat16), "clip", scatter_dimension=0, tiled=True
        ).astype(jnp.float32),
        lax.psum_scatter(
            wgrad_down.astype(jnp.bfloat16), "clip", scatter_dimension=0, tiled=True
        ).astype(jnp.float32),
    )
    owned = (
        lax.psum_scatter(
            partial_owned[0].astype(jnp.bfloat16), "seq", scatter_dimension=0, tiled=True
        ).astype(jnp.float32),
        lax.psum_scatter(
            partial_owned[1].astype(jnp.bfloat16), "seq", scatter_dimension=0, tiled=True
        ).astype(jnp.float32),
        lax.psum_scatter(
            partial_owned[2].astype(jnp.bfloat16), "seq", scatter_dimension=0, tiled=True
        ).astype(jnp.float32),
        lax.psum_scatter(
            partial_owned[3].astype(jnp.bfloat16), "seq", scatter_dimension=0, tiled=True
        ).astype(jnp.float32),
        lax.psum_scatter(
            partial_owned[4].astype(jnp.bfloat16), "seq", scatter_dimension=0, tiled=True
        ).astype(jnp.float32),
        lax.psum_scatter(
            partial_owned[5].astype(jnp.bfloat16), "seq", scatter_dimension=1, tiled=True
        ).astype(jnp.float32),
        lax.psum_scatter(
            partial_owned[6].astype(jnp.bfloat16), "seq", scatter_dimension=0, tiled=True
        ).astype(jnp.float32),
        lax.psum_scatter(
            partial_owned[7].astype(jnp.bfloat16), "seq", scatter_dimension=0, tiled=True
        ).astype(jnp.float32),
    )
    grad_gate_total = lax.psum(grad_head_gate, ("clip", "seq"))
    grad_condition = lax.psum(grad_cond_part, "seq")
    return (
        block_out,
        grad_tokens,
        grad_caption,
        grad_condition,
        owned[0],
        owned[1],
        owned[2],
        owned[3],
        owned[4],
        owned[5],
        grad_gate_total,
        owned[6],
        owned[7],
    )


def flip(value, axis):
    return lax.ppermute(value, axis, [(0, 1), (1, 0)])


def from_ahead(value, axis, step):
    count = lax.axis_size(axis)
    return lax.ppermute(value, axis, [((i + step) % count, i) for i in range(count)])


def swap_z(value, bit):
    return lax.ppermute(value, "z", [(i, i ^ bit) for i in range(4)])


def seq_terms(value):
    value = value + flip(value, "x")
    return [value] + [from_ahead(value, "z", k) for k in (1, 2, 3)]


def share(copies):
    return lax.all_to_all(copies, ("z", "x"), 0, 0, tiled=True)


def eight_sum(parts):
    total = parts[0]
    for s in range(1, 8):
        total = total + parts[s]
    return total


def spread(out):
    for s in range(1, 8):
        out[s] = out[0]


def four_sum(parts):
    return (parts[0] + parts[2]) + (parts[1] + parts[3])


def gather_chips(value):
    from_y = flip(value, "y")
    return [value, flip(value, "x"), from_y, flip(from_y, "x")]


def gather_clip(value):
    from_y = flip(value, "y")
    return [value, flip(value, "core"), from_y, flip(from_y, "core")]


def together(*values):
    return lax.optimization_barrier(values)


def rms_scale(square_mean):
    return lax.rsqrt(square_mean + epsilon)


def whole(shape):
    return pl.BlockSpec(shape, lambda step: (0,) * len(shape), pipeline_mode=pl.Buffered(1))


class Line:
    def __init__(self):
        self.last = ()

    def __call__(self, body, outs, *operands, scalars=0, scratch=(), after=(), far=0):
        held = pl.BlockSpec(memory_space=pltpu.SMEM)
        unread = pl.BlockSpec(memory_space=pl.ANY)
        waits = tuple(after) + self.last
        count, skip = len(operands), len(waits)

        def run(*refs):
            body(*refs[:count], *refs[count + skip :])

        given = pl.pallas_call(
            run,
            out_shape=[jax.ShapeDtypeStruct(shape, kind) for shape, kind in outs],
            grid=(1,),
            in_specs=[held] * scalars
            + [whole(value.shape) for value in operands[scalars : count - far]]
            + [unread] * far
            + [unread] * skip,
            out_specs=[whole(shape) for shape, kind in outs],
            scratch_shapes=list(scratch),
            compiler_params=pltpu.CompilerParams(vmem_limit_bytes=50 * 2**20),
        )(*operands, *waits)
        self.last = (min(given, key=lambda value: value.size),)
        return given


def alone(*args, **kinds):
    return Line()(*args, **kinds)


def dot(a, b):
    return jnp.dot(a, b, preferred_element_type=f32)


def dot_rows(a, b):
    return lax.dot_general(a, b, (((1,), (1,)), ((), ())), preferred_element_type=f32)


def dot_cols(a, b):
    return lax.dot_general(a, b, (((0,), (0,)), ((), ())), preferred_element_type=f32)


def round_up(value):
    return -(-value // 128) * 128


def prep_body(attn, gateup, cap, mod, extra, attn_out, ffn_out, cap_out, mod_out):
    width = attn.shape[1] // 3
    cols = width // 8
    pad = attn_out.shape[2] - 3 * cols
    for s in range(8):
        parts = [attn[:, p * width + s * cols : p * width + (s + 1) * cols] for p in range(3)]
        parts.append(jnp.zeros((attn.shape[0], pad), bf16))
        attn_out[s] = jnp.concatenate(parts, axis=1)
    own = gateup.shape[1] // 64
    for g in range(8):
        for part in range(2):
            for z in range(4):
                source = (part * 32 + (g // 2) * 8 + z * 2 + g % 2) * own
                target = (part * 4 + z) * own
                ffn_out[g, :, target : target + own] = gateup[:, source : source + own]
    own = cap_out.shape[2]
    for o in range(32):
        cap_out[o] = cap[:, o * own : (o + 1) * own]
    span = mod.shape[1]
    mod_out[:, :span] = mod[...]
    mod_out[:, span:] = extra[...]


def owner_of(place, r):
    return (place[0] ^ r) * 8 + place[5]


def modulate_body(place, cond, p0, p1, p2, p3, out):
    span = p0.shape[1] - 384
    chunk = span // 32
    gain = chunk // 4
    total = jnp.zeros((8, span), f32)
    for r, piece in enumerate((p0, p1, p2, p3)):
        row = cond[pl.ds(owner_of(place, r), 1), :]
        row = (row / (1.0 + jnp.exp(-row))).astype(bf16).astype(f32)
        row = jnp.broadcast_to(row, (8, row.shape[1])).astype(bf16)
        total = total + dot(row, piece[:, :span])
    out[...] = jnp.zeros(out.shape, f32)
    for i in range(32):
        out[i : i + 1, :chunk] = total[0:1, i * chunk : (i + 1) * chunk]
    for r, piece in enumerate((p0, p1, p2, p3)):
        extra = piece[0:16, span : span + 256].astype(f32)
        at = pl.ds(owner_of(place, r), 1)
        parts = [extra[0:1, :256]] + [extra[8 + g : 9 + g, :gain] for g in range(7)]
        parts.append(jnp.zeros((1, out.shape[1] - 256 - 7 * gain), f32))
        out[at, :] = out[at, :] + jnp.concatenate(parts, axis=1)


def vector_body(place, a, b, c, d, vector_out, column_out, small, turned):
    chunk = vector_out.shape[1] // 8
    gain = chunk // 4
    small[...] = four_sum([a[...], b[...], c[...], d[...]])
    vector_out[...] = jnp.zeros(vector_out.shape, f32)
    for i in range(32):
        to = (i % 8) * chunk
        vector_out[i // 8 : i // 8 + 1, to : to + chunk] = small[i : i + 1, :chunk]
        for g in range(7):
            vector_out[4 + g : 5 + g, i * gain : (i + 1) * gain] = small[
                i : i + 1, 256 + g * gain : 256 + (g + 1) * gain
            ]
    vector_out[1:2] = jnp.tanh(vector_out[1:2])
    vector_out[3:4] = jnp.tanh(vector_out[3:4])
    turned[...] = jnp.zeros(turned.shape, f32)
    for j in range(4):
        row = small[pl.ds(place[5] * 4 + j, 1), :]
        for p in range(3):
            turned[p : p + 1, j * gain : (j + 1) * gain] = row[
                :, 256 + (4 + p) * gain : 256 + (5 + p) * gain
            ]
    column_out[...] = turned[...].T


def caption_slice(weight, s):
    cols = weight.shape[1] // 16
    return jnp.concatenate(
        [weight[:, (p * 8 + s) * cols : (p * 8 + s + 1) * cols] for p in range(2)], axis=1
    )


def caption_body(place, cap, weight, keep_out, send_out):
    for s in range(8):
        own = caption_slice(weight, s)
        j, k = (s % 2) ^ place[2], (s // 2 - place[1] + 4) % 4
        for r in range(4):
            part = dot(cap[place[0] ^ r], own).astype(bf16)
            if r % 2:
                send_out[r // 2, j, k] = part
            else:
                keep_out[r // 2, j, k] = part


def qkv_body(place, tokens, *refs):
    weights = refs[:4]
    vector, normed_out, proj_out, stats_out = refs[4:]
    total, width = tokens.shape
    step = total // 4
    block = width // 4
    cols = width // 8
    scale, gain = vector[0:1], vector[4:5]
    for b in range(4):
        at = slice(b * step, (b + 1) * step)
        value = tokens[at].astype(f32)
        inverse = rms_scale(jnp.mean(value * value, axis=1, keepdims=True))
        normed_out[at] = (value * inverse * gain * (1.0 + scale)).astype(bf16)
    for b in range(4):
        at = slice(b * step, (b + 1) * step)
        part = jnp.zeros((step, weights[0].shape[1]), f32)
        for r, weight in enumerate(weights):
            from_col = pl.multiple_of((place[0] ^ r) * block, 128)
            part = part + dot(normed_out[at, pl.ds(from_col, block)], weight[...])
        proj_out[:, at] = part.T
    stats_out[...] = jnp.zeros(stats_out.shape, f32)
    query, key = proj_out[:cols], proj_out[cols : 2 * cols]
    stats_out[0:1, :] = jnp.sum(query * query, axis=0, keepdims=True)
    stats_out[1:2, :] = jnp.sum(key * key, axis=0, keepdims=True)


def add_four_body(keep, got, *outs):
    for k, out in enumerate(outs):
        out[...] = (keep[k].astype(f32) + got[k].astype(f32)).astype(bf16)


def text_body(a, b, c, d, text_out, stats_out):
    total = four_sum([v[...].astype(f32) for v in (a, b, c, d)])
    text_out[...] = total.T
    key = text_out[: text_out.shape[0] // 2]
    stats_out[...] = jnp.broadcast_to(jnp.sum(key * key, axis=0, keepdims=True), stats_out.shape)


def turn(value, cosine, sine):
    half = value.shape[0] // 2
    front, back = value[:half], value[half:]
    return jnp.concatenate([front * cosine - back * sine, back * cosine + front * sine], axis=0)


def text_softmax(scores, length):
    place = lax.broadcasted_iota(jnp.int32, scores.shape, 0)
    scores = jnp.where(place < length, scores, -1e30)
    shifted = jnp.exp(scores - jnp.max(scores, axis=0, keepdims=True))
    return shifted / jnp.sum(shifted, axis=0, keepdims=True)


def attend_body(
    heads,
    proj,
    stats_a,
    stats_b,
    stats_c,
    stats_d,
    gains,
    cosine,
    sine,
    query_out,
    key_out,
    value_out,
    self_out,
    sum_out,
    stats_out,
):
    total = proj.shape[1]
    cols = query_out.shape[0]
    dim = cols // heads
    width = cols * 8
    step = total // 2
    score_scale = dim ** (-0.5)
    stats_out[...] = four_sum([stats_a[...], stats_b[...], stats_c[...], stats_d[...]])
    scales = rms_scale(stats_out[0:2, :] / width)
    value_out[...] = proj[2 * cols : 3 * cols].astype(bf16)
    sum_out[...] = jnp.zeros(sum_out.shape, f32)
    for h in range(heads):
        at = slice(h * dim, (h + 1) * dim)
        query = proj[at] * scales[0:1] * gains[at, 0:1]
        query_out[at] = turn(query, cosine[...], sine[...]).astype(bf16)
        key = proj[cols + h * dim : cols + (h + 1) * dim] * scales[1:2] * gains[at, 1:2]
        key_out[at] = turn(key, cosine[...], sine[...]).astype(bf16)
        key_rows = key_out[at].T
        for b in range(2):
            to = slice(b * step, (b + 1) * step)
            scores = dot(key_rows, query_out[at, to]) * score_scale
            most = jnp.max(scores, axis=0, keepdims=True)
            weights = jnp.exp(scores - most)
            whole = jnp.sum(weights, axis=0, keepdims=True)
            sum_out[h : h + 1, to] = most + jnp.log(whole)
            self_out[at, to] = dot(value_out[at], weights.astype(bf16)) * (1.0 / whole)


def cross_body(
    heads,
    gate,
    length,
    query,
    self_out,
    text,
    stats_a,
    stats_b,
    stats_c,
    stats_d,
    squares,
    gains,
    mixed_out,
    cross_out,
    text_key_out,
    text_value_out,
    stats_out,
):
    cols, total = query.shape
    dim = cols // heads
    width = cols * 8
    step = total // 2
    piece = mixed_out.shape[2]
    score_scale = dim ** (-0.5)
    text_stats = four_sum([stats_a[...], stats_b[...], stats_c[...], stats_d[...]])
    stats_out[...] = squares[...]
    stats_out[2:3, : text.shape[1]] = text_stats[0:1]
    text_scale = rms_scale(text_stats[0:1] / width)
    text_key_out[...] = (text[:cols] * text_scale * gains[:cols, 2:3]).astype(bf16)
    text_value_out[...] = text[cols : 2 * cols].astype(bf16)
    for h in range(heads):
        at = slice(h * dim, (h + 1) * dim)
        text_rows = text_key_out[at].T
        for b in range(2):
            to = slice(b * step, (b + 1) * step)
            text_weights = text_softmax(dot(text_rows, query[at, to]) * score_scale, length[0])
            cross = dot(text_value_out[at], text_weights.astype(bf16))
            cross_out[at, to] = cross
            mixed = (self_out[at, to] + gate[h] * cross).astype(bf16)
            for s in range(step // piece):
                mixed_out[b * (step // piece) + s, at] = mixed[:, s * piece : (s + 1) * piece]


def stack_body(*refs):
    rows = refs[0].shape[0]
    for i, piece in enumerate(refs[:-1]):
        refs[-1][i * rows : (i + 1) * rows] = piece[...]


def all_ahead(value):
    return [value] + [from_ahead(value, "z", k) for k in (1, 2, 3)]


def output_weight_body(place, *refs):
    own = refs[0].shape[0] // 8
    for r in range(4):
        for j in range(2):
            for k in range(4):
                owner = ((place[0] ^ r) * 4 + (place[1] ^ k)) * 2 + (place[2] ^ j)
                at = (j * 4 + k) * own
                refs[4][pl.ds(pl.multiple_of(owner * own, 16), own), :] = refs[r][at : at + own, :]


def output_body(
    mixed, weight, token, vector, proj_out, residual_out, normed_out, plane_out
):
    proj = dot_cols(mixed[...], weight[...])
    proj_out[...] = proj
    normed = proj * rms_scale(jnp.mean(proj * proj, axis=1, keepdims=True))
    residual = token[...].astype(f32) + vector[1:2] * normed * vector[5:6]
    residual_out[...] = residual
    normed = residual * rms_scale(jnp.mean(residual * residual, axis=1, keepdims=True))
    normed_out[...] = (normed * vector[6:7] * (1.0 + vector[2:3])).astype(bf16)
    own = plane_out.shape[1] // 4
    for g in range(8):
        for z in range(4):
            source = (((g // 2) * 4 + z) * 2 + g % 2) * own
            plane_out[g, z * own : (z + 1) * own] = mixed[source : source + own, :]


def spread_out(parts, own_out, mid_out, x_out, y_out):
    half = own_out.shape[0] // 2
    own, for_x, for_y, far = parts
    own_out[...] = own
    mid_out[:half] = for_y[:half]
    mid_out[half:] = for_x[half:]
    x_out[:half] = for_x[:half].astype(bf16)
    x_out[half:] = far[:half].astype(bf16)
    y_out[:half] = for_y[half:].astype(bf16)
    y_out[half:] = far[half:].astype(bf16)


def feed_body(*refs):
    pieces, gateups, downs = refs[:4], refs[4:6], refs[6:8]
    normed_out, gate_up_out, active_out = refs[8:11]
    rows = pieces[0].shape[0]
    hidden = downs[0].shape[0]
    step = rows * 2
    for r in range(4):
        normed_out[r * rows : (r + 1) * rows] = pieces[r][...]
    parts = []
    for b in range(2):
        at = slice(b * step, (b + 1) * step)
        total = None
        for core in range(2):
            both = dot(normed_out[at], gateups[core][...])
            gate_up_out[core, at] = both
            gate, up = both[:, :hidden], both[:, hidden:]
            active = (gate * jax.nn.sigmoid(gate) * up).astype(bf16)
            active_out[core, at] = active
            part = dot(active, downs[core][...])
            total = part if total is None else total + part
        parts += [total[:rows], total[rows:]]
    spread_out(parts, *refs[11:])


def scatter_two_body(own, mid, by_x, by_y, own_out, y_out, x_out):
    half = own.shape[0] // 2
    own_out[:half] = own[:half] + by_x[:half].astype(f32)
    own_out[half:] = own[half:] + by_y[:half].astype(f32)
    y_out[...] = (mid[:half] + by_x[half:].astype(f32)).astype(bf16)
    x_out[...] = (mid[half:] + by_y[half:].astype(f32)).astype(bf16)


def scatter_chips(line, own, mid, to_x, to_y, between=None):
    rows, width = own.shape
    by_x, by_y = flip(to_x, "x"), flip(to_y, "y")
    if between is not None:
        between()
    own, to_y, to_x = line(
        scatter_two_body,
        [((rows, width), f32), ((rows // 2, width), bf16), ((rows // 2, width), bf16)],
        own,
        mid,
        by_x,
        by_y,
    )
    return own, flip(to_y, "y"), flip(to_x, "x")


def whole_sum(own, by_y, by_x):
    half = own.shape[0] // 2
    return jnp.concatenate(
        [own[:half] + by_y[...].astype(f32), own[half:] + by_x[...].astype(f32)], axis=0
    )


def rms_pull(normed, inverse, grad):
    return (grad - normed * jnp.mean(grad * normed, axis=1, keepdims=True)) * inverse


def middle_body(own, by_y, by_x, residual, cot, vector, block_out, grad_out, sum_out):
    down = whole_sum(own, by_y, by_x)
    inverse = rms_scale(jnp.mean(down * down, axis=1, keepdims=True))
    normed = down * inverse
    gate, gain = vector[3:4], vector[7:8]
    block_out[...] = residual[...] + gate * normed * gain
    upstream = cot[...].astype(f32)
    sum_out[...] = jnp.broadcast_to(
        jnp.sum(upstream * normed, axis=0, keepdims=True), sum_out.shape
    )
    grad_out[...] = rms_pull(normed, inverse, upstream * gate * gain).astype(bf16)


def feed_back_body(*refs):
    pieces, gateups, downs, gate_up = refs[:4], refs[4:6], refs[6:8], refs[8]
    grad_out, hidden_out = refs[9:11]
    rows = pieces[0].shape[0]
    hidden = downs[0].shape[0]
    step = rows * 2
    for r in range(4):
        grad_out[r * rows : (r + 1) * rows] = pieces[r][...]
    parts = []
    for b in range(2):
        at = slice(b * step, (b + 1) * step)
        total = None
        for core in range(2):
            active_grad = dot_rows(grad_out[at], downs[core][...])
            gate, up = gate_up[core, at, :hidden], gate_up[core, at, hidden:]
            sigmoid = jax.nn.sigmoid(gate)
            gate_grad = active_grad * up * sigmoid * (1.0 + gate * (1.0 - sigmoid))
            hidden_out[core, at, :hidden] = gate_grad.astype(bf16)
            hidden_out[core, at, hidden:] = (active_grad * gate * sigmoid).astype(bf16)
            part = dot_rows(hidden_out[core, at], gateups[core][...])
            total = part if total is None else total + part
        parts += [total[:rows], total[rows:]]
    spread_out(parts, *refs[11:])


def feed_weight_body(active, down_grad, normed, hidden_grad, *outs):
    width = normed.shape[1]
    block = width // 4
    own = block // 4
    for core in range(2):
        down_out, gateup_out = outs[core], outs[2 + core]
        down_out[...] = dot_cols(active[core], down_grad[...]).astype(bf16)
        for c in range(4):
            part = dot_cols(normed[:, c * block : (c + 1) * block], hidden_grad[core]).astype(bf16)
            for z in range(4):
                gateup_out[z, c * own : (c + 1) * own] = part[z * own : (z + 1) * own]


def add_two_body(a, b, c, d, first_out, second_out):
    first_out[...] = (a[...].astype(f32) + b[...].astype(f32)).astype(bf16)
    second_out[...] = (c[...].astype(f32) + d[...].astype(f32)).astype(bf16)


def residual_back_body(
    own,
    by_y,
    by_x,
    residual,
    proj,
    cot,
    vector,
    weight,
    residual_grad_out,
    grad_out,
    mixed_out,
    sum_out,
):
    grad = whole_sum(own, by_y, by_x)
    value = residual[...]
    inverse = rms_scale(jnp.mean(value * value, axis=1, keepdims=True))
    normed = value * inverse
    sum_out[...] = jnp.zeros(sum_out.shape, f32)
    sum_out[1:2] = jnp.sum(grad * normed, axis=0, keepdims=True)
    grad = cot[...].astype(f32) + rms_pull(
        normed, inverse, grad * vector[6:7] * (1.0 + vector[2:3])
    )
    residual_grad_out[...] = grad
    value = proj[...]
    inverse = rms_scale(jnp.mean(value * value, axis=1, keepdims=True))
    normed = value * inverse
    sum_out[0:1] = jnp.sum(grad * normed, axis=0, keepdims=True)
    grad = rms_pull(normed, inverse, grad * vector[1:2] * vector[5:6]).astype(bf16)
    grad_out[...] = grad
    mixed_out[...] = dot_rows(weight[...], grad).astype(bf16)


def text_back_body(
    heads,
    gate,
    length,
    pieces,
    query,
    text_key,
    text_value,
    cross,
    text,
    stats,
    gains,
    grad_out,
    query_out,
    key_out,
    value_out,
    stats_out,
    gain_out,
    gate_out,
):
    cols, total = query.shape
    dim = cols // heads
    width = cols * 8
    step = total // 2
    score_scale = dim ** (-0.5)
    piece = pieces.shape[2]
    for s in range(pieces.shape[0]):
        grad_out[:, s * piece : (s + 1) * piece] = pieces[s]
    gate_out[...] = jnp.zeros(gate_out.shape, f32)
    for h in range(heads):
        at = slice(h * dim, (h + 1) * dim)
        text_rows, value_rows = text_key[at].T, text_value[at].T
        grad = grad_out[at].astype(f32)
        gate_sum = jnp.sum(jnp.sum(grad * cross[at], axis=0, keepdims=True), axis=1, keepdims=True)
        gate_out[h : h + 1, :] = jnp.broadcast_to(
            gate_sum * (1.0 - gate[h] * gate[h]), (1, gate_out.shape[1])
        )
        key_grad = jnp.zeros((dim, text_key.shape[1]), f32)
        value_grad = jnp.zeros((dim, text_key.shape[1]), f32)
        for b in range(2):
            to = slice(b * step, (b + 1) * step)
            block, back = query[at, to], grad_out[at, to]
            weights = text_softmax(dot(text_rows, block) * score_scale, length[0])
            upstream = dot(value_rows, back) * gate[h]
            center = jnp.sum(weights * upstream, axis=0, keepdims=True)
            score_grad = (weights * (upstream - center)).astype(bf16)
            query_out[at, to] = dot(text_key[at], score_grad)
            key_grad = key_grad + dot_rows(block, score_grad)
            value_grad = value_grad + dot_rows(back, weights.astype(bf16))
        key_out[at] = key_grad * score_scale
        value_out[at] = value_grad * gate[h]
    text_scale = rms_scale(stats[2:3, : text.shape[1]] / width)
    normed = text[:cols] * text_scale
    gain_out[...] = jnp.zeros(gain_out.shape, f32)
    gain_out[:cols] = jnp.broadcast_to(
        jnp.sum(key_out[...] * normed, axis=1, keepdims=True), (cols, gain_out.shape[1])
    )
    key_out[...] = key_out[...] * gains[:cols, 2:3]
    stats_out[...] = jnp.broadcast_to(
        jnp.sum(key_out[...] * normed, axis=0, keepdims=True), stats_out.shape
    )


def text_proj_back_body(key, value, text, stats, means, grad_out):
    cols = key.shape[0]
    width = cols * 8
    text_scale = rms_scale(stats[2:3, : text.shape[1]] / width)
    normed = text[:cols] * text_scale
    mean = eight_sum(means)[2:3, : text.shape[1]] / width
    before = (key[...] - normed * mean) * text_scale
    grad_out[...] = jnp.concatenate([before, value[...]], axis=0).T.astype(bf16)


def caption_back_body(place, cap, *refs):
    grads, (weight, cond, weight_out, piece_out, blocks) = refs[:4], refs[4:]
    cols = weight.shape[1] // 16
    rows = cap.shape[1]
    own_rows = rows // 8
    for j in range(2):
        for k in range(4):
            at = slice((j * 4 + k) * rows, (j * 4 + k + 1) * rows)
            part = None
            for r in range(4):
                term = dot_cols(cap[place[0] ^ r], grads[r][at, :])
                part = term if part is None else part + term
            blocks[(place[1] + k) % 4 * 2 + (place[2] ^ j)] = part
    for s in range(8):
        for p in range(2):
            weight_out[:, (p * 8 + s) * cols : (p * 8 + s + 1) * cols] = blocks[
                s, :, p * cols : (p + 1) * cols
            ]
    for s in range(8):
        blocks[s] = caption_slice(weight, s).astype(f32)
    for r in range(4):
        clip = place[0] ^ r
        total = None
        for j in range(2):
            for k in range(4):
                at = slice((j * 4 + k) * rows, (j * 4 + k + 1) * rows)
                own = blocks[(place[1] + k) % 4 * 2 + (place[2] ^ j)].astype(bf16)
                term = dot_rows(grads[r][at, :], own)
                total = term if total is None else total + term
        for s in range(8):
            piece_out[clip * 8 + s, :own_rows] = total[s * own_rows : (s + 1) * own_rows]
            piece_out[clip * 8 + s, own_rows:] = cond[clip]


def attend_back_body(
    heads,
    grad,
    query,
    key,
    value,
    self_out,
    sums,
    text_query,
    text_stats,
    proj,
    stats,
    gains,
    cosine,
    sine,
    query_in_out,
    key_in_out,
    value_grad_out,
    stats_out,
    gain_out,
):
    cols, total = query.shape
    dim = cols // heads
    width = cols * 8
    step = total // 2
    score_scale = dim ** (-0.5)
    scales = rms_scale(stats[0:2, :] / width)
    stats_out[0] = jnp.zeros(stats_out.shape[1:], f32)
    gain_out[...] = jnp.zeros(gain_out.shape, f32)
    query_total = jnp.zeros((1, total), f32)
    key_total = jnp.zeros((1, total), f32)
    for h in range(heads):
        at = slice(h * dim, (h + 1) * dim)
        key_rows, value_rows = key[at].T, value[at].T
        delta = jnp.sum(grad[at].astype(f32) * self_out[at], axis=0, keepdims=True)
        key_grad = jnp.zeros((dim, total), f32)
        value_grad = jnp.zeros((dim, total), f32)
        query_parts = []
        for b in range(2):
            to = slice(b * step, (b + 1) * step)
            block, back = query[at, to], grad[at, to]
            weights = jnp.exp(dot(key_rows, block) * score_scale - sums[h : h + 1, to])
            value_grad = value_grad + dot_rows(back, weights.astype(bf16))
            score_grad = (weights * (dot(value_rows, back) - delta[:, to])).astype(bf16)
            key_grad = key_grad + dot_rows(block, score_grad)
            query_parts.append(dot(key[at], score_grad))
        value_grad_out[at] = value_grad.astype(bf16)
        query_grad = (jnp.concatenate(query_parts, axis=1) + text_query[at]) * score_scale
        query_grad = turn(query_grad, cosine[...], -sine[...])
        key_grad = turn(key_grad * score_scale, cosine[...], -sine[...])
        query_normed = proj[at] * scales[0:1]
        key_normed = proj[cols + h * dim : cols + (h + 1) * dim] * scales[1:2]
        gain_out[at, 0:1] = jnp.sum(query_grad * query_normed, axis=1, keepdims=True)
        gain_out[at, 1:2] = jnp.sum(key_grad * key_normed, axis=1, keepdims=True)
        query_grad = query_grad * gains[at, 0:1]
        key_grad = key_grad * gains[at, 1:2]
        query_in_out[at] = query_grad
        key_in_out[at] = key_grad
        query_total = query_total + jnp.sum(query_grad * query_normed, axis=0, keepdims=True)
        key_total = key_total + jnp.sum(key_grad * key_normed, axis=0, keepdims=True)
    stats_out[0, 0:1, :] = query_total
    stats_out[0, 1:2, :] = key_total
    stats_out[0, 2:3, : text_stats.shape[1]] = text_stats[0:1]
    spread(stats_out)


def project_back_body(place, *refs):
    tokens, weights = refs[0], refs[1:5]
    query_in, key_in, value_grad, proj, stats = refs[5:10]
    mean_parts, normed, vector = refs[10:13]
    middle_sums, residual_sums, own_gains, text_gains, gate_sums = refs[13:18]
    part_out, near_out, far_out, sums_out = refs[18:22]
    low, turned, unit, sum_out = refs[22:]
    cols, total = query_in.shape
    width = normed.shape[1]
    block = width // 4
    rows = total // 8
    scales = rms_scale(stats[0:2, :] / width)
    means = eight_sum(mean_parts) / width
    low[...] = jnp.zeros(low.shape, bf16)
    low[:cols] = (
        (query_in[...] - proj[:cols] * scales[0:1] * means[0:1, :]) * scales[0:1]
    ).astype(bf16)
    low[cols : 2 * cols] = (
        (key_in[...] - proj[cols : 2 * cols] * scales[1:2] * means[1:2, :]) * scales[1:2]
    ).astype(bf16)
    low[2 * cols : 3 * cols] = value_grad[...]
    turned[...] = low[...].T
    sum_out[...] = jnp.zeros(sum_out.shape, f32)
    for b in range(4):
        at = slice(b * 2 * rows, (b + 1) * 2 * rows)
        value = tokens[at].astype(f32)
        unit[...] = value * rms_scale(jnp.mean(value * value, axis=1, keepdims=True))
        for r in range(4):
            to_col = pl.ds(pl.multiple_of((place[0] ^ r) * block, 128), block)
            part = dot_rows(turned[at], weights[r][...])
            sum_out[0:1, to_col] = sum_out[0:1, to_col] + jnp.sum(
                part * unit[:, to_col], axis=0, keepdims=True
            )
            part_out[at, to_col] = part.astype(bf16)
    for r in range(4):
        from_col = pl.ds(pl.multiple_of((place[0] ^ r) * block, 128), block)
        part = dot(low[...], normed[:, from_col]).T.astype(bf16)
        if r % 2:
            far_out[r // 2] = part
        else:
            near_out[r // 2] = part
    sum_out[1:3] = residual_sums[0:2]
    sum_out[3:4] = middle_sums[0:1]
    lane = lax.broadcasted_iota(jnp.int32, (1, width), 1)
    mine = lane // cols == place[5]
    own_rows, text_row = own_gains[...].T, text_gains[...].T
    for at, row in ((4, own_rows[0:1]), (5, own_rows[1:2]), (6, text_row[0:1])):
        wide = jnp.concatenate([row[:, :cols]] * 8, axis=1)
        sum_out[at : at + 1] = jnp.where(mine, wide, 0.0)
    heads = 3
    gates = jnp.zeros((1, width), f32)
    for h in range(heads):
        gates = jnp.where(lane == place[5] * heads + h, gate_sums[h : h + 1, 0:1], gates)
    sum_out[7:8] = gates
    for s in range(8):
        sums_out[s] = sum_out[...]


def add_body(a, b, out):
    out[...] = (a[...].astype(f32) + b[...].astype(f32)).astype(bf16)


def add_pair_body(keep, got, keep_out, send_out):
    keep_out[...] = (keep[0].astype(f32) + got[0].astype(f32)).astype(bf16)
    send_out[...] = (keep[1].astype(f32) + got[1].astype(f32)).astype(bf16)


def final_body(grad_normed, residual_grad, token, vector, out):
    grad = grad_normed[...].astype(f32)
    value = token[...].astype(f32)
    inverse = rms_scale(jnp.mean(value * value, axis=1, keepdims=True))
    out[...] = residual_grad[...] + rms_pull(
        value * inverse, inverse, grad * vector[4:5] * (1.0 + vector[0:1])
    )


def modulation_back_body(parts, vector, shared_out):
    sums = eight_sum(parts)
    width = sums.shape[1]
    scale_attn, gate_attn, scale_ffn, gate_ffn = [vector[i : i + 1] for i in range(4)]
    gains = [vector[4 + i : 5 + i] for i in range(4)]
    zero, one, two, three = [sums[i : i + 1] for i in range(4)]
    rows = [
        gains[0] * zero,
        gains[1] * one * (1.0 - gate_attn * gate_attn),
        gains[2] * two,
        gains[3] * three * (1.0 - gate_ffn * gate_ffn),
    ]
    shared_out[...] = jnp.zeros(shared_out.shape, f32)
    for i in range(4):
        shared_out[i : i + 1] = rows[i]
    shared_out[4:5] = (1.0 + scale_attn) * zero
    shared_out[5:6] = gate_attn * one
    shared_out[6:7] = (1.0 + scale_ffn) * two
    shared_out[7:8] = gate_ffn * three
    shared_out[8:12] = sums[4:8]


def modulation_weight_body(
    place, t0, t1, t2, t3, p0, p1, p2, p3, weight_out, total_out, cond_out, square
):
    width = t0.shape[1]
    rows = weight_out.shape[0]
    span = 4 * width
    owner = owner_of(place, 0)
    total_out[...] = (t0[...] + t1[...]) + (t2[...] + t3[...])
    lane = lax.broadcasted_iota(jnp.int32, (rows, square.shape[0]), 1)
    columns = []
    for piece in (p0, p1, p2, p3):
        cond = piece[:, span + 256 : span + 384].astype(f32)
        cond = (cond / (1.0 + jnp.exp(-cond))).astype(bf16).astype(f32)
        square[...] = jnp.zeros(square.shape, f32)
        square[:rows] = cond
        turned = square[...].T[:rows]
        columns.append(jnp.sum(jnp.where(lane == owner, turned, 0.0), axis=1, keepdims=True))
    for i in range(4):
        part = None
        for column, shared in zip(columns, (t0, t1, t2, t3)):
            term = column * shared[i : i + 1, :]
            part = term if part is None else part + term
        weight_out[:, i * width : (i + 1) * width] = part
    lanes = cond_out.shape[2]
    for r, shared in enumerate((t0, t1, t2, t3)):
        back = jnp.zeros((8, rows), f32)
        for i in range(4):
            back = back + lax.dot_general(
                jnp.broadcast_to(shared[i : i + 1, :], (8, width)),
                p0[:, i * width : (i + 1) * width].astype(f32),
                (((1,), (1,)), ((), ())),
                precision=highest,
                preferred_element_type=f32,
            )
        cond_out[place[0] ^ r] = jnp.concatenate(
            [back, jnp.zeros((8, lanes - rows), f32)], axis=1
        )


def attention_grad_body(pieces, grad_out):
    cols = grad_out.shape[1] // 24
    for s in range(8):
        for p in range(3):
            grad_out[:, (p * 8 + s) * cols : (p * 8 + s + 1) * cols] = pieces[
                s, :, p * cols : (p + 1) * cols
            ].astype(f32)


def gateup_grad_body(pieces, grad_out):
    own = grad_out.shape[1] // 64
    for g in range(8):
        for part in range(2):
            for z in range(4):
                target = (part * 32 + (g // 2) * 8 + z * 2 + g % 2) * own
                source = (part * 4 + z) * own
                grad_out[:, target : target + own] = pieces[g, :, source : source + own].astype(f32)


def caption_grad_body(pieces, grad_out, cond_out):
    own = pieces.shape[2]
    rows = grad_out.shape[0]
    for o in range(32):
        grad_out[:, o * own : (o + 1) * own] = pieces[o, :rows]
        cond_out[o : o + 1] = pieces[o, rows : rows + 1]


def output_grad_body(place, mixed, *refs):
    grads, weight_outs, held, done = refs[:8], refs[8:12], refs[12], refs[13]
    rows = mixed.shape[2]
    copies = [
        pltpu.make_async_copy(grads[r], held.at[pl.ds(r * rows, rows)], done.at[r])
        for r in range(8)
    ]
    for copy in copies:
        copy.start()
    total = None
    for r in range(8):
        copies[r].wait()
        core, y, x = r // 4, (r // 2) % 2, r % 2
        source = ((place[3] ^ y) * 2 + (place[4] ^ core)) * 2 + (place[2] ^ x)
        part = dot(mixed[source], held[r * rows : (r + 1) * rows])
        total = part if total is None else total + part
    own = total.shape[0] // 4
    held[: total.shape[0]] = total.astype(bf16)
    for k in range(4):
        source = pl.multiple_of((place[1] + k) % 4 * own, 16)
        weight_outs[k][...] = held[pl.ds(source, own), :]


def output_sum_body(a, b, c, d, out):
    out[...] = four_sum([v[...].astype(f32) for v in (a, b, c, d)])


def local_fast(
    tokens,
    caption,
    condition,
    caption_len,
    frame_shape,
    rope_shift,
    w_modulation,
    mod_bias,
    w_attention,
    w_output,
    w_caption,
    norm_gains,
    head_gate,
    w_gateup,
    w_down,
    cotangent,
):
    seq_axes = ("z", "x")
    all_axes = ("y", "core") + seq_axes
    plane_axes = ("y", "core", "x")
    rows, width = tokens.shape[1:]
    total = rows * 8
    heads = head_gate.shape[0]
    head_dim = width // heads
    own_heads = heads // 8
    cols = own_heads * head_dim
    wide_cols = round_up(3 * cols)
    text_rows = caption.shape[1]
    text_total = text_rows * 8
    attn_rows = w_attention.shape[0]
    z_at, x_at = lax.axis_index("z"), lax.axis_index("x")
    y_at, core_at = lax.axis_index("y"), lax.axis_index("core")
    seq_at = z_at * 2 + x_at
    clip_at = y_at * 2 + core_at
    owner = clip_at * 8 + seq_at
    place = jnp.stack([clip_at, z_at, x_at, y_at, core_at, seq_at]).astype(jnp.int32)

    line = Line()
    own_tokens = tokens[0]
    token_all = lax.all_gather(own_tokens, seq_axes, axis=0, tiled=True)

    cap_cols = w_caption.shape[0]
    hidden_own = w_down.shape[0]
    hidden = 4 * hidden_own
    cond_rows, span = w_modulation.shape
    bias_len = mod_bias.shape[0]
    gain_cols = norm_gains.shape[1]
    cond_square = condition.reshape(32, cond_rows)
    extra = jnp.concatenate(
        [
            jnp.pad(mod_bias[None], ((0, 31), (0, 256 - bias_len)))
            + jnp.pad(norm_gains, ((8, 17), (0, 256 - gain_cols))),
            jnp.pad(cond_square, ((0, 0), (0, 128 - cond_rows))),
        ],
        axis=1,
    )
    attn_piece, ffn_piece, cap_piece, mod_piece = alone(
        prep_body,
        [
            ((8, attn_rows, wide_cols), bf16),
            ((8, w_gateup.shape[0], 8 * hidden_own), bf16),
            ((32, text_rows, cap_cols), bf16),
            ((cond_rows, span + 384), bf16),
        ],
        w_attention,
        w_gateup,
        caption[0],
        w_modulation,
        extra,
    )
    mod_y, mod_core = flip(mod_piece, "y"), flip(mod_piece, "core")
    attn_0 = lax.all_to_all(attn_piece, seq_axes, 0, 0, tiled=True).reshape(-1, wide_cols)
    mod_piece, mod_y, mod_core, attn_0, cap_piece, ffn_piece = together(
        mod_piece, mod_y, mod_core, attn_0, cap_piece, ffn_piece
    )

    mod_parts = [mod_piece, mod_core, mod_y, flip(mod_y, "core")]
    attn_2, attn_1 = flip(attn_0, "y"), flip(attn_0, "core")
    cap_all = lax.all_to_all(cap_piece, all_axes, 0, 0, tiled=True)
    (small,) = line(
        modulate_body,
        [((32, 640), f32)],
        place,
        cond_square.astype(f32),
        *mod_parts,
        scalars=1,
    )
    vector, own_gains = line(
        vector_body,
        [((16, width), f32), ((256, 128), f32)],
        place,
        *seq_terms(small),
        scalars=1,
        scratch=[pltpu.VMEM((32, 640), f32), pltpu.VMEM((128, 256), f32)],
    )
    vector, attn_0, attn_1, attn_2, cap_all, ffn_piece, own_out, w_down = together(
        vector, attn_0, attn_1, attn_2, cap_all, ffn_piece, w_output, w_down
    )

    cap_all = cap_all.reshape(4, text_total, cap_cols)
    attn_3 = flip(attn_2, "core")
    four_text = (4, text_total, 2 * cols)
    cap_keep, cap_send = line(
        caption_body,
        [((2, 2) + four_text, bf16)] * 2,
        place,
        cap_all,
        w_caption,
        scalars=1,
    )
    out_near = swap_z(own_out, 1)
    ffn_piece = lax.all_to_all(ffn_piece, plane_axes, 0, 0, tiled=True)
    block = 2 * ffn_piece.shape[1]
    cap_keep, cap_send = line(
        add_pair_body, [((2,) + four_text, bf16)] * 2, cap_keep, flip(cap_send, "core")
    )
    attn_3, cap_send, cap_keep = together(attn_3, cap_send, cap_keep)

    attn_parts = (attn_0, attn_1, attn_2, attn_3)
    cap_send = flip(cap_send, "y")
    normed_all, projected, squares = line(
        qkv_body,
        [((total, width), bf16), ((wide_cols, total), f32), ((8, total), f32)],
        place,
        token_all,
        *attn_parts,
        vector,
        scalars=1,
    )
    squares = seq_terms(squares)
    (out_pair,) = line(
        stack_body, [((2 * attn_rows, width), bf16)], own_out, out_near, after=(squares[0],)
    )
    out_far = swap_z(out_pair, 2)
    cap_keep, cap_send = line(add_pair_body, [(four_text, bf16)] * 2, cap_keep, cap_send)
    cap_send = flip(cap_send, "x")
    text_parts = line(
        add_four_body, [(four_text[1:], bf16)] * 4, cap_keep, cap_send, after=tuple(squares[1:])
    )
    out_far, squares, text_parts, ffn_piece = together(out_far, squares, text_parts, ffn_piece)
    own_gateup = lax.all_gather(ffn_piece.reshape(4, block, -1), "z", axis=0)

    text_parts = [text_parts[0]] + [from_ahead(text_parts[4 - k], "z", k) for k in (1, 2, 3)]
    (out_z,) = line(stack_body, [((4 * attn_rows, width), bf16)], out_pair, out_far)
    out_x = flip(out_z, "x")

    head_low = lax.dynamic_slice_in_dim(head_gate, seq_at * own_heads, own_heads)
    tanh_gate = jnp.tanh(head_low.astype(f32))
    position = jnp.arange(total, dtype=jnp.int32)
    angles = rope_angles(frame_shape[0], rope_shift[0], position, head_dim // 2).T
    cosine = jnp.cos(angles)
    sine = jnp.sin(angles)
    flat = (cols, total)
    queries, key_rows, values, self_out, log_sum, squares = line(
        functools.partial(attend_body, own_heads),
        [
            (flat, bf16),
            (flat, bf16),
            (flat, bf16),
            (flat, f32),
            ((8, total), f32),
            ((8, total), f32),
        ],
        projected,
        *squares,
        own_gains,
        cosine,
        sine,
    )
    self_out, out_x = together(self_out, out_x)
    (out_0,) = line(stack_body, [((8 * attn_rows, width), bf16)], out_z, out_x)
    out_2 = flip(out_0, "y")

    text_proj, text_squares = line(
        text_body, [((2 * cols, text_total), f32), ((8, text_total), f32)], *text_parts
    )
    text_squares = seq_terms(text_squares)
    mixed_pieces, cross_out, text_keys, text_values, squares = line(
        functools.partial(cross_body, own_heads),
        [
            ((8, cols, rows), bf16),
            (flat, f32),
            ((cols, text_total), bf16),
            ((cols, text_total), bf16),
            ((8, total), f32),
        ],
        tanh_gate,
        caption_len,
        queries,
        self_out,
        text_proj,
        *text_squares,
        squares,
        own_gains,
        scalars=2,
    )
    mixed_pieces, out_2, out_0 = together(mixed_pieces, out_2, out_0)
    mixed_own = lax.all_to_all(mixed_pieces, seq_axes, 0, 0, tiled=True).reshape(width, rows)
    out_1, out_3 = flip(out_0, "core"), flip(out_2, "core")
    (full_out,) = line(
        output_weight_body,
        [((width, width), bf16)],
        place,
        out_0,
        out_1,
        out_2,
        out_3,
        scalars=1,
    )
    own_gateup, mixed_own, w_down, full_out = together(own_gateup, mixed_own, w_down, full_out)
    own_down = lax.all_gather(w_down, "z", axis=0, tiled=True)
    own_gateup = jnp.transpose(own_gateup, (1, 0, 2, 3)).reshape(width, -1)
    gateups = (own_gateup, flip(own_gateup, "core"))
    own_shape = (rows, width)
    attn_proj, residual, normed_ffn, mixed_plane = line(
        output_body,
        [
            (own_shape, f32),
            (own_shape, f32),
            (own_shape, bf16),
            ((8, 4 * attn_rows, rows), bf16),
        ],
        mixed_own,
        full_out,
        own_tokens,
        vector,
    )

    chip_shape = (4 * rows, width)
    on_way = [(own_shape, f32), (own_shape, f32), (own_shape, bf16), (own_shape, bf16)]
    normed_parts = gather_chips(normed_ffn)
    own_down = together(own_down, normed_parts[1], normed_parts[3])[0]
    downs = (own_down, flip(own_down, "core"))
    normed_ffn_all, gate_up, activated, *parts = line(
        feed_body,
        [
            (chip_shape, bf16),
            ((2, 4 * rows, 2 * hidden), f32),
            ((2, 4 * rows, hidden), bf16),
        ]
        + on_way,
        *normed_parts,
        *gateups,
        *downs,
    )
    block_out, grad_down, middle_sums = line(
        middle_body,
        [(own_shape, f32), (own_shape, bf16), ((8, width), f32)],
        *scatter_chips(line, *parts),
        residual,
        cotangent[0],
        vector,
    )

    grad_down_all, grad_gate_up, *parts = line(
        feed_back_body,
        [(chip_shape, bf16), ((2, 4 * rows, 2 * hidden), bf16)] + on_way,
        *gather_chips(grad_down),
        *gateups,
        *downs,
        gate_up,
    )
    ffn_grads = []

    def feed_weights():
        ffn_grads.extend(
            line(
                feed_weight_body,
                [((hidden, width), bf16)] * 2 + [((4, 4 * block, 2 * hidden), bf16)] * 2,
                activated,
                grad_down_all,
                normed_ffn_all,
                grad_gate_up,
            )
        )

    ffn_parts = scatter_chips(line, *parts, feed_weights)
    down_got, gateup_got = flip(ffn_grads[1], "core"), flip(ffn_grads[3], "core")

    wgrad_down, wgrad_gateup = line(
        add_two_body,
        [((hidden, width), bf16), ((4, 4 * block, 2 * hidden), bf16)],
        ffn_grads[0],
        down_got,
        ffn_grads[2],
        gateup_got,
    )
    wgrad_gateup = lax.psum_scatter(wgrad_gateup, "z", scatter_dimension=0, tiled=False)
    wgrad_down = lax.psum_scatter(wgrad_down, "z", scatter_dimension=0, tiled=True)

    grad_residual, grad_attn, grad_mixed, residual_sums = line(
        residual_back_body,
        [(own_shape, f32), (own_shape, bf16), ((width, rows), bf16), ((8, width), f32)],
        *ffn_parts,
        residual,
        attn_proj,
        cotangent[0],
        vector,
        full_out,
    )
    grad_pieces = lax.all_to_all(grad_mixed.reshape(8, cols, rows), seq_axes, 0, 0, tiled=True)
    grad_by_x, grad_by_y = flip(grad_attn, "x"), flip(grad_attn, "y")
    grad_pieces, grad_by_x, grad_by_y, mixed_plane = together(
        grad_pieces, grad_by_x, grad_by_y, mixed_plane
    )
    mixed_plane = lax.all_to_all(mixed_plane, plane_axes, 0, 0, tiled=True)
    grad_far = flip(grad_by_y, "x")

    (
        grad_mixed,
        text_query,
        text_key_in,
        text_value_grad,
        text_stats,
        text_gain,
        gate_sum,
    ) = line(
        functools.partial(text_back_body, own_heads),
        [
            (flat, bf16),
            (flat, f32),
            ((cols, text_total), f32),
            ((cols, text_total), f32),
            ((8, text_total), f32),
            ((256, 128), f32),
            ((8, 128), f32),
        ],
        tanh_gate,
        caption_len,
        grad_pieces,
        queries,
        text_keys,
        text_values,
        cross_out,
        text_proj,
        squares,
        own_gains,
        scalars=2,
    )
    query_in, key_in, value_grad, means, own_gain_sums = line(
        functools.partial(attend_back_body, own_heads),
        [
            (flat, f32),
            (flat, f32),
            (flat, bf16),
            ((8, 8, total), f32),
            ((256, 128), f32),
        ],
        grad_mixed,
        queries,
        key_rows,
        values,
        self_out,
        log_sum,
        text_query,
        text_stats,
        projected,
        squares,
        own_gains,
        cosine,
        sine,
    )
    means, mixed_plane = together(means, mixed_plane)
    means = share(means)
    (grad_text_proj,) = line(
        text_proj_back_body,
        [((text_total, 2 * cols), bf16)],
        text_key_in,
        text_value_grad,
        text_proj,
        squares,
        means,
    )
    means, grad_text_proj, grad_far = together(means, grad_text_proj, grad_far)

    text_parts = all_ahead(grad_text_proj)
    quarter = width // 4
    grad_normed, near_part, far_part, sums = line(
        project_back_body,
        [((total, width), bf16)]
        + [((2, quarter, wide_cols), bf16)] * 2
        + [((8, 8, width), f32)],
        place,
        token_all,
        *attn_parts,
        query_in,
        key_in,
        value_grad,
        projected,
        squares,
        means,
        normed_all,
        vector,
        middle_sums,
        residual_sums,
        own_gain_sums,
        text_gain,
        gate_sum,
        scalars=1,
        scratch=[
            pltpu.VMEM((wide_cols, total), bf16),
            pltpu.VMEM((total, wide_cols), bf16),
            pltpu.VMEM((2 * rows, width), f32),
            pltpu.VMEM((8, width), f32),
        ],
    )
    grad_normed, far_part, sums, text_parts = together(grad_normed, far_part, sums, text_parts)

    grad_normed = lax.psum_scatter(grad_normed, seq_axes, scatter_dimension=0, tiled=True)
    (text_z,) = line(stack_body, [((4 * text_total, 2 * cols), bf16)], *text_parts)
    text_x = flip(text_z, "x")
    far_part = flip(far_part, "core")
    wide = (quarter, wide_cols)
    near_part, far_part = line(add_pair_body, [(wide, bf16)] * 2, near_part, far_part)
    far_part, text_x, sums = together(far_part, text_x, sums)

    far_part = flip(far_part, "y")
    sums = share(sums)
    (text_seq,) = line(stack_body, [((8 * text_total, 2 * cols), bf16)], text_z, text_x)
    far_part, text_seq = together(far_part, text_seq)

    text_y, text_core = flip(text_seq, "y"), flip(text_seq, "core")
    (wgrad_attention,) = line(add_body, [(wide, bf16)], near_part, far_part)
    (shared,) = line(modulation_back_body, [((16, width), f32)], sums, vector)
    shared_y, shared_core = flip(shared, "y"), flip(shared, "core")
    wgrad_attention = together(wgrad_attention, sums)[0]
    wgrad_attention = lax.all_to_all(
        wgrad_attention.reshape(8, attn_rows, wide_cols), seq_axes, 0, 0, tiled=True
    )
    shared_y, shared_core, text_core, text_y, grad_attn, grad_by_x, grad_by_y, grad_far = together(
        shared_y, shared_core, text_core, text_y, grad_attn, grad_by_x, grad_by_y, grad_far
    )

    grad_attn_parts = [grad_attn, grad_by_x, grad_by_y, grad_far]
    grad_attn_parts = grad_attn_parts + [flip(piece, "core") for piece in grad_attn_parts]
    wgrad_modulation, shared, cond_back = line(
        modulation_weight_body,
        [(w_modulation.shape, f32), ((16, width), f32), ((4, 8, cap_cols), f32)],
        place,
        shared,
        shared_core,
        shared_y,
        flip(shared_y, "core"),
        *mod_parts,
        scalars=1,
        scratch=[pltpu.VMEM((128, 128), f32)],
    )
    wgrad_caption, cap_pieces = line(
        caption_back_body,
        [(w_caption.shape, f32), ((32, text_rows + 8, cap_cols), f32)],
        place,
        cap_all,
        text_seq,
        text_core,
        text_y,
        flip(text_y, "core"),
        w_caption,
        cond_back,
        scalars=1,
        scratch=[pltpu.VMEM((8, cap_cols, 2 * cols), f32)],
    )
    cap_pieces, wgrad_attention = together(cap_pieces, wgrad_attention)

    cap_pieces = lax.all_to_all(cap_pieces, all_axes, 0, 0, tiled=True)
    wgrad_parts = line(
        output_grad_body,
        [((attn_rows, width), bf16)] * 4,
        place,
        mixed_plane,
        *grad_attn_parts,
        scalars=1,
        far=8,
        scratch=[pltpu.VMEM((total, width), bf16), pltpu.SemaphoreType.DMA((8,))],
    )
    wgrad_parts = [wgrad_parts[0]] + [from_ahead(wgrad_parts[4 - k], "z", k) for k in (1, 2, 3)]
    (wgrad_attention,) = line(attention_grad_body, [(w_attention.shape, f32)], wgrad_attention)
    cap_pieces, wgrad_gateup = together(cap_pieces, wgrad_gateup)

    wgrad_gateup = lax.all_to_all(
        wgrad_gateup.reshape(8, block // 2, -1), plane_axes, 0, 0, tiled=True
    )
    wgrad_gateup, wgrad_parts = together(wgrad_gateup, wgrad_parts)
    grad_caption, cond_back = line(
        caption_grad_body, [((text_rows, 32 * cap_cols), f32), ((32, cap_cols), f32)], cap_pieces
    )
    (wgrad_output,) = line(output_sum_body, [((attn_rows, width), f32)], *wgrad_parts)
    (wgrad_gateup,) = line(gateup_grad_body, [(w_gateup.shape, f32)], wgrad_gateup)
    (grad_tokens,) = line(
        final_body, [(own_shape, f32)], grad_normed, grad_residual, own_tokens, vector
    )
    bias_grad = lax.dynamic_slice(shared, (clip_at, seq_at * bias_len), (1, bias_len))[0]
    gain_grads = lax.dynamic_slice(shared, (4, owner * gain_cols), (7, gain_cols))
    grad_gate_total = shared[11, :heads]
    cond_back = cond_back[:, :cond_rows].reshape(1, -1)
    cond_float = condition.astype(f32)
    cond_sigmoid = jax.nn.sigmoid(cond_float)
    grad_condition = cond_back * cond_sigmoid * (1.0 + cond_float * (1.0 - cond_sigmoid))

    return (
        block_out[None],
        grad_tokens[None],
        grad_caption[None],
        grad_condition,
        wgrad_modulation,
        bias_grad,
        wgrad_attention,
        wgrad_output,
        wgrad_caption,
        gain_grads,
        grad_gate_total,
        wgrad_gateup,
        wgrad_down.astype(f32),
    )


def specs(clip, seq):
    both = clip + seq
    placed = (
        P(clip, seq, None),
        P(clip, seq, None),
        P(clip, None),
        P(clip),
        P(clip, None),
        P(clip, None),
        P(both, None),
        P(both),
        P(both, None),
        P(both, None),
        P(both, None),
        P(None, both),
        P(),
        P(both, None),
        P(both, None),
        P(clip, seq, None),
    )
    given = (
        P(clip, seq, None),
        P(clip, seq, None),
        P(clip, seq, None),
        P(clip, None),
        P(both, None),
        P(both),
        P(both, None),
        P(both, None),
        P(both, None),
        P(None, both),
        P(),
        P(both, None),
        P(both, None),
    )
    return placed, given


def solution(mesh):
    if dict(mesh.shape) == {"clip": 4, "seq": 8}:
        grid = Mesh(mesh.devices.reshape(2, 2, 4, 2), ("y", "core", "z", "x"))
        placed, given = specs(("y", "core"), ("z", "x"))
        return jax.shard_map(
            local_fast, mesh=grid, in_specs=placed, out_specs=given, check_vma=False
        )
    placed, given = specs(("clip",), ("seq",))
    return jax.shard_map(local, mesh=mesh, in_specs=placed, out_specs=given, check_vma=False)
```

```python
import functools
import math

import jax
import jax.numpy as jnp
from jax import lax
from jax.experimental import pallas as pl
from jax.experimental.pallas import tpu as pltpu
from jax.sharding import Mesh
from jax.sharding import PartitionSpec as P

epsilon = 1e-06
theta_base = 10000.0
highest = lax.Precision.HIGHEST
bf16 = jnp.bfloat16
f32 = jnp.float32


def rms_norm(value):
    return value * lax.rsqrt(jnp.mean(value * value, axis=-1, keepdims=True) + epsilon)


def rms_back(value, upstream):
    return jax.vjp(rms_norm, value)[1](upstream)[0]


def rope_angles(shape_row, shift_row, position, half_dim):
    across = shape_row[2] + 1
    column_place = position % across + shift_row[2]
    row_place = position // across % shape_row[1] + shift_row[1]
    frame_place = position // (across * shape_row[1]) + shift_row[0]
    frame_count = half_dim // 4
    row_count = 3 * half_dim // 8
    column_count = half_dim - frame_count - row_count
    pieces = []
    for place_index, group_size in (
        (frame_place, frame_count),
        (row_place, row_count),
        (column_place, column_count),
    ):
        frequency = theta_base ** (-jnp.arange(group_size, dtype=jnp.float32) / group_size)
        pieces.append(place_index.astype(jnp.float32)[:, None] * frequency[None, :])
    return jnp.concatenate(pieces, axis=1)


def rotate(value, cosine, sine_table):
    half_dim = value.shape[-1] // 2
    front_half = value[..., :half_dim]
    back_half = value[..., half_dim:]
    return jnp.concatenate(
        [
            front_half * cosine - back_half * sine_table,
            back_half * cosine + front_half * sine_table,
        ],
        axis=-1,
    )


def soft_weights(scores):
    shifted = jnp.exp(scores - jnp.max(scores, axis=-1, keepdims=True))
    return shifted / jnp.sum(shifted, axis=-1, keepdims=True)


def local(
    tokens,
    caption,
    condition,
    caption_len,
    frame_shape,
    rope_shift,
    w_modulation,
    mod_bias,
    w_attention,
    w_output,
    w_caption,
    norm_gains,
    head_gate,
    w_gateup,
    w_down,
    cotangent,
):
    clip_count, local_len, model_width = tokens.shape
    head_count = head_gate.shape[0]
    head_dim = model_width // head_count
    score_scale = head_dim ** (-0.5)
    row_total = clip_count * local_len
    text_local = caption.shape[1]
    text_total = text_local * lax.axis_size("seq")
    gathered = (
        lax.all_gather(w_modulation, ("clip", "seq"), axis=0, tiled=True),
        lax.all_gather(mod_bias, ("clip", "seq"), axis=0, tiled=True),
        lax.all_gather(w_attention, ("clip", "seq"), axis=0, tiled=True),
        lax.all_gather(w_output, ("clip", "seq"), axis=0, tiled=True),
        lax.all_gather(w_caption, ("clip", "seq"), axis=0, tiled=True),
        lax.all_gather(norm_gains, ("clip", "seq"), axis=1, tiled=True),
    )
    full_mod, full_bias, full_attn, full_out, full_caption, full_gains = gathered
    gain_rows = full_gains.astype(jnp.float32)
    tanh_gate = jnp.tanh(head_gate.astype(jnp.float32))
    cond_float = condition.astype(jnp.float32)
    cond_act = jax.nn.silu(cond_float).astype(jnp.bfloat16)
    modulation = jnp.dot(cond_act, full_mod, preferred_element_type=jnp.float32) + full_bias.astype(
        jnp.float32
    )
    scale_attn = modulation[:, None, :model_width]
    gate_attn = jnp.tanh(modulation[:, None, model_width : 2 * model_width])
    scale_ffn = modulation[:, None, 2 * model_width : 3 * model_width]
    gate_ffn = jnp.tanh(modulation[:, None, 3 * model_width :])
    token_float = tokens.astype(jnp.float32)
    token_normed = rms_norm(token_float)
    normed_flat = (
        (token_normed * gain_rows[0] * (1.0 + scale_attn))
        .astype(jnp.bfloat16)
        .reshape(row_total, model_width)
    )
    projected = jnp.dot(normed_flat, full_attn, preferred_element_type=jnp.float32).reshape(
        clip_count, local_len, 3 * model_width
    )
    query_pre = projected[..., :model_width]
    key_pre = projected[..., model_width : 2 * model_width]
    query_normed = rms_norm(query_pre)
    key_normed = rms_norm(key_pre)
    position = lax.axis_index("seq") * local_len + jnp.arange(local_len, dtype=jnp.int32)
    angles = jax.vmap(
        lambda shape_row, shift_row: rope_angles(shape_row, shift_row, position, head_dim // 2)
    )(frame_shape, rope_shift)
    cosine = jnp.cos(angles)[:, :, None, :]
    sine_table = jnp.sin(angles)[:, :, None, :]
    split_shape = (clip_count, local_len, head_count, head_dim)
    queries = rotate((query_normed * gain_rows[4]).reshape(split_shape), cosine, sine_table).astype(
        jnp.bfloat16
    )
    key_rows = rotate((key_normed * gain_rows[5]).reshape(split_shape), cosine, sine_table).astype(
        jnp.bfloat16
    )
    value_rows = projected[..., 2 * model_width :].reshape(split_shape).astype(jnp.bfloat16)
    caption_flat = caption.reshape(clip_count * text_local, caption.shape[2])
    text_proj = jnp.dot(caption_flat, full_caption, preferred_element_type=jnp.float32).reshape(
        clip_count, text_local, 2 * model_width
    )
    text_key_pre = text_proj[..., :model_width]
    text_key_normed = rms_norm(text_key_pre)
    text_shape = (clip_count, text_local, head_count, head_dim)
    text_keys = (text_key_normed * gain_rows[6]).astype(jnp.bfloat16).reshape(text_shape)
    text_values = text_proj[..., model_width:].astype(jnp.bfloat16).reshape(text_shape)
    all_text_keys, all_text_values = (
        lax.all_gather(text_keys, "seq", axis=1, tiled=True),
        lax.all_gather(text_values, "seq", axis=1, tiled=True),
    )
    stat_shape = (clip_count, head_count, local_len)
    start_stats = (jnp.full(stat_shape, -1e30, jnp.float32), jnp.zeros(stat_shape, jnp.float32))
    piece_keys = lax.all_gather(key_rows, "seq", axis=1, tiled=True)
    key_count = piece_keys.shape[1]
    block_len = math.gcd(key_count, 512)

    def stat_one_block(block_index, inner_state):
        row_max, row_sum = inner_state
        block_keys = lax.dynamic_slice_in_dim(piece_keys, block_index * block_len, block_len, 1)
        scores = (
            jnp.einsum("cqhd,ckhd->chqk", queries, block_keys, preferred_element_type=jnp.float32)
            * score_scale
        )
        new_max = jnp.maximum(row_max, jnp.max(scores, axis=-1))
        row_sum = row_sum * jnp.exp(row_max - new_max) + jnp.sum(
            jnp.exp(scores - new_max[..., None]), axis=-1
        )
        return (new_max, row_sum)

    row_max, row_sum = lax.fori_loop(0, key_count // block_len, stat_one_block, start_stats)
    log_sum = row_max + jnp.log(row_sum)
    attend_piece_keys = lax.all_gather(key_rows, "seq", axis=1, tiled=True)
    piece_values = lax.all_gather(value_rows, "seq", axis=1, tiled=True)
    key_count = attend_piece_keys.shape[1]
    attend_block_len = math.gcd(key_count, 512)

    def attend_one_block(block_index, weighted):
        block_keys = lax.dynamic_slice_in_dim(
            attend_piece_keys, block_index * attend_block_len, attend_block_len, 1
        )
        block_values = lax.dynamic_slice_in_dim(
            piece_values, block_index * attend_block_len, attend_block_len, 1
        )
        scores = (
            jnp.einsum("cqhd,ckhd->chqk", queries, block_keys, preferred_element_type=jnp.float32)
            * score_scale
        )
        probs = jnp.exp(scores - log_sum[..., None]).astype(jnp.bfloat16)
        return weighted + jnp.einsum(
            "chqk,ckhd->chqd", probs, block_values, preferred_element_type=jnp.float32
        )

    weighted = lax.fori_loop(
        0,
        key_count // attend_block_len,
        attend_one_block,
        jnp.zeros(stat_shape + (head_dim,), jnp.float32),
    )
    self_out = jnp.transpose(weighted, (0, 2, 1, 3))
    usable = jnp.arange(text_total, dtype=jnp.int32)[None, :] < caption_len[:, None]
    text_scores = (
        jnp.einsum("cqhd,ckhd->chqk", queries, all_text_keys, preferred_element_type=jnp.float32)
        * score_scale
    )
    text_scores = jnp.where(usable[:, None, None, :], text_scores, -1e30)
    text_weights = soft_weights(text_scores)
    text_low = text_weights.astype(jnp.bfloat16)
    cross_out = jnp.einsum(
        "chqk,ckhd->cqhd", text_low, all_text_values, preferred_element_type=jnp.float32
    )
    mixed_heads = self_out + tanh_gate[None, None, :, None] * cross_out
    mixed_flat = mixed_heads.reshape(row_total, model_width).astype(jnp.bfloat16)
    attn_proj = jnp.dot(mixed_flat, full_out, preferred_element_type=jnp.float32).reshape(
        clip_count, local_len, model_width
    )
    attn_normed = rms_norm(attn_proj)
    residual = token_float + gate_attn * attn_normed * gain_rows[1]
    full_gateup, full_down = (
        lax.all_gather(w_gateup, ("clip", "seq"), axis=0, tiled=True),
        lax.all_gather(w_down, ("clip", "seq"), axis=0, tiled=True),
    )
    hidden_units = full_down.shape[0]
    residual_normed = rms_norm(residual)
    normed_ffn = (
        (residual_normed * gain_rows[2] * (1.0 + scale_ffn))
        .astype(jnp.bfloat16)
        .reshape(row_total, model_width)
    )
    gate_up = jnp.dot(normed_ffn, full_gateup, preferred_element_type=jnp.float32)
    gate_part = gate_up[:, :hidden_units]
    up_part = gate_up[:, hidden_units:]
    gate_sigmoid = jax.nn.sigmoid(gate_part)
    activated = (gate_part * gate_sigmoid * up_part).astype(jnp.bfloat16)
    down_proj = jnp.dot(activated, full_down, preferred_element_type=jnp.float32).reshape(
        clip_count, local_len, model_width
    )
    down_normed = rms_norm(down_proj)
    block_out = residual + gate_ffn * down_normed * gain_rows[3]
    upstream = cotangent.astype(jnp.float32)
    gain_three = jnp.sum(upstream * gate_ffn * down_normed, axis=(0, 1))
    grad_gate_ffn = jnp.sum(upstream * down_normed * gain_rows[3], axis=1) * (
        1.0 - gate_ffn[:, 0] * gate_ffn[:, 0]
    )
    grad_down = (
        rms_back(down_proj, upstream * gate_ffn * gain_rows[3])
        .astype(jnp.bfloat16)
        .reshape(row_total, model_width)
    )
    full_gateup, full_down = (
        lax.all_gather(w_gateup, ("clip", "seq"), axis=0, tiled=True),
        lax.all_gather(w_down, ("clip", "seq"), axis=0, tiled=True),
    )
    wgrad_down = jnp.dot(activated.T, grad_down, preferred_element_type=jnp.float32)
    grad_act = jnp.dot(grad_down, full_down.T, preferred_element_type=jnp.float32)
    grad_gate_part = grad_act * up_part * gate_sigmoid * (1.0 + gate_part * (1.0 - gate_sigmoid))
    grad_up_part = grad_act * gate_part * gate_sigmoid
    grad_gate_up = jnp.concatenate([grad_gate_part, grad_up_part], axis=1).astype(jnp.bfloat16)
    wgrad_gateup = jnp.dot(normed_ffn.T, grad_gate_up, preferred_element_type=jnp.float32)
    grad_normed_ffn = jnp.dot(
        grad_gate_up, full_gateup.T, preferred_element_type=jnp.float32
    ).reshape(clip_count, local_len, model_width)
    gain_two = jnp.sum(grad_normed_ffn * residual_normed * (1.0 + scale_ffn), axis=(0, 1))
    grad_scale_ffn = jnp.sum(grad_normed_ffn * residual_normed * gain_rows[2], axis=1)
    grad_residual = upstream + rms_back(
        residual, grad_normed_ffn * gain_rows[2] * (1.0 + scale_ffn)
    )
    gain_one = jnp.sum(grad_residual * gate_attn * attn_normed, axis=(0, 1))
    grad_gate_attn = jnp.sum(grad_residual * attn_normed * gain_rows[1], axis=1) * (
        1.0 - gate_attn[:, 0] * gate_attn[:, 0]
    )
    grad_attn = (
        rms_back(attn_proj, grad_residual * gate_attn * gain_rows[1])
        .astype(jnp.bfloat16)
        .reshape(row_total, model_width)
    )
    full_mod, full_attn, full_out, full_caption = (
        lax.all_gather(w_modulation, ("clip", "seq"), axis=0, tiled=True),
        lax.all_gather(w_attention, ("clip", "seq"), axis=0, tiled=True),
        lax.all_gather(w_output, ("clip", "seq"), axis=0, tiled=True),
        lax.all_gather(w_caption, ("clip", "seq"), axis=0, tiled=True),
    )
    wgrad_output = jnp.dot(mixed_flat.T, grad_attn, preferred_element_type=jnp.float32)
    grad_mixed = (
        jnp.dot(grad_attn, full_out.T, preferred_element_type=jnp.float32)
        .reshape(split_shape)
        .astype(jnp.bfloat16)
    )
    grad_float = grad_mixed.astype(jnp.float32)
    grad_head_gate = jnp.sum(grad_float * cross_out, axis=(0, 1, 3)) * (1.0 - tanh_gate * tanh_gate)
    delta_rows = jnp.sum(grad_float * self_out, axis=-1)
    delta_heads = jnp.transpose(delta_rows, (0, 2, 1))
    lse_rows = jnp.transpose(log_sum, (0, 2, 1))
    text_grad = (
        jnp.einsum(
            "cqhd,ckhd->chqk", grad_mixed, all_text_values, preferred_element_type=jnp.float32
        )
        * tanh_gate[None, :, None, None]
    )
    text_center = jnp.sum(text_weights * text_grad, axis=-1, keepdims=True)
    grad_text_scores = (text_weights * (text_grad - text_center)).astype(jnp.bfloat16)
    grad_queries = (
        jnp.einsum(
            "chqk,ckhd->cqhd", grad_text_scores, all_text_keys, preferred_element_type=jnp.float32
        )
        * score_scale
    )
    grad_text_keys = (
        jnp.einsum("chqk,cqhd->ckhd", grad_text_scores, queries, preferred_element_type=jnp.float32)
        * score_scale
    )
    grad_text_values = (
        jnp.einsum("chqk,cqhd->ckhd", text_low, grad_mixed, preferred_element_type=jnp.float32)
        * tanh_gate[None, None, :, None]
    )
    text_back_keys, text_back_values = (
        lax.psum_scatter(
            grad_text_keys.astype(jnp.bfloat16), "seq", scatter_dimension=1, tiled=True
        ).astype(jnp.float32),
        lax.psum_scatter(
            grad_text_values.astype(jnp.bfloat16), "seq", scatter_dimension=1, tiled=True
        ).astype(jnp.float32),
    )
    query_piece_keys = lax.all_gather(key_rows, "seq", axis=1, tiled=True)
    query_piece_values = lax.all_gather(value_rows, "seq", axis=1, tiled=True)
    key_count = query_piece_keys.shape[1]
    query_block_len = math.gcd(key_count, 512)

    def query_one_block(block_index, inner_state):
        block_keys = lax.dynamic_slice_in_dim(
            query_piece_keys, block_index * query_block_len, query_block_len, 1
        )
        block_values = lax.dynamic_slice_in_dim(
            query_piece_values, block_index * query_block_len, query_block_len, 1
        )
        scores = (
            jnp.einsum("cqhd,ckhd->chqk", queries, block_keys, preferred_element_type=jnp.float32)
            * score_scale
        )
        probs = jnp.exp(scores - log_sum[..., None])
        grad_probs = jnp.einsum(
            "cqhd,ckhd->chqk", grad_mixed, block_values, preferred_element_type=jnp.float32
        )
        grad_scores = (probs * (grad_probs - delta_heads[..., None])).astype(jnp.bfloat16)
        return (
            inner_state
            + jnp.einsum(
                "chqk,ckhd->cqhd", grad_scores, block_keys, preferred_element_type=jnp.float32
            )
            * score_scale
        )

    grad_self_queries = lax.fori_loop(
        0, key_count // query_block_len, query_one_block, jnp.zeros(split_shape, jnp.float32)
    )
    grad_queries = grad_queries + grad_self_queries
    zero_grads = (jnp.zeros(split_shape, jnp.float32), jnp.zeros(split_shape, jnp.float32))
    piece_queries = lax.all_gather(queries.astype(jnp.float32), "seq", axis=1, tiled=True).astype(
        jnp.bfloat16
    )
    piece_grads = lax.all_gather(grad_float, "seq", axis=1, tiled=True).astype(jnp.bfloat16)
    piece_lse = lax.all_gather(lse_rows, "seq", axis=1, tiled=True)
    piece_delta = lax.all_gather(delta_rows, "seq", axis=1, tiled=True)
    query_count = piece_queries.shape[1]
    key_block_len = math.gcd(query_count, 512)

    def key_one_block(block_index, inner_state):
        grad_key_acc, grad_value_acc = inner_state
        block_queries = lax.dynamic_slice_in_dim(
            piece_queries, block_index * key_block_len, key_block_len, 1
        )
        block_grads = lax.dynamic_slice_in_dim(
            piece_grads, block_index * key_block_len, key_block_len, 1
        )
        block_lse = jnp.transpose(
            lax.dynamic_slice_in_dim(piece_lse, block_index * key_block_len, key_block_len, 1),
            (0, 2, 1),
        )
        block_delta = jnp.transpose(
            lax.dynamic_slice_in_dim(piece_delta, block_index * key_block_len, key_block_len, 1),
            (0, 2, 1),
        )
        scores = (
            jnp.einsum(
                "cqhd,ckhd->chqk", block_queries, key_rows, preferred_element_type=jnp.float32
            )
            * score_scale
        )
        probs = jnp.exp(scores - block_lse[..., None])
        grad_value_acc = grad_value_acc + jnp.einsum(
            "chqk,cqhd->ckhd",
            probs.astype(jnp.bfloat16),
            block_grads,
            preferred_element_type=jnp.float32,
        )
        grad_probs = jnp.einsum(
            "cqhd,ckhd->chqk", block_grads, value_rows, preferred_element_type=jnp.float32
        )
        grad_scores = (probs * (grad_probs - block_delta[..., None])).astype(jnp.bfloat16)
        grad_key_acc = (
            grad_key_acc
            + jnp.einsum(
                "chqk,cqhd->ckhd", grad_scores, block_queries, preferred_element_type=jnp.float32
            )
            * score_scale
        )
        return (grad_key_acc, grad_value_acc)

    grad_keys, grad_values = lax.fori_loop(
        0, query_count // key_block_len, key_one_block, zero_grads
    )
    flat_shape = (clip_count, local_len, model_width)
    grad_query_rot = rotate(grad_queries, cosine, -sine_table).reshape(flat_shape)
    grad_key_rot = rotate(grad_keys, cosine, -sine_table).reshape(flat_shape)
    gain_four = jnp.sum(grad_query_rot * query_normed, axis=(0, 1))
    gain_five = jnp.sum(grad_key_rot * key_normed, axis=(0, 1))
    grad_query_pre = rms_back(query_pre, grad_query_rot * gain_rows[4])
    grad_key_pre = rms_back(key_pre, grad_key_rot * gain_rows[5])
    grad_projected = (
        jnp.concatenate([grad_query_pre, grad_key_pre, grad_values.reshape(flat_shape)], axis=-1)
        .astype(jnp.bfloat16)
        .reshape(row_total, 3 * model_width)
    )
    wgrad_attention = jnp.dot(normed_flat.T, grad_projected, preferred_element_type=jnp.float32)
    grad_normed = jnp.dot(grad_projected, full_attn.T, preferred_element_type=jnp.float32).reshape(
        flat_shape
    )
    gain_zero = jnp.sum(grad_normed * token_normed * (1.0 + scale_attn), axis=(0, 1))
    grad_scale_attn = jnp.sum(grad_normed * token_normed * gain_rows[0], axis=1)
    grad_tokens = grad_residual + rms_back(
        token_float, grad_normed * gain_rows[0] * (1.0 + scale_attn)
    )
    grad_text_key_rows = text_back_keys.reshape(clip_count, text_local, model_width)
    gain_six = jnp.sum(grad_text_key_rows * text_key_normed, axis=(0, 1))
    grad_text_pre = rms_back(text_key_pre, grad_text_key_rows * gain_rows[6])
    grad_text_proj = (
        jnp.concatenate(
            [grad_text_pre, text_back_values.reshape(clip_count, text_local, model_width)], axis=-1
        )
        .astype(jnp.bfloat16)
        .reshape(clip_count * text_local, 2 * model_width)
    )
    wgrad_caption = jnp.dot(caption_flat.T, grad_text_proj, preferred_element_type=jnp.float32)
    grad_caption = jnp.dot(
        grad_text_proj, full_caption.T, preferred_element_type=jnp.float32
    ).reshape(clip_count, text_local, caption.shape[2])
    grad_mod_row = jnp.concatenate(
        [grad_scale_attn, grad_gate_attn, grad_scale_ffn, grad_gate_ffn], axis=1
    )
    bias_grad = jnp.sum(grad_mod_row, axis=0)
    wgrad_modulation = jnp.dot(cond_act.astype(jnp.float32).T, grad_mod_row, precision=highest)
    cond_sigmoid = jax.nn.sigmoid(cond_float)
    grad_cond_act = jnp.dot(grad_mod_row, full_mod.astype(jnp.float32).T, precision=highest)
    grad_cond_part = grad_cond_act * cond_sigmoid * (1.0 + cond_float * (1.0 - cond_sigmoid))
    gain_grads = jnp.stack(
        [gain_zero, gain_one, gain_two, gain_three, gain_four, gain_five, gain_six]
    )
    partial_owned = (
        lax.psum_scatter(
            wgrad_modulation.astype(jnp.bfloat16), "clip", scatter_dimension=0, tiled=True
        ).astype(jnp.float32),
        lax.psum_scatter(
            bias_grad.astype(jnp.bfloat16), "clip", scatter_dimension=0, tiled=True
        ).astype(jnp.float32),
        lax.psum_scatter(
            wgrad_attention.astype(jnp.bfloat16), "clip", scatter_dimension=0, tiled=True
        ).astype(jnp.float32),
        lax.psum_scatter(
            wgrad_output.astype(jnp.bfloat16), "clip", scatter_dimension=0, tiled=True
        ).astype(jnp.float32),
        lax.psum_scatter(
            wgrad_caption.astype(jnp.bfloat16), "clip", scatter_dimension=0, tiled=True
        ).astype(jnp.float32),
        lax.psum_scatter(
            gain_grads.astype(jnp.bfloat16), "clip", scatter_dimension=1, tiled=True
        ).astype(jnp.float32),
        lax.psum_scatter(
            wgrad_gateup.astype(jnp.bfloat16), "clip", scatter_dimension=0, tiled=True
        ).astype(jnp.float32),
        lax.psum_scatter(
            wgrad_down.astype(jnp.bfloat16), "clip", scatter_dimension=0, tiled=True
        ).astype(jnp.float32),
    )
    owned = (
        lax.psum_scatter(
            partial_owned[0].astype(jnp.bfloat16), "seq", scatter_dimension=0, tiled=True
        ).astype(jnp.float32),
        lax.psum_scatter(
            partial_owned[1].astype(jnp.bfloat16), "seq", scatter_dimension=0, tiled=True
        ).astype(jnp.float32),
        lax.psum_scatter(
            partial_owned[2].astype(jnp.bfloat16), "seq", scatter_dimension=0, tiled=True
        ).astype(jnp.float32),
        lax.psum_scatter(
            partial_owned[3].astype(jnp.bfloat16), "seq", scatter_dimension=0, tiled=True
        ).astype(jnp.float32),
        lax.psum_scatter(
            partial_owned[4].astype(jnp.bfloat16), "seq", scatter_dimension=0, tiled=True
        ).astype(jnp.float32),
        lax.psum_scatter(
            partial_owned[5].astype(jnp.bfloat16), "seq", scatter_dimension=1, tiled=True
        ).astype(jnp.float32),
        lax.psum_scatter(
            partial_owned[6].astype(jnp.bfloat16), "seq", scatter_dimension=0, tiled=True
        ).astype(jnp.float32),
        lax.psum_scatter(
            partial_owned[7].astype(jnp.bfloat16), "seq", scatter_dimension=0, tiled=True
        ).astype(jnp.float32),
    )
    grad_gate_total = lax.psum(grad_head_gate, ("clip", "seq"))
    grad_condition = lax.psum(grad_cond_part, "seq")
    return (
        block_out,
        grad_tokens,
        grad_caption,
        grad_condition,
        owned[0],
        owned[1],
        owned[2],
        owned[3],
        owned[4],
        owned[5],
        grad_gate_total,
        owned[6],
        owned[7],
    )


def flip(value, axis):
    return lax.ppermute(value, axis, [(0, 1), (1, 0)])


def from_ahead(value, axis, step):
    count = lax.axis_size(axis)
    return lax.ppermute(value, axis, [((i + step) % count, i) for i in range(count)])


def swap_z(value, bit):
    return lax.ppermute(value, "z", [(i, i ^ bit) for i in range(4)])


def seq_terms(value):
    value = value + flip(value, "x")
    return [value] + [from_ahead(value, "z", k) for k in (1, 2, 3)]


def share(copies):
    return lax.all_to_all(copies, ("z", "x"), 0, 0, tiled=True)


def eight_sum(parts):
    total = parts[0]
    for s in range(1, 8):
        total = total + parts[s]
    return total


def spread(out):
    for s in range(1, 8):
        out[s] = out[0]


def four_sum(parts):
    return (parts[0] + parts[2]) + (parts[1] + parts[3])


def gather_chips(value):
    from_y = flip(value, "y")
    return [value, flip(value, "x"), from_y, flip(from_y, "x")]


def gather_clip(value):
    from_y = flip(value, "y")
    return [value, flip(value, "core"), from_y, flip(from_y, "core")]


def together(*values):
    return lax.optimization_barrier(values)


def rms_scale(square_mean):
    return lax.rsqrt(square_mean + epsilon)


def whole(shape):
    return pl.BlockSpec(shape, lambda step: (0,) * len(shape), pipeline_mode=pl.Buffered(1))


class Line:
    def __init__(self):
        self.last = ()

    def __call__(self, body, outs, *operands, scalars=0, scratch=(), after=(), far=0):
        held = pl.BlockSpec(memory_space=pltpu.SMEM)
        unread = pl.BlockSpec(memory_space=pl.ANY)
        waits = tuple(after) + self.last
        count, skip = len(operands), len(waits)

        def run(*refs):
            body(*refs[:count], *refs[count + skip :])

        given = pl.pallas_call(
            run,
            out_shape=[jax.ShapeDtypeStruct(shape, kind) for shape, kind in outs],
            grid=(1,),
            in_specs=[held] * scalars
            + [whole(value.shape) for value in operands[scalars : count - far]]
            + [unread] * far
            + [unread] * skip,
            out_specs=[whole(shape) for shape, kind in outs],
            scratch_shapes=list(scratch),
            compiler_params=pltpu.CompilerParams(vmem_limit_bytes=50 * 2**20),
        )(*operands, *waits)
        self.last = (min(given, key=lambda value: value.size),)
        return given


def alone(*args, **kinds):
    return Line()(*args, **kinds)


def dot(a, b):
    return jnp.dot(a, b, preferred_element_type=f32)


def dot_rows(a, b):
    return lax.dot_general(a, b, (((1,), (1,)), ((), ())), preferred_element_type=f32)


def dot_cols(a, b):
    return lax.dot_general(a, b, (((0,), (0,)), ((), ())), preferred_element_type=f32)


def round_up(value):
    return -(-value // 128) * 128


def prep_body(attn, gateup, cap, mod, extra, attn_out, ffn_out, cap_out, mod_out):
    width = attn.shape[1] // 3
    cols = width // 8
    pad = attn_out.shape[2] - 3 * cols
    for s in range(8):
        parts = [attn[:, p * width + s * cols : p * width + (s + 1) * cols] for p in range(3)]
        parts.append(jnp.zeros((attn.shape[0], pad), bf16))
        attn_out[s] = jnp.concatenate(parts, axis=1)
    own = gateup.shape[1] // 64
    for g in range(8):
        for part in range(2):
            for z in range(4):
                source = (part * 32 + (g // 2) * 8 + z * 2 + g % 2) * own
                target = (part * 4 + z) * own
                ffn_out[g, :, target : target + own] = gateup[:, source : source + own]
    own = cap_out.shape[2]
    for o in range(32):
        cap_out[o] = cap[:, o * own : (o + 1) * own]
    span = mod.shape[1]
    mod_out[:, :span] = mod[...]
    mod_out[:, span:] = extra[...]


def owner_of(place, r):
    return (place[0] ^ r) * 8 + place[5]


def modulate_body(place, cond, p0, p1, p2, p3, out):
    span = p0.shape[1] - 384
    chunk = span // 32
    gain = chunk // 4
    total = jnp.zeros((8, span), f32)
    for r, piece in enumerate((p0, p1, p2, p3)):
        row = cond[pl.ds(owner_of(place, r), 1), :]
        row = (row / (1.0 + jnp.exp(-row))).astype(bf16).astype(f32)
        row = jnp.broadcast_to(row, (8, row.shape[1])).astype(bf16)
        total = total + dot(row, piece[:, :span])
    out[...] = jnp.zeros(out.shape, f32)
    for i in range(32):
        out[i : i + 1, :chunk] = total[0:1, i * chunk : (i + 1) * chunk]
    for r, piece in enumerate((p0, p1, p2, p3)):
        extra = piece[0:16, span : span + 256].astype(f32)
        at = pl.ds(owner_of(place, r), 1)
        parts = [extra[0:1, :256]] + [extra[8 + g : 9 + g, :gain] for g in range(7)]
        parts.append(jnp.zeros((1, out.shape[1] - 256 - 7 * gain), f32))
        out[at, :] = out[at, :] + jnp.concatenate(parts, axis=1)


def vector_body(place, a, b, c, d, vector_out, column_out, small, turned):
    chunk = vector_out.shape[1] // 8
    gain = chunk // 4
    small[...] = four_sum([a[...], b[...], c[...], d[...]])
    vector_out[...] = jnp.zeros(vector_out.shape, f32)
    for i in range(32):
        to = (i % 8) * chunk
        vector_out[i // 8 : i // 8 + 1, to : to + chunk] = small[i : i + 1, :chunk]
        for g in range(7):
            vector_out[4 + g : 5 + g, i * gain : (i + 1) * gain] = small[
                i : i + 1, 256 + g * gain : 256 + (g + 1) * gain
            ]
    vector_out[1:2] = jnp.tanh(vector_out[1:2])
    vector_out[3:4] = jnp.tanh(vector_out[3:4])
    turned[...] = jnp.zeros(turned.shape, f32)
    for j in range(4):
        row = small[pl.ds(place[5] * 4 + j, 1), :]
        for p in range(3):
            turned[p : p + 1, j * gain : (j + 1) * gain] = row[
                :, 256 + (4 + p) * gain : 256 + (5 + p) * gain
            ]
    column_out[...] = turned[...].T


def caption_slice(weight, s):
    cols = weight.shape[1] // 16
    return jnp.concatenate(
        [weight[:, (p * 8 + s) * cols : (p * 8 + s + 1) * cols] for p in range(2)], axis=1
    )


def caption_body(place, cap, weight, keep_out, send_out):
    for s in range(8):
        own = caption_slice(weight, s)
        j, k = (s % 2) ^ place[2], (s // 2 - place[1] + 4) % 4
        for r in range(4):
            part = dot(cap[place[0] ^ r], own).astype(bf16)
            if r % 2:
                send_out[r // 2, j, k] = part
            else:
                keep_out[r // 2, j, k] = part


def qkv_body(place, tokens, *refs):
    weights = refs[:4]
    vector, normed_out, proj_out, stats_out = refs[4:]
    total, width = tokens.shape
    step = total // 4
    block = width // 4
    cols = width // 8
    scale, gain = vector[0:1], vector[4:5]
    for b in range(4):
        at = slice(b * step, (b + 1) * step)
        value = tokens[at].astype(f32)
        inverse = rms_scale(jnp.mean(value * value, axis=1, keepdims=True))
        normed_out[at] = (value * inverse * gain * (1.0 + scale)).astype(bf16)
    for b in range(4):
        at = slice(b * step, (b + 1) * step)
        part = jnp.zeros((step, weights[0].shape[1]), f32)
        for r, weight in enumerate(weights):
            from_col = pl.multiple_of((place[0] ^ r) * block, 128)
            part = part + dot(normed_out[at, pl.ds(from_col, block)], weight[...])
        proj_out[:, at] = part.T
    stats_out[...] = jnp.zeros(stats_out.shape, f32)
    query, key = proj_out[:cols], proj_out[cols : 2 * cols]
    stats_out[0:1, :] = jnp.sum(query * query, axis=0, keepdims=True)
    stats_out[1:2, :] = jnp.sum(key * key, axis=0, keepdims=True)


def add_four_body(keep, got, *outs):
    for k, out in enumerate(outs):
        out[...] = (keep[k].astype(f32) + got[k].astype(f32)).astype(bf16)


def text_body(a, b, c, d, text_out, stats_out):
    total = four_sum([v[...].astype(f32) for v in (a, b, c, d)])
    text_out[...] = total.T
    key = text_out[: text_out.shape[0] // 2]
    stats_out[...] = jnp.broadcast_to(jnp.sum(key * key, axis=0, keepdims=True), stats_out.shape)


def turn(value, cosine, sine):
    half = value.shape[0] // 2
    front, back = value[:half], value[half:]
    return jnp.concatenate([front * cosine - back * sine, back * cosine + front * sine], axis=0)


def text_softmax(scores, length):
    place = lax.broadcasted_iota(jnp.int32, scores.shape, 0)
    scores = jnp.where(place < length, scores, -1e30)
    shifted = jnp.exp(scores - jnp.max(scores, axis=0, keepdims=True))
    return shifted / jnp.sum(shifted, axis=0, keepdims=True)


def attend_body(
    heads,
    proj,
    stats_a,
    stats_b,
    stats_c,
    stats_d,
    gains,
    cosine,
    sine,
    query_out,
    key_out,
    value_out,
    self_out,
    sum_out,
    stats_out,
):
    total = proj.shape[1]
    cols = query_out.shape[0]
    dim = cols // heads
    width = cols * 8
    step = total // 2
    score_scale = dim ** (-0.5)
    stats_out[...] = four_sum([stats_a[...], stats_b[...], stats_c[...], stats_d[...]])
    scales = rms_scale(stats_out[0:2, :] / width)
    value_out[...] = proj[2 * cols : 3 * cols].astype(bf16)
    sum_out[...] = jnp.zeros(sum_out.shape, f32)
    for h in range(heads):
        at = slice(h * dim, (h + 1) * dim)
        query = proj[at] * scales[0:1] * gains[at, 0:1]
        query_out[at] = turn(query, cosine[...], sine[...]).astype(bf16)
        key = proj[cols + h * dim : cols + (h + 1) * dim] * scales[1:2] * gains[at, 1:2]
        key_out[at] = turn(key, cosine[...], sine[...]).astype(bf16)
        key_rows = key_out[at].T
        for b in range(2):
            to = slice(b * step, (b + 1) * step)
            scores = dot(key_rows, query_out[at, to]) * score_scale
            most = jnp.max(scores, axis=0, keepdims=True)
            weights = jnp.exp(scores - most)
            whole = jnp.sum(weights, axis=0, keepdims=True)
            sum_out[h : h + 1, to] = most + jnp.log(whole)
            self_out[at, to] = dot(value_out[at], weights.astype(bf16)) * (1.0 / whole)


def cross_body(
    heads,
    gate,
    length,
    query,
    self_out,
    text,
    stats_a,
    stats_b,
    stats_c,
    stats_d,
    squares,
    gains,
    mixed_out,
    cross_out,
    text_key_out,
    text_value_out,
    stats_out,
):
    cols, total = query.shape
    dim = cols // heads
    width = cols * 8
    step = total // 2
    piece = mixed_out.shape[2]
    score_scale = dim ** (-0.5)
    text_stats = four_sum([stats_a[...], stats_b[...], stats_c[...], stats_d[...]])
    stats_out[...] = squares[...]
    stats_out[2:3, : text.shape[1]] = text_stats[0:1]
    text_scale = rms_scale(text_stats[0:1] / width)
    text_key_out[...] = (text[:cols] * text_scale * gains[:cols, 2:3]).astype(bf16)
    text_value_out[...] = text[cols : 2 * cols].astype(bf16)
    for h in range(heads):
        at = slice(h * dim, (h + 1) * dim)
        text_rows = text_key_out[at].T
        for b in range(2):
            to = slice(b * step, (b + 1) * step)
            text_weights = text_softmax(dot(text_rows, query[at, to]) * score_scale, length[0])
            cross = dot(text_value_out[at], text_weights.astype(bf16))
            cross_out[at, to] = cross
            mixed = (self_out[at, to] + gate[h] * cross).astype(bf16)
            for s in range(step // piece):
                mixed_out[b * (step // piece) + s, at] = mixed[:, s * piece : (s + 1) * piece]


def stack_body(*refs):
    rows = refs[0].shape[0]
    for i, piece in enumerate(refs[:-1]):
        refs[-1][i * rows : (i + 1) * rows] = piece[...]


def all_ahead(value):
    return [value] + [from_ahead(value, "z", k) for k in (1, 2, 3)]


def output_weight_body(place, *refs):
    own = refs[0].shape[0] // 8
    for r in range(4):
        for j in range(2):
            for k in range(4):
                owner = ((place[0] ^ r) * 4 + (place[1] ^ k)) * 2 + (place[2] ^ j)
                at = (j * 4 + k) * own
                refs[4][pl.ds(pl.multiple_of(owner * own, 16), own), :] = refs[r][at : at + own, :]


def output_body(
    mixed, weight, token, vector, proj_out, residual_out, normed_out, plane_out
):
    proj = dot_cols(mixed[...], weight[...])
    proj_out[...] = proj
    normed = proj * rms_scale(jnp.mean(proj * proj, axis=1, keepdims=True))
    residual = token[...].astype(f32) + vector[1:2] * normed * vector[5:6]
    residual_out[...] = residual
    normed = residual * rms_scale(jnp.mean(residual * residual, axis=1, keepdims=True))
    normed_out[...] = (normed * vector[6:7] * (1.0 + vector[2:3])).astype(bf16)
    own = plane_out.shape[1] // 4
    for g in range(8):
        for z in range(4):
            source = (((g // 2) * 4 + z) * 2 + g % 2) * own
            plane_out[g, z * own : (z + 1) * own] = mixed[source : source + own, :]


def spread_out(parts, own_out, mid_out, x_out, y_out):
    half = own_out.shape[0] // 2
    own, for_x, for_y, far = parts
    own_out[...] = own
    mid_out[:half] = for_y[:half]
    mid_out[half:] = for_x[half:]
    x_out[:half] = for_x[:half].astype(bf16)
    x_out[half:] = far[:half].astype(bf16)
    y_out[:half] = for_y[half:].astype(bf16)
    y_out[half:] = far[half:].astype(bf16)


def feed_body(*refs):
    pieces, gateups, downs = refs[:4], refs[4:6], refs[6:8]
    normed_out, gate_up_out, active_out = refs[8:11]
    rows = pieces[0].shape[0]
    hidden = downs[0].shape[0]
    step = rows * 2
    for r in range(4):
        normed_out[r * rows : (r + 1) * rows] = pieces[r][...]
    parts = []
    for b in range(2):
        at = slice(b * step, (b + 1) * step)
        total = None
        for core in range(2):
            both = dot(normed_out[at], gateups[core][...])
            gate_up_out[core, at] = both
            gate, up = both[:, :hidden], both[:, hidden:]
            active = (gate * jax.nn.sigmoid(gate) * up).astype(bf16)
            active_out[core, at] = active
            part = dot(active, downs[core][...])
            total = part if total is None else total + part
        parts += [total[:rows], total[rows:]]
    spread_out(parts, *refs[11:])


def scatter_two_body(own, mid, by_x, by_y, own_out, y_out, x_out):
    half = own.shape[0] // 2
    own_out[:half] = own[:half] + by_x[:half].astype(f32)
    own_out[half:] = own[half:] + by_y[:half].astype(f32)
    y_out[...] = (mid[:half] + by_x[half:].astype(f32)).astype(bf16)
    x_out[...] = (mid[half:] + by_y[half:].astype(f32)).astype(bf16)


def scatter_chips(line, own, mid, to_x, to_y, between=None):
    rows, width = own.shape
    by_x, by_y = flip(to_x, "x"), flip(to_y, "y")
    if between is not None:
        between()
    own, to_y, to_x = line(
        scatter_two_body,
        [((rows, width), f32), ((rows // 2, width), bf16), ((rows // 2, width), bf16)],
        own,
        mid,
        by_x,
        by_y,
    )
    return own, flip(to_y, "y"), flip(to_x, "x")


def whole_sum(own, by_y, by_x):
    half = own.shape[0] // 2
    return jnp.concatenate(
        [own[:half] + by_y[...].astype(f32), own[half:] + by_x[...].astype(f32)], axis=0
    )


def rms_pull(normed, inverse, grad):
    return (grad - normed * jnp.mean(grad * normed, axis=1, keepdims=True)) * inverse


def middle_body(own, by_y, by_x, residual, cot, vector, block_out, grad_out, sum_out):
    down = whole_sum(own, by_y, by_x)
    inverse = rms_scale(jnp.mean(down * down, axis=1, keepdims=True))
    normed = down * inverse
    gate, gain = vector[3:4], vector[7:8]
    block_out[...] = residual[...] + gate * normed * gain
    upstream = cot[...].astype(f32)
    sum_out[...] = jnp.broadcast_to(
        jnp.sum(upstream * normed, axis=0, keepdims=True), sum_out.shape
    )
    grad_out[...] = rms_pull(normed, inverse, upstream * gate * gain).astype(bf16)


def feed_back_body(*refs):
    pieces, gateups, downs, gate_up = refs[:4], refs[4:6], refs[6:8], refs[8]
    grad_out, hidden_out = refs[9:11]
    rows = pieces[0].shape[0]
    hidden = downs[0].shape[0]
    step = rows * 2
    for r in range(4):
        grad_out[r * rows : (r + 1) * rows] = pieces[r][...]
    parts = []
    for b in range(2):
        at = slice(b * step, (b + 1) * step)
        total = None
        for core in range(2):
            active_grad = dot_rows(grad_out[at], downs[core][...])
            gate, up = gate_up[core, at, :hidden], gate_up[core, at, hidden:]
            sigmoid = jax.nn.sigmoid(gate)
            gate_grad = active_grad * up * sigmoid * (1.0 + gate * (1.0 - sigmoid))
            hidden_out[core, at, :hidden] = gate_grad.astype(bf16)
            hidden_out[core, at, hidden:] = (active_grad * gate * sigmoid).astype(bf16)
            part = dot_rows(hidden_out[core, at], gateups[core][...])
            total = part if total is None else total + part
        parts += [total[:rows], total[rows:]]
    spread_out(parts, *refs[11:])


def down_weight_body(active, down_grad, *outs):
    for core in range(2):
        outs[core][...] = dot_cols(active[core], down_grad[...]).astype(bf16)


def gateup_weight_body(normed, hidden_grad, *outs):
    width = normed.shape[1]
    block = width // 4
    own = block // 4
    for core in range(2):
        for c in range(4):
            part = dot_cols(normed[:, c * block : (c + 1) * block], hidden_grad[core]).astype(bf16)
            for z in range(4):
                outs[core][z, c * own : (c + 1) * own] = part[z * own : (z + 1) * own]


def residual_back_body(
    own,
    by_y,
    by_x,
    residual,
    proj,
    cot,
    vector,
    weight,
    residual_grad_out,
    grad_out,
    mixed_out,
    sum_out,
):
    grad = whole_sum(own, by_y, by_x)
    value = residual[...]
    inverse = rms_scale(jnp.mean(value * value, axis=1, keepdims=True))
    normed = value * inverse
    sum_out[...] = jnp.zeros(sum_out.shape, f32)
    sum_out[1:2] = jnp.sum(grad * normed, axis=0, keepdims=True)
    grad = cot[...].astype(f32) + rms_pull(
        normed, inverse, grad * vector[6:7] * (1.0 + vector[2:3])
    )
    residual_grad_out[...] = grad
    value = proj[...]
    inverse = rms_scale(jnp.mean(value * value, axis=1, keepdims=True))
    normed = value * inverse
    sum_out[0:1] = jnp.sum(grad * normed, axis=0, keepdims=True)
    grad = rms_pull(normed, inverse, grad * vector[1:2] * vector[5:6]).astype(bf16)
    grad_out[...] = grad
    mixed_out[...] = dot_rows(weight[...], grad).astype(bf16)


def text_back_body(
    heads,
    gate,
    length,
    pieces,
    query,
    text_key,
    text_value,
    cross,
    text,
    stats,
    gains,
    grad_out,
    query_out,
    key_out,
    value_out,
    stats_out,
    gain_out,
    gate_out,
):
    cols, total = query.shape
    dim = cols // heads
    width = cols * 8
    step = total // 2
    score_scale = dim ** (-0.5)
    piece = pieces.shape[2]
    for s in range(pieces.shape[0]):
        grad_out[:, s * piece : (s + 1) * piece] = pieces[s]
    gate_out[...] = jnp.zeros(gate_out.shape, f32)
    for h in range(heads):
        at = slice(h * dim, (h + 1) * dim)
        text_rows, value_rows = text_key[at].T, text_value[at].T
        grad = grad_out[at].astype(f32)
        gate_sum = jnp.sum(jnp.sum(grad * cross[at], axis=0, keepdims=True), axis=1, keepdims=True)
        gate_out[h : h + 1, :] = jnp.broadcast_to(
            gate_sum * (1.0 - gate[h] * gate[h]), (1, gate_out.shape[1])
        )
        key_grad = jnp.zeros((dim, text_key.shape[1]), f32)
        value_grad = jnp.zeros((dim, text_key.shape[1]), f32)
        for b in range(2):
            to = slice(b * step, (b + 1) * step)
            block, back = query[at, to], grad_out[at, to]
            weights = text_softmax(dot(text_rows, block) * score_scale, length[0])
            upstream = dot(value_rows, back) * gate[h]
            center = jnp.sum(weights * upstream, axis=0, keepdims=True)
            score_grad = (weights * (upstream - center)).astype(bf16)
            query_out[at, to] = dot(text_key[at], score_grad)
            key_grad = key_grad + dot_rows(block, score_grad)
            value_grad = value_grad + dot_rows(back, weights.astype(bf16))
        key_out[at] = key_grad * score_scale
        value_out[at] = value_grad * gate[h]
    text_scale = rms_scale(stats[2:3, : text.shape[1]] / width)
    normed = text[:cols] * text_scale
    gain_out[...] = jnp.zeros(gain_out.shape, f32)
    gain_out[:cols] = jnp.broadcast_to(
        jnp.sum(key_out[...] * normed, axis=1, keepdims=True), (cols, gain_out.shape[1])
    )
    key_out[...] = key_out[...] * gains[:cols, 2:3]
    stats_out[...] = jnp.broadcast_to(
        jnp.sum(key_out[...] * normed, axis=0, keepdims=True), stats_out.shape
    )


def text_proj_back_body(key, value, text, stats, means, w0, w1, w2, w3, *outs):
    cols = key.shape[0]
    width = cols * 8
    text_scale = rms_scale(stats[2:3, : text.shape[1]] / width)
    normed = text[:cols] * text_scale
    mean = eight_sum(means)[2:3, : text.shape[1]] / width
    before = (key[...] - normed * mean) * text_scale
    grad = jnp.concatenate([before, value[...]], axis=0).T.astype(bf16)
    own, wide = w0.shape[0], grad.shape[1]
    rows = grad.shape[0] * wide // width
    for k, piece in enumerate((w0, w1, w2, w3)):
        outs[k][:own] = piece[...]
        for q in range(width // wide):
            outs[k][own : own + rows, q * wide : (q + 1) * wide] = grad[
                q * rows : (q + 1) * rows
            ]


def text_stack_body(a, b, c, d, out):
    wide = out.shape[1]
    total = out.shape[0] // 4
    count = a.shape[1] // wide
    rows = total // count
    for k, piece in enumerate((a, b, c, d)):
        for q in range(count):
            out[k * total + q * rows : k * total + (q + 1) * rows] = piece[
                piece.shape[0] - rows :, q * wide : (q + 1) * wide
            ]


def caption_back_body(place, cap, *refs):
    grads, (weight, cond, weight_out, piece_out, blocks) = refs[:4], refs[4:]
    cols = weight.shape[1] // 16
    rows = cap.shape[1]
    own_rows = rows // 8
    for j in range(2):
        for k in range(4):
            at = slice((j * 4 + k) * rows, (j * 4 + k + 1) * rows)
            part = None
            for r in range(4):
                term = dot_cols(cap[place[0] ^ r], grads[r][at, :])
                part = term if part is None else part + term
            blocks[(place[1] + k) % 4 * 2 + (place[2] ^ j)] = part
    for s in range(8):
        for p in range(2):
            weight_out[:, (p * 8 + s) * cols : (p * 8 + s + 1) * cols] = blocks[
                s, :, p * cols : (p + 1) * cols
            ]
    for s in range(8):
        blocks[s] = caption_slice(weight, s).astype(f32)
    for r in range(4):
        clip = place[0] ^ r
        total = None
        for j in range(2):
            for k in range(4):
                at = slice((j * 4 + k) * rows, (j * 4 + k + 1) * rows)
                own = blocks[(place[1] + k) % 4 * 2 + (place[2] ^ j)].astype(bf16)
                term = dot_rows(grads[r][at, :], own)
                total = term if total is None else total + term
        for s in range(8):
            piece_out[clip * 8 + s, :own_rows] = total[s * own_rows : (s + 1) * own_rows]
            piece_out[clip * 8 + s, own_rows:] = cond[clip]


def attend_back_body(
    heads,
    grad,
    query,
    key,
    value,
    self_out,
    sums,
    text_query,
    text_stats,
    proj,
    stats,
    gains,
    cosine,
    sine,
    query_in_out,
    key_in_out,
    value_grad_out,
    stats_out,
    gain_out,
):
    cols, total = query.shape
    dim = cols // heads
    width = cols * 8
    step = total // 2
    score_scale = dim ** (-0.5)
    scales = rms_scale(stats[0:2, :] / width)
    stats_out[0] = jnp.zeros(stats_out.shape[1:], f32)
    gain_out[...] = jnp.zeros(gain_out.shape, f32)
    query_total = jnp.zeros((1, total), f32)
    key_total = jnp.zeros((1, total), f32)
    for h in range(heads):
        at = slice(h * dim, (h + 1) * dim)
        key_rows, value_rows = key[at].T, value[at].T
        delta = jnp.sum(grad[at].astype(f32) * self_out[at], axis=0, keepdims=True)
        key_grad = jnp.zeros((dim, total), f32)
        value_grad = jnp.zeros((dim, total), f32)
        query_parts = []
        for b in range(2):
            to = slice(b * step, (b + 1) * step)
            block, back = query[at, to], grad[at, to]
            weights = jnp.exp(dot(key_rows, block) * score_scale - sums[h : h + 1, to])
            value_grad = value_grad + dot_rows(back, weights.astype(bf16))
            score_grad = (weights * (dot(value_rows, back) - delta[:, to])).astype(bf16)
            key_grad = key_grad + dot_rows(block, score_grad)
            query_parts.append(dot(key[at], score_grad))
        value_grad_out[at] = value_grad.astype(bf16)
        query_grad = (jnp.concatenate(query_parts, axis=1) + text_query[at]) * score_scale
        query_grad = turn(query_grad, cosine[...], -sine[...])
        key_grad = turn(key_grad * score_scale, cosine[...], -sine[...])
        query_normed = proj[at] * scales[0:1]
        key_normed = proj[cols + h * dim : cols + (h + 1) * dim] * scales[1:2]
        gain_out[at, 0:1] = jnp.sum(query_grad * query_normed, axis=1, keepdims=True)
        gain_out[at, 1:2] = jnp.sum(key_grad * key_normed, axis=1, keepdims=True)
        query_grad = query_grad * gains[at, 0:1]
        key_grad = key_grad * gains[at, 1:2]
        query_in_out[at] = query_grad
        key_in_out[at] = key_grad
        query_total = query_total + jnp.sum(query_grad * query_normed, axis=0, keepdims=True)
        key_total = key_total + jnp.sum(key_grad * key_normed, axis=0, keepdims=True)
    stats_out[0, 0:1, :] = query_total
    stats_out[0, 1:2, :] = key_total
    stats_out[0, 2:3, : text_stats.shape[1]] = text_stats[0:1]
    spread(stats_out)


def project_back_body(place, *refs):
    tokens, weights = refs[0], refs[1:5]
    query_in, key_in, value_grad, proj, stats = refs[5:10]
    mean_parts, normed, vector = refs[10:13]
    middle_sums, residual_sums, own_gains, text_gains, gate_sums = refs[13:18]
    part_out, near_out, far_out, sums_out = refs[18:22]
    low, turned, unit, sum_out = refs[22:]
    cols, total = query_in.shape
    width = normed.shape[1]
    block = width // 4
    rows = total // 8
    scales = rms_scale(stats[0:2, :] / width)
    means = eight_sum(mean_parts) / width
    low[...] = jnp.zeros(low.shape, bf16)
    low[:cols] = (
        (query_in[...] - proj[:cols] * scales[0:1] * means[0:1, :]) * scales[0:1]
    ).astype(bf16)
    low[cols : 2 * cols] = (
        (key_in[...] - proj[cols : 2 * cols] * scales[1:2] * means[1:2, :]) * scales[1:2]
    ).astype(bf16)
    low[2 * cols : 3 * cols] = value_grad[...]
    turned[...] = low[...].T
    sum_out[...] = jnp.zeros(sum_out.shape, f32)
    for b in range(4):
        at = slice(b * 2 * rows, (b + 1) * 2 * rows)
        value = tokens[at].astype(f32)
        unit[...] = value * rms_scale(jnp.mean(value * value, axis=1, keepdims=True))
        for r in range(4):
            to_col = pl.ds(pl.multiple_of((place[0] ^ r) * block, 128), block)
            part = dot_rows(turned[at], weights[r][...])
            sum_out[0:1, to_col] = sum_out[0:1, to_col] + jnp.sum(
                part * unit[:, to_col], axis=0, keepdims=True
            )
            part_out[at, to_col] = part.astype(bf16)
    for r in range(4):
        from_col = pl.ds(pl.multiple_of((place[0] ^ r) * block, 128), block)
        part = dot(low[...], normed[:, from_col]).T.astype(bf16)
        if r % 2:
            far_out[r // 2] = part
        else:
            near_out[r // 2] = part
    sum_out[1:3] = residual_sums[0:2]
    sum_out[3:4] = middle_sums[0:1]
    lane = lax.broadcasted_iota(jnp.int32, (1, width), 1)
    mine = lane // cols == place[5]
    own_rows, text_row = own_gains[...].T, text_gains[...].T
    for at, row in ((4, own_rows[0:1]), (5, own_rows[1:2]), (6, text_row[0:1])):
        wide = jnp.concatenate([row[:, :cols]] * 8, axis=1)
        sum_out[at : at + 1] = jnp.where(mine, wide, 0.0)
    heads = 3
    gates = jnp.zeros((1, width), f32)
    for h in range(heads):
        gates = jnp.where(lane == place[5] * heads + h, gate_sums[h : h + 1, 0:1], gates)
    sum_out[7:8] = gates
    for s in range(8):
        sums_out[s] = sum_out[...]


def add_body(a, b, out):
    out[...] = (a[...].astype(f32) + b[...].astype(f32)).astype(bf16)


def add_pair_body(keep, got, keep_out, send_out):
    keep_out[...] = (keep[0].astype(f32) + got[0].astype(f32)).astype(bf16)
    send_out[...] = (keep[1].astype(f32) + got[1].astype(f32)).astype(bf16)


def final_body(grad_normed, residual_grad, token, vector, out):
    grad = grad_normed[...].astype(f32)
    value = token[...].astype(f32)
    inverse = rms_scale(jnp.mean(value * value, axis=1, keepdims=True))
    out[...] = residual_grad[...] + rms_pull(
        value * inverse, inverse, grad * vector[4:5] * (1.0 + vector[0:1])
    )


def modulation_back_body(parts, vector, shared_out):
    sums = eight_sum(parts)
    width = sums.shape[1]
    scale_attn, gate_attn, scale_ffn, gate_ffn = [vector[i : i + 1] for i in range(4)]
    gains = [vector[4 + i : 5 + i] for i in range(4)]
    zero, one, two, three = [sums[i : i + 1] for i in range(4)]
    rows = [
        gains[0] * zero,
        gains[1] * one * (1.0 - gate_attn * gate_attn),
        gains[2] * two,
        gains[3] * three * (1.0 - gate_ffn * gate_ffn),
    ]
    shared_out[...] = jnp.zeros(shared_out.shape, f32)
    for i in range(4):
        shared_out[i : i + 1] = rows[i]
    shared_out[4:5] = (1.0 + scale_attn) * zero
    shared_out[5:6] = gate_attn * one
    shared_out[6:7] = (1.0 + scale_ffn) * two
    shared_out[7:8] = gate_ffn * three
    shared_out[8:12] = sums[4:8]


def modulation_weight_body(
    place, t0, t1, t2, t3, p0, p1, p2, p3, weight_out, total_out, cond_out, square
):
    width = t0.shape[1]
    rows = weight_out.shape[0]
    span = 4 * width
    owner = owner_of(place, 0)
    total_out[...] = (t0[...] + t1[...]) + (t2[...] + t3[...])
    lane = lax.broadcasted_iota(jnp.int32, (rows, square.shape[0]), 1)
    columns = []
    for piece in (p0, p1, p2, p3):
        cond = piece[:, span + 256 : span + 384].astype(f32)
        cond = (cond / (1.0 + jnp.exp(-cond))).astype(bf16).astype(f32)
        square[...] = jnp.zeros(square.shape, f32)
        square[:rows] = cond
        turned = square[...].T[:rows]
        columns.append(jnp.sum(jnp.where(lane == owner, turned, 0.0), axis=1, keepdims=True))
    for i in range(4):
        part = None
        for column, shared in zip(columns, (t0, t1, t2, t3)):
            term = column * shared[i : i + 1, :]
            part = term if part is None else part + term
        weight_out[:, i * width : (i + 1) * width] = part
    lanes = cond_out.shape[2]
    for r, shared in enumerate((t0, t1, t2, t3)):
        back = jnp.zeros((8, rows), f32)
        for i in range(4):
            back = back + lax.dot_general(
                jnp.broadcast_to(shared[i : i + 1, :], (8, width)),
                p0[:, i * width : (i + 1) * width].astype(f32),
                (((1,), (1,)), ((), ())),
                precision=highest,
                preferred_element_type=f32,
            )
        cond_out[place[0] ^ r] = jnp.concatenate(
            [back, jnp.zeros((8, lanes - rows), f32)], axis=1
        )


def attention_grad_body(pieces, grad_out):
    cols = grad_out.shape[1] // 24
    for s in range(8):
        for p in range(3):
            grad_out[:, (p * 8 + s) * cols : (p * 8 + s + 1) * cols] = pieces[
                s, :, p * cols : (p + 1) * cols
            ].astype(f32)


def gateup_grad_body(pieces, grad_out):
    own = grad_out.shape[1] // 64
    for g in range(8):
        for part in range(2):
            for z in range(4):
                target = (part * 32 + (g // 2) * 8 + z * 2 + g % 2) * own
                source = (part * 4 + z) * own
                grad_out[:, target : target + own] = pieces[g, :, source : source + own].astype(f32)


def caption_grad_body(pieces, grad_out, cond_out):
    own = pieces.shape[2]
    rows = grad_out.shape[0]
    for o in range(32):
        grad_out[:, o * own : (o + 1) * own] = pieces[o, :rows]
        cond_out[o : o + 1] = pieces[o, rows : rows + 1]


def output_grad_body(place, mixed, *refs):
    grads, weight_outs, held, done = refs[:8], refs[8:12], refs[12], refs[13]
    rows = mixed.shape[2]
    copies = [
        pltpu.make_async_copy(grads[r], held.at[pl.ds(r * rows, rows)], done.at[r])
        for r in range(8)
    ]
    for copy in copies:
        copy.start()
    total = None
    for r in range(8):
        copies[r].wait()
        core, y, x = r // 4, (r // 2) % 2, r % 2
        source = ((place[3] ^ y) * 2 + (place[4] ^ core)) * 2 + (place[2] ^ x)
        part = dot(mixed[source], held[r * rows : (r + 1) * rows])
        total = part if total is None else total + part
    own = total.shape[0] // 4
    held[: total.shape[0]] = total.astype(bf16)
    for k in range(4):
        source = pl.multiple_of((place[1] + k) % 4 * own, 16)
        weight_outs[k][...] = held[pl.ds(source, own), :]


def output_sum_body(a, b, c, d, out):
    out[...] = four_sum([v[: out.shape[0]].astype(f32) for v in (a, b, c, d)])


def local_fast(
    tokens,
    caption,
    condition,
    caption_len,
    frame_shape,
    rope_shift,
    w_modulation,
    mod_bias,
    w_attention,
    w_output,
    w_caption,
    norm_gains,
    head_gate,
    w_gateup,
    w_down,
    cotangent,
):
    seq_axes = ("z", "x")
    all_axes = ("y", "core") + seq_axes
    plane_axes = ("y", "core", "x")
    rows, width = tokens.shape[1:]
    total = rows * 8
    heads = head_gate.shape[0]
    head_dim = width // heads
    own_heads = heads // 8
    cols = own_heads * head_dim
    wide_cols = round_up(3 * cols)
    text_rows = caption.shape[1]
    text_total = text_rows * 8
    attn_rows = w_attention.shape[0]
    z_at, x_at = lax.axis_index("z"), lax.axis_index("x")
    y_at, core_at = lax.axis_index("y"), lax.axis_index("core")
    seq_at = z_at * 2 + x_at
    clip_at = y_at * 2 + core_at
    owner = clip_at * 8 + seq_at
    place = jnp.stack([clip_at, z_at, x_at, y_at, core_at, seq_at]).astype(jnp.int32)

    line = Line()
    own_tokens = tokens[0]
    token_all = lax.all_gather(own_tokens, seq_axes, axis=0, tiled=True)

    cap_cols = w_caption.shape[0]
    hidden_own = w_down.shape[0]
    hidden = 4 * hidden_own
    cond_rows, span = w_modulation.shape
    bias_len = mod_bias.shape[0]
    gain_cols = norm_gains.shape[1]
    cond_square = condition.reshape(32, cond_rows)
    extra = jnp.concatenate(
        [
            jnp.pad(mod_bias[None], ((0, 31), (0, 256 - bias_len)))
            + jnp.pad(norm_gains, ((8, 17), (0, 256 - gain_cols))),
            jnp.pad(cond_square, ((0, 0), (0, 128 - cond_rows))),
        ],
        axis=1,
    )
    attn_piece, ffn_piece, cap_piece, mod_piece = alone(
        prep_body,
        [
            ((8, attn_rows, wide_cols), bf16),
            ((8, w_gateup.shape[0], 8 * hidden_own), bf16),
            ((32, text_rows, cap_cols), bf16),
            ((cond_rows, span + 384), bf16),
        ],
        w_attention,
        w_gateup,
        caption[0],
        w_modulation,
        extra,
    )
    mod_y, mod_core = flip(mod_piece, "y"), flip(mod_piece, "core")
    attn_0 = lax.all_to_all(attn_piece, seq_axes, 0, 0, tiled=True).reshape(-1, wide_cols)
    mod_piece, mod_y, mod_core, attn_0, cap_piece, ffn_piece = together(
        mod_piece, mod_y, mod_core, attn_0, cap_piece, ffn_piece
    )

    mod_parts = [mod_piece, mod_core, mod_y, flip(mod_y, "core")]
    attn_2, attn_1 = flip(attn_0, "y"), flip(attn_0, "core")
    cap_all = lax.all_to_all(cap_piece, all_axes, 0, 0, tiled=True)
    (small,) = line(
        modulate_body,
        [((32, 640), f32)],
        place,
        cond_square.astype(f32),
        *mod_parts,
        scalars=1,
    )
    vector, own_gains = line(
        vector_body,
        [((16, width), f32), ((256, 128), f32)],
        place,
        *seq_terms(small),
        scalars=1,
        scratch=[pltpu.VMEM((32, 640), f32), pltpu.VMEM((128, 256), f32)],
    )
    vector, attn_0, attn_1, attn_2, cap_all, ffn_piece, own_out, w_down = together(
        vector, attn_0, attn_1, attn_2, cap_all, ffn_piece, w_output, w_down
    )

    cap_all = cap_all.reshape(4, text_total, cap_cols)
    attn_3 = flip(attn_2, "core")
    four_text = (4, text_total, 2 * cols)
    cap_keep, cap_send = line(
        caption_body,
        [((2, 2) + four_text, bf16)] * 2,
        place,
        cap_all,
        w_caption,
        scalars=1,
    )
    out_near = swap_z(own_out, 1)
    own_down = lax.all_gather(w_down, "z", axis=0, tiled=True)
    ffn_piece = lax.all_to_all(ffn_piece, plane_axes, 0, 0, tiled=True)
    block = 2 * ffn_piece.shape[1]
    cap_keep, cap_send = line(
        add_pair_body, [((2,) + four_text, bf16)] * 2, cap_keep, flip(cap_send, "core")
    )
    attn_3, cap_send, cap_keep = together(attn_3, cap_send, cap_keep)

    attn_parts = (attn_0, attn_1, attn_2, attn_3)
    cap_send = flip(cap_send, "y")
    normed_all, projected, squares = line(
        qkv_body,
        [((total, width), bf16), ((wide_cols, total), f32), ((8, total), f32)],
        place,
        token_all,
        *attn_parts,
        vector,
        scalars=1,
    )
    squares = seq_terms(squares)
    (out_pair,) = line(
        stack_body, [((2 * attn_rows, width), bf16)], own_out, out_near, after=(squares[0],)
    )
    out_far = swap_z(out_pair, 2)
    cap_keep, cap_send = line(add_pair_body, [(four_text, bf16)] * 2, cap_keep, cap_send)
    cap_send = flip(cap_send, "x")
    text_parts = line(
        add_four_body, [(four_text[1:], bf16)] * 4, cap_keep, cap_send, after=tuple(squares[1:])
    )
    out_far, squares, text_parts, ffn_piece, own_down = together(
        out_far, squares, text_parts, ffn_piece, own_down
    )

    text_parts = [text_parts[0]] + [from_ahead(text_parts[4 - k], "z", k) for k in (1, 2, 3)]
    (out_z,) = line(stack_body, [((4 * attn_rows, width), bf16)], out_pair, out_far)
    out_x = flip(out_z, "x")

    head_low = lax.dynamic_slice_in_dim(head_gate, seq_at * own_heads, own_heads)
    tanh_gate = jnp.tanh(head_low.astype(f32))
    position = jnp.arange(total, dtype=jnp.int32)
    angles = rope_angles(frame_shape[0], rope_shift[0], position, head_dim // 2).T
    cosine = jnp.cos(angles)
    sine = jnp.sin(angles)
    flat = (cols, total)
    queries, key_rows, values, self_out, log_sum, squares = line(
        functools.partial(attend_body, own_heads),
        [
            (flat, bf16),
            (flat, bf16),
            (flat, bf16),
            (flat, f32),
            ((8, total), f32),
            ((8, total), f32),
        ],
        projected,
        *squares,
        own_gains,
        cosine,
        sine,
    )
    self_out, out_x, text_parts, ffn_piece = together(self_out, out_x, text_parts, ffn_piece)
    own_gateup = lax.all_gather(ffn_piece.reshape(4, block, -1), "z", axis=0)
    own_gateup = jnp.transpose(own_gateup, (1, 0, 2, 3)).reshape(width, -1)
    (out_0,) = line(stack_body, [((8 * attn_rows, width), bf16)], out_z, out_x)
    out_2 = flip(out_0, "y")

    text_proj, text_squares = line(
        text_body, [((2 * cols, text_total), f32), ((8, text_total), f32)], *text_parts
    )
    text_squares = seq_terms(text_squares)
    mixed_pieces, cross_out, text_keys, text_values, squares = line(
        functools.partial(cross_body, own_heads),
        [
            ((8, cols, rows), bf16),
            (flat, f32),
            ((cols, text_total), bf16),
            ((cols, text_total), bf16),
            ((8, total), f32),
        ],
        tanh_gate,
        caption_len,
        queries,
        self_out,
        text_proj,
        *text_squares,
        squares,
        own_gains,
        scalars=2,
    )
    mixed_pieces, out_2, out_0 = together(mixed_pieces, out_2, out_0)
    mixed_own = lax.all_to_all(mixed_pieces, seq_axes, 0, 0, tiled=True).reshape(width, rows)
    out_1, out_3 = flip(out_0, "core"), flip(out_2, "core")
    (full_out,) = line(
        output_weight_body,
        [((width, width), bf16)],
        place,
        out_0,
        out_1,
        out_2,
        out_3,
        scalars=1,
    )
    mixed_own, full_out = together(mixed_own, full_out)
    own_shape = (rows, width)
    attn_proj, residual, normed_ffn, mixed_plane = line(
        output_body,
        [
            (own_shape, f32),
            (own_shape, f32),
            (own_shape, bf16),
            ((8, 4 * attn_rows, rows), bf16),
        ],
        mixed_own,
        full_out,
        own_tokens,
        vector,
    )

    chip_shape = (4 * rows, width)
    on_way = [(own_shape, f32), (own_shape, f32), (own_shape, bf16), (own_shape, bf16)]
    normed_parts = gather_chips(normed_ffn)
    own_gateup = together(own_gateup, normed_parts[1], normed_parts[2])[0]
    gateups = (own_gateup, flip(own_gateup, "core"))
    own_down = together(own_down, normed_ffn)[0]
    downs = (own_down, flip(own_down, "core"))
    normed_ffn_all, gate_up, activated, *parts = line(
        feed_body,
        [
            (chip_shape, bf16),
            ((2, 4 * rows, 2 * hidden), f32),
            ((2, 4 * rows, hidden), bf16),
        ]
        + on_way,
        *normed_parts,
        *gateups,
        *downs,
    )
    block_out, grad_down, middle_sums = line(
        middle_body,
        [(own_shape, f32), (own_shape, bf16), ((8, width), f32)],
        *scatter_chips(line, *parts),
        residual,
        cotangent[0],
        vector,
    )

    grad_down_all, grad_gate_up, *parts = line(
        feed_back_body,
        [(chip_shape, bf16), ((2, 4 * rows, 2 * hidden), bf16)] + on_way,
        *gather_chips(grad_down),
        *gateups,
        *downs,
        gate_up,
    )
    ffn_grads = []

    def feed_weights():
        down_own, down_other = line(
            down_weight_body, [((hidden, width), bf16)] * 2, activated, grad_down_all
        )
        gateup_own, gateup_other = line(
            gateup_weight_body,
            [((4, 4 * block, 2 * hidden), bf16)] * 2,
            normed_ffn_all,
            grad_gate_up,
        )
        (down_sum,) = line(
            add_body, [((hidden, width), bf16)], down_own, flip(down_other, "core")
        )
        ffn_grads.extend([down_sum, gateup_own, flip(gateup_other, "core")])

    ffn_parts = scatter_chips(line, *parts, feed_weights)
    wgrad_down = lax.psum_scatter(ffn_grads[0], "z", scatter_dimension=0, tiled=True)
    (wgrad_gateup,) = line(
        add_body, [((4, 4 * block, 2 * hidden), bf16)], ffn_grads[1], ffn_grads[2]
    )

    grad_residual, grad_attn, grad_mixed, residual_sums = line(
        residual_back_body,
        [(own_shape, f32), (own_shape, bf16), ((width, rows), bf16), ((8, width), f32)],
        *ffn_parts,
        residual,
        attn_proj,
        cotangent[0],
        vector,
        full_out,
    )
    grad_mixed, wgrad_down, wgrad_gateup = together(grad_mixed, wgrad_down, wgrad_gateup)
    wgrad_gateup = lax.psum_scatter(wgrad_gateup, "z", scatter_dimension=0, tiled=False)
    grad_pieces = lax.all_to_all(grad_mixed.reshape(8, cols, rows), seq_axes, 0, 0, tiled=True)
    grad_by_x, grad_by_y = flip(grad_attn, "x"), flip(grad_attn, "y")
    grad_pieces, grad_by_x, grad_by_y, mixed_plane = together(
        grad_pieces, grad_by_x, grad_by_y, mixed_plane
    )
    mixed_plane = lax.all_to_all(mixed_plane, plane_axes, 0, 0, tiled=True)
    grad_far = flip(grad_by_y, "x")

    (
        grad_mixed,
        text_query,
        text_key_in,
        text_value_grad,
        text_stats,
        text_gain,
        gate_sum,
    ) = line(
        functools.partial(text_back_body, own_heads),
        [
            (flat, bf16),
            (flat, f32),
            ((cols, text_total), f32),
            ((cols, text_total), f32),
            ((8, text_total), f32),
            ((256, 128), f32),
            ((8, 128), f32),
        ],
        tanh_gate,
        caption_len,
        grad_pieces,
        queries,
        text_keys,
        text_values,
        cross_out,
        text_proj,
        squares,
        own_gains,
        scalars=2,
    )
    query_in, key_in, value_grad, means, own_gain_sums = line(
        functools.partial(attend_back_body, own_heads),
        [
            (flat, f32),
            (flat, f32),
            (flat, bf16),
            ((8, 8, total), f32),
            ((256, 128), f32),
        ],
        grad_mixed,
        queries,
        key_rows,
        values,
        self_out,
        log_sum,
        text_query,
        text_stats,
        projected,
        squares,
        own_gains,
        cosine,
        sine,
    )
    means, mixed_plane, grad_attn, grad_by_x, grad_by_y, grad_far = together(
        means, mixed_plane, grad_attn, grad_by_x, grad_by_y, grad_far
    )
    means = share(means)
    grad_attn_parts = [grad_attn, grad_by_x, grad_by_y, grad_far]
    grad_attn_parts = grad_attn_parts + [flip(piece, "core") for piece in grad_attn_parts]
    wgrad_parts = line(
        output_grad_body,
        [((attn_rows, width), bf16)] * 4,
        place,
        mixed_plane,
        *grad_attn_parts,
        scalars=1,
        far=8,
        scratch=[pltpu.VMEM((total, width), bf16), pltpu.SemaphoreType.DMA((8,))],
    )
    pack = (attn_rows + text_total * 2 * cols // width, width)
    packs = line(
        text_proj_back_body,
        [(pack, bf16)] * 4,
        text_key_in,
        text_value_grad,
        text_proj,
        squares,
        means,
        *wgrad_parts,
    )
    means, packs, wgrad_gateup = together(means, packs, wgrad_gateup)

    packs = [packs[0]] + [from_ahead(packs[4 - k], "z", k) for k in (1, 2, 3)]
    wgrad_gateup = lax.all_to_all(
        wgrad_gateup.reshape(8, block // 2, -1), plane_axes, 0, 0, tiled=True
    )
    quarter = width // 4
    grad_normed, near_part, far_part, sums = line(
        project_back_body,
        [((total, width), bf16)]
        + [((2, quarter, wide_cols), bf16)] * 2
        + [((8, 8, width), f32)],
        place,
        token_all,
        *attn_parts,
        query_in,
        key_in,
        value_grad,
        projected,
        squares,
        means,
        normed_all,
        vector,
        middle_sums,
        residual_sums,
        own_gain_sums,
        text_gain,
        gate_sum,
        scalars=1,
        scratch=[
            pltpu.VMEM((wide_cols, total), bf16),
            pltpu.VMEM((total, wide_cols), bf16),
            pltpu.VMEM((2 * rows, width), f32),
            pltpu.VMEM((8, width), f32),
        ],
    )
    grad_normed, far_part, sums, packs, wgrad_gateup = together(
        grad_normed, far_part, sums, packs, wgrad_gateup
    )

    grad_normed = lax.psum_scatter(grad_normed, seq_axes, scatter_dimension=0, tiled=True)
    (text_z,) = line(text_stack_body, [((4 * text_total, 2 * cols), bf16)], *packs)
    text_x = flip(text_z, "x")
    far_part = flip(far_part, "core")
    wide = (quarter, wide_cols)
    near_part, far_part = line(add_pair_body, [(wide, bf16)] * 2, near_part, far_part)
    far_part, text_x, sums = together(far_part, text_x, sums)

    far_part = flip(far_part, "y")
    sums = share(sums)
    (text_seq,) = line(stack_body, [((8 * text_total, 2 * cols), bf16)], text_z, text_x)
    (wgrad_gateup,) = line(gateup_grad_body, [(w_gateup.shape, f32)], wgrad_gateup)
    far_part, text_seq = together(far_part, text_seq)

    text_y, text_core = flip(text_seq, "y"), flip(text_seq, "core")
    (wgrad_attention,) = line(add_body, [(wide, bf16)], near_part, far_part)
    (shared,) = line(modulation_back_body, [((16, width), f32)], sums, vector)
    shared_y, shared_core = flip(shared, "y"), flip(shared, "core")
    wgrad_attention = together(wgrad_attention, sums)[0]
    wgrad_attention = lax.all_to_all(
        wgrad_attention.reshape(8, attn_rows, wide_cols), seq_axes, 0, 0, tiled=True
    )
    shared_y, shared_core, text_core, text_y = together(shared_y, shared_core, text_core, text_y)

    wgrad_modulation, shared, cond_back = line(
        modulation_weight_body,
        [(w_modulation.shape, f32), ((16, width), f32), ((4, 8, cap_cols), f32)],
        place,
        shared,
        shared_core,
        shared_y,
        flip(shared_y, "core"),
        *mod_parts,
        scalars=1,
        scratch=[pltpu.VMEM((128, 128), f32)],
    )
    wgrad_caption, cap_pieces = line(
        caption_back_body,
        [(w_caption.shape, f32), ((32, text_rows + 8, cap_cols), f32)],
        place,
        cap_all,
        text_seq,
        text_core,
        text_y,
        flip(text_y, "core"),
        w_caption,
        cond_back,
        scalars=1,
        scratch=[pltpu.VMEM((8, cap_cols, 2 * cols), f32)],
    )
    cap_pieces, wgrad_attention = together(cap_pieces, wgrad_attention)

    cap_pieces = lax.all_to_all(cap_pieces, all_axes, 0, 0, tiled=True)
    (wgrad_attention,) = line(attention_grad_body, [(w_attention.shape, f32)], wgrad_attention)
    (wgrad_output,) = line(output_sum_body, [((attn_rows, width), f32)], *packs)

    grad_caption, cond_back = line(
        caption_grad_body, [((text_rows, 32 * cap_cols), f32), ((32, cap_cols), f32)], cap_pieces
    )
    (grad_tokens,) = line(
        final_body, [(own_shape, f32)], grad_normed, grad_residual, own_tokens, vector
    )
    bias_grad = lax.dynamic_slice(shared, (clip_at, seq_at * bias_len), (1, bias_len))[0]
    gain_grads = lax.dynamic_slice(shared, (4, owner * gain_cols), (7, gain_cols))
    grad_gate_total = shared[11, :heads]
    cond_back = cond_back[:, :cond_rows].reshape(1, -1)
    cond_float = condition.astype(f32)
    cond_sigmoid = jax.nn.sigmoid(cond_float)
    grad_condition = cond_back * cond_sigmoid * (1.0 + cond_float * (1.0 - cond_sigmoid))

    return (
        block_out[None],
        grad_tokens[None],
        grad_caption[None],
        grad_condition,
        wgrad_modulation,
        bias_grad,
        wgrad_attention,
        wgrad_output,
        wgrad_caption,
        gain_grads,
        grad_gate_total,
        wgrad_gateup,
        wgrad_down.astype(f32),
    )


def specs(clip, seq):
    both = clip + seq
    placed = (
        P(clip, seq, None),
        P(clip, seq, None),
        P(clip, None),
        P(clip),
        P(clip, None),
        P(clip, None),
        P(both, None),
        P(both),
        P(both, None),
        P(both, None),
        P(both, None),
        P(None, both),
        P(),
        P(both, None),
        P(both, None),
        P(clip, seq, None),
    )
    given = (
        P(clip, seq, None),
        P(clip, seq, None),
        P(clip, seq, None),
        P(clip, None),
        P(both, None),
        P(both),
        P(both, None),
        P(both, None),
        P(both, None),
        P(None, both),
        P(),
        P(both, None),
        P(both, None),
    )
    return placed, given


def solution(mesh):
    if dict(mesh.shape) == {"clip": 4, "seq": 8}:
        grid = Mesh(mesh.devices.reshape(2, 2, 4, 2), ("y", "core", "z", "x"))
        placed, given = specs(("y", "core"), ("z", "x"))
        return jax.shard_map(
            local_fast, mesh=grid, in_specs=placed, out_specs=given, check_vma=False
        )
    placed, given = specs(("clip",), ("seq",))
    return jax.shard_map(local, mesh=mesh, in_specs=placed, out_specs=given, check_vma=False)
```

```python
import functools
import math

import jax
import jax.numpy as jnp
from jax import lax
from jax.experimental import pallas as pl
from jax.experimental.pallas import tpu as pltpu
from jax.sharding import Mesh
from jax.sharding import PartitionSpec as P

epsilon = 1e-06
theta_base = 10000.0
highest = lax.Precision.HIGHEST
bf16 = jnp.bfloat16
f32 = jnp.float32


def rms_norm(value):
    return value * lax.rsqrt(jnp.mean(value * value, axis=-1, keepdims=True) + epsilon)


def rms_back(value, upstream):
    return jax.vjp(rms_norm, value)[1](upstream)[0]


def rope_angles(shape_row, shift_row, position, half_dim):
    across = shape_row[2] + 1
    column_place = position % across + shift_row[2]
    row_place = position // across % shape_row[1] + shift_row[1]
    frame_place = position // (across * shape_row[1]) + shift_row[0]
    frame_count = half_dim // 4
    row_count = 3 * half_dim // 8
    column_count = half_dim - frame_count - row_count
    pieces = []
    for place_index, group_size in (
        (frame_place, frame_count),
        (row_place, row_count),
        (column_place, column_count),
    ):
        frequency = theta_base ** (-jnp.arange(group_size, dtype=jnp.float32) / group_size)
        pieces.append(place_index.astype(jnp.float32)[:, None] * frequency[None, :])
    return jnp.concatenate(pieces, axis=1)


def rotate(value, cosine, sine_table):
    half_dim = value.shape[-1] // 2
    front_half = value[..., :half_dim]
    back_half = value[..., half_dim:]
    return jnp.concatenate(
        [
            front_half * cosine - back_half * sine_table,
            back_half * cosine + front_half * sine_table,
        ],
        axis=-1,
    )


def soft_weights(scores):
    shifted = jnp.exp(scores - jnp.max(scores, axis=-1, keepdims=True))
    return shifted / jnp.sum(shifted, axis=-1, keepdims=True)


def local(
    tokens,
    caption,
    condition,
    caption_len,
    frame_shape,
    rope_shift,
    w_modulation,
    mod_bias,
    w_attention,
    w_output,
    w_caption,
    norm_gains,
    head_gate,
    w_gateup,
    w_down,
    cotangent,
):
    clip_count, local_len, model_width = tokens.shape
    head_count = head_gate.shape[0]
    head_dim = model_width // head_count
    score_scale = head_dim ** (-0.5)
    row_total = clip_count * local_len
    text_local = caption.shape[1]
    text_total = text_local * lax.axis_size("seq")
    gathered = (
        lax.all_gather(w_modulation, ("clip", "seq"), axis=0, tiled=True),
        lax.all_gather(mod_bias, ("clip", "seq"), axis=0, tiled=True),
        lax.all_gather(w_attention, ("clip", "seq"), axis=0, tiled=True),
        lax.all_gather(w_output, ("clip", "seq"), axis=0, tiled=True),
        lax.all_gather(w_caption, ("clip", "seq"), axis=0, tiled=True),
        lax.all_gather(norm_gains, ("clip", "seq"), axis=1, tiled=True),
    )
    full_mod, full_bias, full_attn, full_out, full_caption, full_gains = gathered
    gain_rows = full_gains.astype(jnp.float32)
    tanh_gate = jnp.tanh(head_gate.astype(jnp.float32))
    cond_float = condition.astype(jnp.float32)
    cond_act = jax.nn.silu(cond_float).astype(jnp.bfloat16)
    modulation = jnp.dot(cond_act, full_mod, preferred_element_type=jnp.float32) + full_bias.astype(
        jnp.float32
    )
    scale_attn = modulation[:, None, :model_width]
    gate_attn = jnp.tanh(modulation[:, None, model_width : 2 * model_width])
    scale_ffn = modulation[:, None, 2 * model_width : 3 * model_width]
    gate_ffn = jnp.tanh(modulation[:, None, 3 * model_width :])
    token_float = tokens.astype(jnp.float32)
    token_normed = rms_norm(token_float)
    normed_flat = (
        (token_normed * gain_rows[0] * (1.0 + scale_attn))
        .astype(jnp.bfloat16)
        .reshape(row_total, model_width)
    )
    projected = jnp.dot(normed_flat, full_attn, preferred_element_type=jnp.float32).reshape(
        clip_count, local_len, 3 * model_width
    )
    query_pre = projected[..., :model_width]
    key_pre = projected[..., model_width : 2 * model_width]
    query_normed = rms_norm(query_pre)
    key_normed = rms_norm(key_pre)
    position = lax.axis_index("seq") * local_len + jnp.arange(local_len, dtype=jnp.int32)
    angles = jax.vmap(
        lambda shape_row, shift_row: rope_angles(shape_row, shift_row, position, head_dim // 2)
    )(frame_shape, rope_shift)
    cosine = jnp.cos(angles)[:, :, None, :]
    sine_table = jnp.sin(angles)[:, :, None, :]
    split_shape = (clip_count, local_len, head_count, head_dim)
    queries = rotate((query_normed * gain_rows[4]).reshape(split_shape), cosine, sine_table).astype(
        jnp.bfloat16
    )
    key_rows = rotate((key_normed * gain_rows[5]).reshape(split_shape), cosine, sine_table).astype(
        jnp.bfloat16
    )
    value_rows = projected[..., 2 * model_width :].reshape(split_shape).astype(jnp.bfloat16)
    caption_flat = caption.reshape(clip_count * text_local, caption.shape[2])
    text_proj = jnp.dot(caption_flat, full_caption, preferred_element_type=jnp.float32).reshape(
        clip_count, text_local, 2 * model_width
    )
    text_key_pre = text_proj[..., :model_width]
    text_key_normed = rms_norm(text_key_pre)
    text_shape = (clip_count, text_local, head_count, head_dim)
    text_keys = (text_key_normed * gain_rows[6]).astype(jnp.bfloat16).reshape(text_shape)
    text_values = text_proj[..., model_width:].astype(jnp.bfloat16).reshape(text_shape)
    all_text_keys, all_text_values = (
        lax.all_gather(text_keys, "seq", axis=1, tiled=True),
        lax.all_gather(text_values, "seq", axis=1, tiled=True),
    )
    stat_shape = (clip_count, head_count, local_len)
    start_stats = (jnp.full(stat_shape, -1e30, jnp.float32), jnp.zeros(stat_shape, jnp.float32))
    piece_keys = lax.all_gather(key_rows, "seq", axis=1, tiled=True)
    key_count = piece_keys.shape[1]
    block_len = math.gcd(key_count, 512)

    def stat_one_block(block_index, inner_state):
        row_max, row_sum = inner_state
        block_keys = lax.dynamic_slice_in_dim(piece_keys, block_index * block_len, block_len, 1)
        scores = (
            jnp.einsum("cqhd,ckhd->chqk", queries, block_keys, preferred_element_type=jnp.float32)
            * score_scale
        )
        new_max = jnp.maximum(row_max, jnp.max(scores, axis=-1))
        row_sum = row_sum * jnp.exp(row_max - new_max) + jnp.sum(
            jnp.exp(scores - new_max[..., None]), axis=-1
        )
        return (new_max, row_sum)

    row_max, row_sum = lax.fori_loop(0, key_count // block_len, stat_one_block, start_stats)
    log_sum = row_max + jnp.log(row_sum)
    attend_piece_keys = lax.all_gather(key_rows, "seq", axis=1, tiled=True)
    piece_values = lax.all_gather(value_rows, "seq", axis=1, tiled=True)
    key_count = attend_piece_keys.shape[1]
    attend_block_len = math.gcd(key_count, 512)

    def attend_one_block(block_index, weighted):
        block_keys = lax.dynamic_slice_in_dim(
            attend_piece_keys, block_index * attend_block_len, attend_block_len, 1
        )
        block_values = lax.dynamic_slice_in_dim(
            piece_values, block_index * attend_block_len, attend_block_len, 1
        )
        scores = (
            jnp.einsum("cqhd,ckhd->chqk", queries, block_keys, preferred_element_type=jnp.float32)
            * score_scale
        )
        probs = jnp.exp(scores - log_sum[..., None]).astype(jnp.bfloat16)
        return weighted + jnp.einsum(
            "chqk,ckhd->chqd", probs, block_values, preferred_element_type=jnp.float32
        )

    weighted = lax.fori_loop(
        0,
        key_count // attend_block_len,
        attend_one_block,
        jnp.zeros(stat_shape + (head_dim,), jnp.float32),
    )
    self_out = jnp.transpose(weighted, (0, 2, 1, 3))
    usable = jnp.arange(text_total, dtype=jnp.int32)[None, :] < caption_len[:, None]
    text_scores = (
        jnp.einsum("cqhd,ckhd->chqk", queries, all_text_keys, preferred_element_type=jnp.float32)
        * score_scale
    )
    text_scores = jnp.where(usable[:, None, None, :], text_scores, -1e30)
    text_weights = soft_weights(text_scores)
    text_low = text_weights.astype(jnp.bfloat16)
    cross_out = jnp.einsum(
        "chqk,ckhd->cqhd", text_low, all_text_values, preferred_element_type=jnp.float32
    )
    mixed_heads = self_out + tanh_gate[None, None, :, None] * cross_out
    mixed_flat = mixed_heads.reshape(row_total, model_width).astype(jnp.bfloat16)
    attn_proj = jnp.dot(mixed_flat, full_out, preferred_element_type=jnp.float32).reshape(
        clip_count, local_len, model_width
    )
    attn_normed = rms_norm(attn_proj)
    residual = token_float + gate_attn * attn_normed * gain_rows[1]
    full_gateup, full_down = (
        lax.all_gather(w_gateup, ("clip", "seq"), axis=0, tiled=True),
        lax.all_gather(w_down, ("clip", "seq"), axis=0, tiled=True),
    )
    hidden_units = full_down.shape[0]
    residual_normed = rms_norm(residual)
    normed_ffn = (
        (residual_normed * gain_rows[2] * (1.0 + scale_ffn))
        .astype(jnp.bfloat16)
        .reshape(row_total, model_width)
    )
    gate_up = jnp.dot(normed_ffn, full_gateup, preferred_element_type=jnp.float32)
    gate_part = gate_up[:, :hidden_units]
    up_part = gate_up[:, hidden_units:]
    gate_sigmoid = jax.nn.sigmoid(gate_part)
    activated = (gate_part * gate_sigmoid * up_part).astype(jnp.bfloat16)
    down_proj = jnp.dot(activated, full_down, preferred_element_type=jnp.float32).reshape(
        clip_count, local_len, model_width
    )
    down_normed = rms_norm(down_proj)
    block_out = residual + gate_ffn * down_normed * gain_rows[3]
    upstream = cotangent.astype(jnp.float32)
    gain_three = jnp.sum(upstream * gate_ffn * down_normed, axis=(0, 1))
    grad_gate_ffn = jnp.sum(upstream * down_normed * gain_rows[3], axis=1) * (
        1.0 - gate_ffn[:, 0] * gate_ffn[:, 0]
    )
    grad_down = (
        rms_back(down_proj, upstream * gate_ffn * gain_rows[3])
        .astype(jnp.bfloat16)
        .reshape(row_total, model_width)
    )
    full_gateup, full_down = (
        lax.all_gather(w_gateup, ("clip", "seq"), axis=0, tiled=True),
        lax.all_gather(w_down, ("clip", "seq"), axis=0, tiled=True),
    )
    wgrad_down = jnp.dot(activated.T, grad_down, preferred_element_type=jnp.float32)
    grad_act = jnp.dot(grad_down, full_down.T, preferred_element_type=jnp.float32)
    grad_gate_part = grad_act * up_part * gate_sigmoid * (1.0 + gate_part * (1.0 - gate_sigmoid))
    grad_up_part = grad_act * gate_part * gate_sigmoid
    grad_gate_up = jnp.concatenate([grad_gate_part, grad_up_part], axis=1).astype(jnp.bfloat16)
    wgrad_gateup = jnp.dot(normed_ffn.T, grad_gate_up, preferred_element_type=jnp.float32)
    grad_normed_ffn = jnp.dot(
        grad_gate_up, full_gateup.T, preferred_element_type=jnp.float32
    ).reshape(clip_count, local_len, model_width)
    gain_two = jnp.sum(grad_normed_ffn * residual_normed * (1.0 + scale_ffn), axis=(0, 1))
    grad_scale_ffn = jnp.sum(grad_normed_ffn * residual_normed * gain_rows[2], axis=1)
    grad_residual = upstream + rms_back(
        residual, grad_normed_ffn * gain_rows[2] * (1.0 + scale_ffn)
    )
    gain_one = jnp.sum(grad_residual * gate_attn * attn_normed, axis=(0, 1))
    grad_gate_attn = jnp.sum(grad_residual * attn_normed * gain_rows[1], axis=1) * (
        1.0 - gate_attn[:, 0] * gate_attn[:, 0]
    )
    grad_attn = (
        rms_back(attn_proj, grad_residual * gate_attn * gain_rows[1])
        .astype(jnp.bfloat16)
        .reshape(row_total, model_width)
    )
    full_mod, full_attn, full_out, full_caption = (
        lax.all_gather(w_modulation, ("clip", "seq"), axis=0, tiled=True),
        lax.all_gather(w_attention, ("clip", "seq"), axis=0, tiled=True),
        lax.all_gather(w_output, ("clip", "seq"), axis=0, tiled=True),
        lax.all_gather(w_caption, ("clip", "seq"), axis=0, tiled=True),
    )
    wgrad_output = jnp.dot(mixed_flat.T, grad_attn, preferred_element_type=jnp.float32)
    grad_mixed = (
        jnp.dot(grad_attn, full_out.T, preferred_element_type=jnp.float32)
        .reshape(split_shape)
        .astype(jnp.bfloat16)
    )
    grad_float = grad_mixed.astype(jnp.float32)
    grad_head_gate = jnp.sum(grad_float * cross_out, axis=(0, 1, 3)) * (1.0 - tanh_gate * tanh_gate)
    delta_rows = jnp.sum(grad_float * self_out, axis=-1)
    delta_heads = jnp.transpose(delta_rows, (0, 2, 1))
    lse_rows = jnp.transpose(log_sum, (0, 2, 1))
    text_grad = (
        jnp.einsum(
            "cqhd,ckhd->chqk", grad_mixed, all_text_values, preferred_element_type=jnp.float32
        )
        * tanh_gate[None, :, None, None]
    )
    text_center = jnp.sum(text_weights * text_grad, axis=-1, keepdims=True)
    grad_text_scores = (text_weights * (text_grad - text_center)).astype(jnp.bfloat16)
    grad_queries = (
        jnp.einsum(
            "chqk,ckhd->cqhd", grad_text_scores, all_text_keys, preferred_element_type=jnp.float32
        )
        * score_scale
    )
    grad_text_keys = (
        jnp.einsum("chqk,cqhd->ckhd", grad_text_scores, queries, preferred_element_type=jnp.float32)
        * score_scale
    )
    grad_text_values = (
        jnp.einsum("chqk,cqhd->ckhd", text_low, grad_mixed, preferred_element_type=jnp.float32)
        * tanh_gate[None, None, :, None]
    )
    text_back_keys, text_back_values = (
        lax.psum_scatter(
            grad_text_keys.astype(jnp.bfloat16), "seq", scatter_dimension=1, tiled=True
        ).astype(jnp.float32),
        lax.psum_scatter(
            grad_text_values.astype(jnp.bfloat16), "seq", scatter_dimension=1, tiled=True
        ).astype(jnp.float32),
    )
    query_piece_keys = lax.all_gather(key_rows, "seq", axis=1, tiled=True)
    query_piece_values = lax.all_gather(value_rows, "seq", axis=1, tiled=True)
    key_count = query_piece_keys.shape[1]
    query_block_len = math.gcd(key_count, 512)

    def query_one_block(block_index, inner_state):
        block_keys = lax.dynamic_slice_in_dim(
            query_piece_keys, block_index * query_block_len, query_block_len, 1
        )
        block_values = lax.dynamic_slice_in_dim(
            query_piece_values, block_index * query_block_len, query_block_len, 1
        )
        scores = (
            jnp.einsum("cqhd,ckhd->chqk", queries, block_keys, preferred_element_type=jnp.float32)
            * score_scale
        )
        probs = jnp.exp(scores - log_sum[..., None])
        grad_probs = jnp.einsum(
            "cqhd,ckhd->chqk", grad_mixed, block_values, preferred_element_type=jnp.float32
        )
        grad_scores = (probs * (grad_probs - delta_heads[..., None])).astype(jnp.bfloat16)
        return (
            inner_state
            + jnp.einsum(
                "chqk,ckhd->cqhd", grad_scores, block_keys, preferred_element_type=jnp.float32
            )
            * score_scale
        )

    grad_self_queries = lax.fori_loop(
        0, key_count // query_block_len, query_one_block, jnp.zeros(split_shape, jnp.float32)
    )
    grad_queries = grad_queries + grad_self_queries
    zero_grads = (jnp.zeros(split_shape, jnp.float32), jnp.zeros(split_shape, jnp.float32))
    piece_queries = lax.all_gather(queries.astype(jnp.float32), "seq", axis=1, tiled=True).astype(
        jnp.bfloat16
    )
    piece_grads = lax.all_gather(grad_float, "seq", axis=1, tiled=True).astype(jnp.bfloat16)
    piece_lse = lax.all_gather(lse_rows, "seq", axis=1, tiled=True)
    piece_delta = lax.all_gather(delta_rows, "seq", axis=1, tiled=True)
    query_count = piece_queries.shape[1]
    key_block_len = math.gcd(query_count, 512)

    def key_one_block(block_index, inner_state):
        grad_key_acc, grad_value_acc = inner_state
        block_queries = lax.dynamic_slice_in_dim(
            piece_queries, block_index * key_block_len, key_block_len, 1
        )
        block_grads = lax.dynamic_slice_in_dim(
            piece_grads, block_index * key_block_len, key_block_len, 1
        )
        block_lse = jnp.transpose(
            lax.dynamic_slice_in_dim(piece_lse, block_index * key_block_len, key_block_len, 1),
            (0, 2, 1),
        )
        block_delta = jnp.transpose(
            lax.dynamic_slice_in_dim(piece_delta, block_index * key_block_len, key_block_len, 1),
            (0, 2, 1),
        )
        scores = (
            jnp.einsum(
                "cqhd,ckhd->chqk", block_queries, key_rows, preferred_element_type=jnp.float32
            )
            * score_scale
        )
        probs = jnp.exp(scores - block_lse[..., None])
        grad_value_acc = grad_value_acc + jnp.einsum(
            "chqk,cqhd->ckhd",
            probs.astype(jnp.bfloat16),
            block_grads,
            preferred_element_type=jnp.float32,
        )
        grad_probs = jnp.einsum(
            "cqhd,ckhd->chqk", block_grads, value_rows, preferred_element_type=jnp.float32
        )
        grad_scores = (probs * (grad_probs - block_delta[..., None])).astype(jnp.bfloat16)
        grad_key_acc = (
            grad_key_acc
            + jnp.einsum(
                "chqk,cqhd->ckhd", grad_scores, block_queries, preferred_element_type=jnp.float32
            )
            * score_scale
        )
        return (grad_key_acc, grad_value_acc)

    grad_keys, grad_values = lax.fori_loop(
        0, query_count // key_block_len, key_one_block, zero_grads
    )
    flat_shape = (clip_count, local_len, model_width)
    grad_query_rot = rotate(grad_queries, cosine, -sine_table).reshape(flat_shape)
    grad_key_rot = rotate(grad_keys, cosine, -sine_table).reshape(flat_shape)
    gain_four = jnp.sum(grad_query_rot * query_normed, axis=(0, 1))
    gain_five = jnp.sum(grad_key_rot * key_normed, axis=(0, 1))
    grad_query_pre = rms_back(query_pre, grad_query_rot * gain_rows[4])
    grad_key_pre = rms_back(key_pre, grad_key_rot * gain_rows[5])
    grad_projected = (
        jnp.concatenate([grad_query_pre, grad_key_pre, grad_values.reshape(flat_shape)], axis=-1)
        .astype(jnp.bfloat16)
        .reshape(row_total, 3 * model_width)
    )
    wgrad_attention = jnp.dot(normed_flat.T, grad_projected, preferred_element_type=jnp.float32)
    grad_normed = jnp.dot(grad_projected, full_attn.T, preferred_element_type=jnp.float32).reshape(
        flat_shape
    )
    gain_zero = jnp.sum(grad_normed * token_normed * (1.0 + scale_attn), axis=(0, 1))
    grad_scale_attn = jnp.sum(grad_normed * token_normed * gain_rows[0], axis=1)
    grad_tokens = grad_residual + rms_back(
        token_float, grad_normed * gain_rows[0] * (1.0 + scale_attn)
    )
    grad_text_key_rows = text_back_keys.reshape(clip_count, text_local, model_width)
    gain_six = jnp.sum(grad_text_key_rows * text_key_normed, axis=(0, 1))
    grad_text_pre = rms_back(text_key_pre, grad_text_key_rows * gain_rows[6])
    grad_text_proj = (
        jnp.concatenate(
            [grad_text_pre, text_back_values.reshape(clip_count, text_local, model_width)], axis=-1
        )
        .astype(jnp.bfloat16)
        .reshape(clip_count * text_local, 2 * model_width)
    )
    wgrad_caption = jnp.dot(caption_flat.T, grad_text_proj, preferred_element_type=jnp.float32)
    grad_caption = jnp.dot(
        grad_text_proj, full_caption.T, preferred_element_type=jnp.float32
    ).reshape(clip_count, text_local, caption.shape[2])
    grad_mod_row = jnp.concatenate(
        [grad_scale_attn, grad_gate_attn, grad_scale_ffn, grad_gate_ffn], axis=1
    )
    bias_grad = jnp.sum(grad_mod_row, axis=0)
    wgrad_modulation = jnp.dot(cond_act.astype(jnp.float32).T, grad_mod_row, precision=highest)
    cond_sigmoid = jax.nn.sigmoid(cond_float)
    grad_cond_act = jnp.dot(grad_mod_row, full_mod.astype(jnp.float32).T, precision=highest)
    grad_cond_part = grad_cond_act * cond_sigmoid * (1.0 + cond_float * (1.0 - cond_sigmoid))
    gain_grads = jnp.stack(
        [gain_zero, gain_one, gain_two, gain_three, gain_four, gain_five, gain_six]
    )
    partial_owned = (
        lax.psum_scatter(
            wgrad_modulation.astype(jnp.bfloat16), "clip", scatter_dimension=0, tiled=True
        ).astype(jnp.float32),
        lax.psum_scatter(
            bias_grad.astype(jnp.bfloat16), "clip", scatter_dimension=0, tiled=True
        ).astype(jnp.float32),
        lax.psum_scatter(
            wgrad_attention.astype(jnp.bfloat16), "clip", scatter_dimension=0, tiled=True
        ).astype(jnp.float32),
        lax.psum_scatter(
            wgrad_output.astype(jnp.bfloat16), "clip", scatter_dimension=0, tiled=True
        ).astype(jnp.float32),
        lax.psum_scatter(
            wgrad_caption.astype(jnp.bfloat16), "clip", scatter_dimension=0, tiled=True
        ).astype(jnp.float32),
        lax.psum_scatter(
            gain_grads.astype(jnp.bfloat16), "clip", scatter_dimension=1, tiled=True
        ).astype(jnp.float32),
        lax.psum_scatter(
            wgrad_gateup.astype(jnp.bfloat16), "clip", scatter_dimension=0, tiled=True
        ).astype(jnp.float32),
        lax.psum_scatter(
            wgrad_down.astype(jnp.bfloat16), "clip", scatter_dimension=0, tiled=True
        ).astype(jnp.float32),
    )
    owned = (
        lax.psum_scatter(
            partial_owned[0].astype(jnp.bfloat16), "seq", scatter_dimension=0, tiled=True
        ).astype(jnp.float32),
        lax.psum_scatter(
            partial_owned[1].astype(jnp.bfloat16), "seq", scatter_dimension=0, tiled=True
        ).astype(jnp.float32),
        lax.psum_scatter(
            partial_owned[2].astype(jnp.bfloat16), "seq", scatter_dimension=0, tiled=True
        ).astype(jnp.float32),
        lax.psum_scatter(
            partial_owned[3].astype(jnp.bfloat16), "seq", scatter_dimension=0, tiled=True
        ).astype(jnp.float32),
        lax.psum_scatter(
            partial_owned[4].astype(jnp.bfloat16), "seq", scatter_dimension=0, tiled=True
        ).astype(jnp.float32),
        lax.psum_scatter(
            partial_owned[5].astype(jnp.bfloat16), "seq", scatter_dimension=1, tiled=True
        ).astype(jnp.float32),
        lax.psum_scatter(
            partial_owned[6].astype(jnp.bfloat16), "seq", scatter_dimension=0, tiled=True
        ).astype(jnp.float32),
        lax.psum_scatter(
            partial_owned[7].astype(jnp.bfloat16), "seq", scatter_dimension=0, tiled=True
        ).astype(jnp.float32),
    )
    grad_gate_total = lax.psum(grad_head_gate, ("clip", "seq"))
    grad_condition = lax.psum(grad_cond_part, "seq")
    return (
        block_out,
        grad_tokens,
        grad_caption,
        grad_condition,
        owned[0],
        owned[1],
        owned[2],
        owned[3],
        owned[4],
        owned[5],
        grad_gate_total,
        owned[6],
        owned[7],
    )


def flip(value, axis):
    return lax.ppermute(value, axis, [(0, 1), (1, 0)])


def from_ahead(value, axis, step):
    count = lax.axis_size(axis)
    return lax.ppermute(value, axis, [((i + step) % count, i) for i in range(count)])


def swap_z(value, bit):
    return lax.ppermute(value, "z", [(i, i ^ bit) for i in range(4)])


def seq_terms(value):
    value = value + flip(value, "x")
    return [value] + [from_ahead(value, "z", k) for k in (1, 2, 3)]


def share(copies):
    return lax.all_to_all(copies, ("z", "x"), 0, 0, tiled=True)


def eight_sum(parts):
    total = parts[0]
    for s in range(1, 8):
        total = total + parts[s]
    return total


def spread(out):
    for s in range(1, 8):
        out[s] = out[0]


def four_sum(parts):
    return (parts[0] + parts[2]) + (parts[1] + parts[3])


def gather_chips(value):
    from_y = flip(value, "y")
    return [value, flip(value, "x"), from_y, flip(from_y, "x")]


def gather_clip(value):
    from_y = flip(value, "y")
    return [value, flip(value, "core"), from_y, flip(from_y, "core")]


def together(*values):
    return lax.optimization_barrier(values)


def rms_scale(square_mean):
    return lax.rsqrt(square_mean + epsilon)


def whole(shape):
    return pl.BlockSpec(shape, lambda step: (0,) * len(shape), pipeline_mode=pl.Buffered(1))


class Line:
    def __init__(self):
        self.last = ()

    def __call__(self, body, outs, *operands, scalars=0, scratch=(), after=(), far=0):
        held = pl.BlockSpec(memory_space=pltpu.SMEM)
        unread = pl.BlockSpec(memory_space=pl.ANY)
        waits = tuple(after) + self.last
        count, skip = len(operands), len(waits)

        def run(*refs):
            body(*refs[:count], *refs[count + skip :])

        given = pl.pallas_call(
            run,
            out_shape=[jax.ShapeDtypeStruct(shape, kind) for shape, kind in outs],
            grid=(1,),
            in_specs=[held] * scalars
            + [whole(value.shape) for value in operands[scalars : count - far]]
            + [unread] * far
            + [unread] * skip,
            out_specs=[whole(shape) for shape, kind in outs],
            scratch_shapes=list(scratch),
            compiler_params=pltpu.CompilerParams(vmem_limit_bytes=50 * 2**20),
        )(*operands, *waits)
        self.last = (min(given, key=lambda value: value.size),)
        return given


def alone(*args, **kinds):
    return Line()(*args, **kinds)


def dot(a, b):
    return jnp.dot(a, b, preferred_element_type=f32)


def dot_rows(a, b):
    return lax.dot_general(a, b, (((1,), (1,)), ((), ())), preferred_element_type=f32)


def dot_cols(a, b):
    return lax.dot_general(a, b, (((0,), (0,)), ((), ())), preferred_element_type=f32)


def round_up(value):
    return -(-value // 128) * 128


def prep_body(attn, gateup, cap, mod, extra, attn_out, ffn_out, cap_out, mod_out):
    width = attn.shape[1] // 3
    cols = width // 8
    pad = attn_out.shape[2] - 3 * cols
    for s in range(8):
        parts = [attn[:, p * width + s * cols : p * width + (s + 1) * cols] for p in range(3)]
        parts.append(jnp.zeros((attn.shape[0], pad), bf16))
        attn_out[s] = jnp.concatenate(parts, axis=1)
    own = gateup.shape[1] // 64
    for g in range(8):
        for part in range(2):
            for z in range(4):
                source = (part * 32 + (g // 2) * 8 + z * 2 + g % 2) * own
                target = (part * 4 + z) * own
                ffn_out[g, :, target : target + own] = gateup[:, source : source + own]
    own = cap_out.shape[2]
    for o in range(32):
        cap_out[o] = cap[:, o * own : (o + 1) * own]
    span = mod.shape[1]
    mod_out[:, :span] = mod[...]
    mod_out[:, span:] = extra[...]


def owner_of(place, r):
    return (place[0] ^ r) * 8 + place[5]


def modulate_body(place, cond, p0, p1, p2, p3, out):
    span = p0.shape[1] - 384
    chunk = span // 32
    gain = chunk // 4
    total = jnp.zeros((8, span), f32)
    for r, piece in enumerate((p0, p1, p2, p3)):
        row = cond[pl.ds(owner_of(place, r), 1), :]
        row = (row / (1.0 + jnp.exp(-row))).astype(bf16).astype(f32)
        row = jnp.broadcast_to(row, (8, row.shape[1])).astype(bf16)
        total = total + dot(row, piece[:, :span])
    out[...] = jnp.zeros(out.shape, f32)
    for i in range(32):
        out[i : i + 1, :chunk] = total[0:1, i * chunk : (i + 1) * chunk]
    for r, piece in enumerate((p0, p1, p2, p3)):
        extra = piece[0:16, span : span + 256].astype(f32)
        at = pl.ds(owner_of(place, r), 1)
        parts = [extra[0:1, :256]] + [extra[8 + g : 9 + g, :gain] for g in range(7)]
        parts.append(jnp.zeros((1, out.shape[1] - 256 - 7 * gain), f32))
        out[at, :] = out[at, :] + jnp.concatenate(parts, axis=1)


def vector_body(place, a, b, c, d, vector_out, column_out, small, turned):
    chunk = vector_out.shape[1] // 8
    gain = chunk // 4
    small[...] = four_sum([a[...], b[...], c[...], d[...]])
    vector_out[...] = jnp.zeros(vector_out.shape, f32)
    for i in range(32):
        to = (i % 8) * chunk
        vector_out[i // 8 : i // 8 + 1, to : to + chunk] = small[i : i + 1, :chunk]
        for g in range(7):
            vector_out[4 + g : 5 + g, i * gain : (i + 1) * gain] = small[
                i : i + 1, 256 + g * gain : 256 + (g + 1) * gain
            ]
    vector_out[1:2] = jnp.tanh(vector_out[1:2])
    vector_out[3:4] = jnp.tanh(vector_out[3:4])
    turned[...] = jnp.zeros(turned.shape, f32)
    for j in range(4):
        row = small[pl.ds(place[5] * 4 + j, 1), :]
        for p in range(3):
            turned[p : p + 1, j * gain : (j + 1) * gain] = row[
                :, 256 + (4 + p) * gain : 256 + (5 + p) * gain
            ]
    column_out[...] = turned[...].T


def caption_slice(weight, s):
    cols = weight.shape[1] // 16
    return jnp.concatenate(
        [weight[:, (p * 8 + s) * cols : (p * 8 + s + 1) * cols] for p in range(2)], axis=1
    )


def caption_body(place, cap, weight, keep_out, send_out):
    for s in range(8):
        own = caption_slice(weight, s)
        j, k = (s % 2) ^ place[2], (s // 2 - place[1] + 4) % 4
        for r in range(4):
            part = dot(cap[place[0] ^ r], own).astype(bf16)
            if r % 2:
                send_out[r // 2, j, k] = part
            else:
                keep_out[r // 2, j, k] = part


def qkv_body(place, tokens, *refs):
    weights = refs[:4]
    vector, normed_out, proj_out, stats_out = refs[4:]
    total, width = tokens.shape
    step = total // 4
    block = width // 4
    cols = width // 8
    scale, gain = vector[0:1], vector[4:5]
    for b in range(4):
        at = slice(b * step, (b + 1) * step)
        value = tokens[at].astype(f32)
        inverse = rms_scale(jnp.mean(value * value, axis=1, keepdims=True))
        normed_out[at] = (value * inverse * gain * (1.0 + scale)).astype(bf16)
    for b in range(4):
        at = slice(b * step, (b + 1) * step)
        part = jnp.zeros((step, weights[0].shape[1]), f32)
        for r, weight in enumerate(weights):
            from_col = pl.multiple_of((place[0] ^ r) * block, 128)
            part = part + dot(normed_out[at, pl.ds(from_col, block)], weight[...])
        proj_out[:, at] = part.T
    stats_out[...] = jnp.zeros(stats_out.shape, f32)
    query, key = proj_out[:cols], proj_out[cols : 2 * cols]
    stats_out[0:1, :] = jnp.sum(query * query, axis=0, keepdims=True)
    stats_out[1:2, :] = jnp.sum(key * key, axis=0, keepdims=True)


def add_four_body(keep, got, *outs):
    for k, out in enumerate(outs):
        out[...] = (keep[k].astype(f32) + got[k].astype(f32)).astype(bf16)


def text_body(a, b, c, d, text_out, stats_out):
    total = four_sum([v[...].astype(f32) for v in (a, b, c, d)])
    text_out[...] = total.T
    key = text_out[: text_out.shape[0] // 2]
    stats_out[...] = jnp.broadcast_to(jnp.sum(key * key, axis=0, keepdims=True), stats_out.shape)


def turn(value, cosine, sine):
    half = value.shape[0] // 2
    front, back = value[:half], value[half:]
    return jnp.concatenate([front * cosine - back * sine, back * cosine + front * sine], axis=0)


def text_softmax(scores, length):
    place = lax.broadcasted_iota(jnp.int32, scores.shape, 0)
    scores = jnp.where(place < length, scores, -1e30)
    shifted = jnp.exp(scores - jnp.max(scores, axis=0, keepdims=True))
    return shifted / jnp.sum(shifted, axis=0, keepdims=True)


def attend_body(
    heads,
    proj,
    stats_a,
    stats_b,
    stats_c,
    stats_d,
    gains,
    cosine,
    sine,
    query_out,
    key_out,
    value_out,
    self_out,
    sum_out,
    stats_out,
):
    total = proj.shape[1]
    cols = query_out.shape[0]
    dim = cols // heads
    width = cols * 8
    step = total // 2
    score_scale = dim ** (-0.5)
    stats_out[...] = four_sum([stats_a[...], stats_b[...], stats_c[...], stats_d[...]])
    scales = rms_scale(stats_out[0:2, :] / width)
    value_out[...] = proj[2 * cols : 3 * cols].astype(bf16)
    sum_out[...] = jnp.zeros(sum_out.shape, f32)
    for h in range(heads):
        at = slice(h * dim, (h + 1) * dim)
        query = proj[at] * scales[0:1] * gains[at, 0:1]
        query_out[at] = turn(query, cosine[...], sine[...]).astype(bf16)
        key = proj[cols + h * dim : cols + (h + 1) * dim] * scales[1:2] * gains[at, 1:2]
        key_out[at] = turn(key, cosine[...], sine[...]).astype(bf16)
        key_rows = key_out[at].T
        for b in range(2):
            to = slice(b * step, (b + 1) * step)
            scores = dot(key_rows, query_out[at, to]) * score_scale
            most = jnp.max(scores, axis=0, keepdims=True)
            weights = jnp.exp(scores - most)
            whole = jnp.sum(weights, axis=0, keepdims=True)
            sum_out[h : h + 1, to] = most + jnp.log(whole)
            self_out[at, to] = dot(value_out[at], weights.astype(bf16)) * (1.0 / whole)


def cross_body(
    heads,
    gate,
    length,
    query,
    self_out,
    text,
    stats_a,
    stats_b,
    stats_c,
    stats_d,
    squares,
    gains,
    mixed_out,
    cross_out,
    text_key_out,
    text_value_out,
    stats_out,
):
    cols, total = query.shape
    dim = cols // heads
    width = cols * 8
    step = total // 2
    piece = mixed_out.shape[2]
    score_scale = dim ** (-0.5)
    text_stats = four_sum([stats_a[...], stats_b[...], stats_c[...], stats_d[...]])
    stats_out[...] = squares[...]
    stats_out[2:3, : text.shape[1]] = text_stats[0:1]
    text_scale = rms_scale(text_stats[0:1] / width)
    text_key_out[...] = (text[:cols] * text_scale * gains[:cols, 2:3]).astype(bf16)
    text_value_out[...] = text[cols : 2 * cols].astype(bf16)
    for h in range(heads):
        at = slice(h * dim, (h + 1) * dim)
        text_rows = text_key_out[at].T
        for b in range(2):
            to = slice(b * step, (b + 1) * step)
            text_weights = text_softmax(dot(text_rows, query[at, to]) * score_scale, length[0])
            cross = dot(text_value_out[at], text_weights.astype(bf16))
            cross_out[at, to] = cross
            mixed = (self_out[at, to] + gate[h] * cross).astype(bf16)
            for s in range(step // piece):
                mixed_out[b * (step // piece) + s, at] = mixed[:, s * piece : (s + 1) * piece]


def stack_body(*refs):
    rows = refs[0].shape[0]
    for i, piece in enumerate(refs[:-1]):
        refs[-1][i * rows : (i + 1) * rows] = piece[...]


def all_ahead(value):
    return [value] + [from_ahead(value, "z", k) for k in (1, 2, 3)]


def output_weight_body(place, *refs):
    own = refs[0].shape[0] // 8
    for r in range(4):
        for j in range(2):
            for k in range(4):
                owner = ((place[0] ^ r) * 4 + (place[1] ^ k)) * 2 + (place[2] ^ j)
                at = (j * 4 + k) * own
                refs[4][pl.ds(pl.multiple_of(owner * own, 16), own), :] = refs[r][at : at + own, :]


def output_body(
    mixed, weight, token, vector, proj_out, residual_out, normed_out, plane_out
):
    proj = dot_cols(mixed[...], weight[...])
    proj_out[...] = proj
    normed = proj * rms_scale(jnp.mean(proj * proj, axis=1, keepdims=True))
    residual = token[...].astype(f32) + vector[1:2] * normed * vector[5:6]
    residual_out[...] = residual
    normed = residual * rms_scale(jnp.mean(residual * residual, axis=1, keepdims=True))
    normed_out[...] = (normed * vector[6:7] * (1.0 + vector[2:3])).astype(bf16)
    own = plane_out.shape[1] // 4
    for g in range(8):
        for z in range(4):
            source = (((g // 2) * 4 + z) * 2 + g % 2) * own
            plane_out[g, z * own : (z + 1) * own] = mixed[source : source + own, :]


def spread_out(parts, own_out, mid_out, x_out, y_out):
    half = own_out.shape[0] // 2
    own, for_x, for_y, far = parts
    own_out[...] = own
    mid_out[:half] = for_y[:half]
    mid_out[half:] = for_x[half:]
    x_out[:half] = for_x[:half].astype(bf16)
    x_out[half:] = far[:half].astype(bf16)
    y_out[:half] = for_y[half:].astype(bf16)
    y_out[half:] = far[half:].astype(bf16)


def feed_body(*refs):
    pieces, gateups, downs = refs[:4], refs[4:6], refs[6:8]
    normed_out, gate_up_out, active_out = refs[8:11]
    rows = pieces[0].shape[0]
    hidden = downs[0].shape[0]
    step = rows * 2
    for r in range(4):
        normed_out[r * rows : (r + 1) * rows] = pieces[r][...]
    parts = []
    for b in range(2):
        at = slice(b * step, (b + 1) * step)
        total = None
        for core in range(2):
            both = dot(normed_out[at], gateups[core][...])
            gate_up_out[core, at] = both
            gate, up = both[:, :hidden], both[:, hidden:]
            active = (gate * jax.nn.sigmoid(gate) * up).astype(bf16)
            active_out[core, at] = active
            part = dot(active, downs[core][...])
            total = part if total is None else total + part
        parts += [total[:rows], total[rows:]]
    spread_out(parts, *refs[11:])


def scatter_two_body(own, mid, by_x, by_y, own_out, y_out, x_out):
    half = own.shape[0] // 2
    own_out[:half] = own[:half] + by_x[:half].astype(f32)
    own_out[half:] = own[half:] + by_y[:half].astype(f32)
    y_out[...] = (mid[:half] + by_x[half:].astype(f32)).astype(bf16)
    x_out[...] = (mid[half:] + by_y[half:].astype(f32)).astype(bf16)


def scatter_chips(line, own, mid, to_x, to_y, between=None):
    rows, width = own.shape
    by_x, by_y = flip(to_x, "x"), flip(to_y, "y")
    if between is not None:
        by_x, by_y, *grads = together(by_x, by_y, *between())
        between.grads = grads
    own, to_y, to_x = line(
        scatter_two_body,
        [((rows, width), f32), ((rows // 2, width), bf16), ((rows // 2, width), bf16)],
        own,
        mid,
        by_x,
        by_y,
    )
    return own, flip(to_y, "y"), flip(to_x, "x")


def whole_sum(own, by_y, by_x):
    half = own.shape[0] // 2
    return jnp.concatenate(
        [own[:half] + by_y[...].astype(f32), own[half:] + by_x[...].astype(f32)], axis=0
    )


def rms_pull(normed, inverse, grad):
    return (grad - normed * jnp.mean(grad * normed, axis=1, keepdims=True)) * inverse


def middle_body(own, by_y, by_x, residual, cot, vector, block_out, grad_out, sum_out):
    down = whole_sum(own, by_y, by_x)
    inverse = rms_scale(jnp.mean(down * down, axis=1, keepdims=True))
    normed = down * inverse
    gate, gain = vector[3:4], vector[7:8]
    block_out[...] = residual[...] + gate * normed * gain
    upstream = cot[...].astype(f32)
    sum_out[...] = jnp.broadcast_to(
        jnp.sum(upstream * normed, axis=0, keepdims=True), sum_out.shape
    )
    grad_out[...] = rms_pull(normed, inverse, upstream * gate * gain).astype(bf16)


def feed_back_body(*refs):
    pieces, gateups, downs, gate_up = refs[:4], refs[4:6], refs[6:8], refs[8]
    grad_out, hidden_out = refs[9:11]
    rows = pieces[0].shape[0]
    hidden = downs[0].shape[0]
    step = rows * 2
    for r in range(4):
        grad_out[r * rows : (r + 1) * rows] = pieces[r][...]
    parts = []
    for b in range(2):
        at = slice(b * step, (b + 1) * step)
        total = None
        for core in range(2):
            active_grad = dot_rows(grad_out[at], downs[core][...])
            gate, up = gate_up[core, at, :hidden], gate_up[core, at, hidden:]
            sigmoid = jax.nn.sigmoid(gate)
            gate_grad = active_grad * up * sigmoid * (1.0 + gate * (1.0 - sigmoid))
            hidden_out[core, at, :hidden] = gate_grad.astype(bf16)
            hidden_out[core, at, hidden:] = (active_grad * gate * sigmoid).astype(bf16)
            part = dot_rows(hidden_out[core, at], gateups[core][...])
            total = part if total is None else total + part
        parts += [total[:rows], total[rows:]]
    spread_out(parts, *refs[11:])


def down_weight_body(active, down_grad, *outs):
    for core in range(2):
        outs[core][...] = dot_cols(active[core], down_grad[...]).astype(bf16)


def gateup_weight_body(normed, hidden_grad, *outs):
    width = normed.shape[1]
    block = width // 4
    own = block // 4
    for core in range(2):
        for c in range(4):
            part = dot_cols(normed[:, c * block : (c + 1) * block], hidden_grad[core]).astype(bf16)
            for z in range(4):
                outs[core][z, c * own : (c + 1) * own] = part[z * own : (z + 1) * own]


def residual_back_body(
    own,
    by_y,
    by_x,
    residual,
    proj,
    cot,
    vector,
    weight,
    residual_grad_out,
    grad_out,
    mixed_out,
    sum_out,
):
    grad = whole_sum(own, by_y, by_x)
    value = residual[...]
    inverse = rms_scale(jnp.mean(value * value, axis=1, keepdims=True))
    normed = value * inverse
    sum_out[...] = jnp.zeros(sum_out.shape, f32)
    sum_out[1:2] = jnp.sum(grad * normed, axis=0, keepdims=True)
    grad = cot[...].astype(f32) + rms_pull(
        normed, inverse, grad * vector[6:7] * (1.0 + vector[2:3])
    )
    residual_grad_out[...] = grad
    value = proj[...]
    inverse = rms_scale(jnp.mean(value * value, axis=1, keepdims=True))
    normed = value * inverse
    sum_out[0:1] = jnp.sum(grad * normed, axis=0, keepdims=True)
    grad = rms_pull(normed, inverse, grad * vector[1:2] * vector[5:6]).astype(bf16)
    grad_out[...] = grad
    mixed_out[...] = dot_rows(weight[...], grad).astype(bf16)


def text_back_body(
    heads,
    gate,
    length,
    pieces,
    query,
    text_key,
    text_value,
    cross,
    text,
    stats,
    gains,
    grad_out,
    query_out,
    key_out,
    value_out,
    stats_out,
    gain_out,
    gate_out,
):
    cols, total = query.shape
    dim = cols // heads
    width = cols * 8
    step = total // 2
    score_scale = dim ** (-0.5)
    piece = pieces.shape[2]
    for s in range(pieces.shape[0]):
        grad_out[:, s * piece : (s + 1) * piece] = pieces[s]
    gate_out[...] = jnp.zeros(gate_out.shape, f32)
    for h in range(heads):
        at = slice(h * dim, (h + 1) * dim)
        text_rows, value_rows = text_key[at].T, text_value[at].T
        grad = grad_out[at].astype(f32)
        gate_sum = jnp.sum(jnp.sum(grad * cross[at], axis=0, keepdims=True), axis=1, keepdims=True)
        gate_out[h : h + 1, :] = jnp.broadcast_to(
            gate_sum * (1.0 - gate[h] * gate[h]), (1, gate_out.shape[1])
        )
        key_grad = jnp.zeros((dim, text_key.shape[1]), f32)
        value_grad = jnp.zeros((dim, text_key.shape[1]), f32)
        for b in range(2):
            to = slice(b * step, (b + 1) * step)
            block, back = query[at, to], grad_out[at, to]
            weights = text_softmax(dot(text_rows, block) * score_scale, length[0])
            upstream = dot(value_rows, back) * gate[h]
            center = jnp.sum(weights * upstream, axis=0, keepdims=True)
            score_grad = (weights * (upstream - center)).astype(bf16)
            query_out[at, to] = dot(text_key[at], score_grad)
            key_grad = key_grad + dot_rows(block, score_grad)
            value_grad = value_grad + dot_rows(back, weights.astype(bf16))
        key_out[at] = key_grad * score_scale
        value_out[at] = value_grad * gate[h]
    text_scale = rms_scale(stats[2:3, : text.shape[1]] / width)
    normed = text[:cols] * text_scale
    gain_out[...] = jnp.zeros(gain_out.shape, f32)
    gain_out[:cols] = jnp.broadcast_to(
        jnp.sum(key_out[...] * normed, axis=1, keepdims=True), (cols, gain_out.shape[1])
    )
    key_out[...] = key_out[...] * gains[:cols, 2:3]
    stats_out[...] = jnp.broadcast_to(
        jnp.sum(key_out[...] * normed, axis=0, keepdims=True), stats_out.shape
    )


def text_proj_back_body(key, value, text, stats, means, w0, w1, w2, w3, *outs):
    cols = key.shape[0]
    width = cols * 8
    text_scale = rms_scale(stats[2:3, : text.shape[1]] / width)
    normed = text[:cols] * text_scale
    mean = eight_sum(means)[2:3, : text.shape[1]] / width
    before = (key[...] - normed * mean) * text_scale
    grad = jnp.concatenate([before, value[...]], axis=0).T.astype(bf16)
    own, wide = w0.shape[0], grad.shape[1]
    rows = grad.shape[0] * wide // width
    for k, piece in enumerate((w0, w1, w2, w3)):
        outs[k][:own] = piece[...]
        for q in range(width // wide):
            outs[k][own : own + rows, q * wide : (q + 1) * wide] = grad[
                q * rows : (q + 1) * rows
            ]


def text_stack_body(a, b, c, d, out):
    wide = out.shape[1]
    total = out.shape[0] // 4
    count = a.shape[1] // wide
    rows = total // count
    for k, piece in enumerate((a, b, c, d)):
        for q in range(count):
            out[k * total + q * rows : k * total + (q + 1) * rows] = piece[
                piece.shape[0] - rows :, q * wide : (q + 1) * wide
            ]


def caption_back_body(place, cap, *refs):
    grads, (weight, cond, weight_out, piece_out, blocks) = refs[:4], refs[4:]
    cols = weight.shape[1] // 16
    rows = cap.shape[1]
    own_rows = rows // 8
    for j in range(2):
        for k in range(4):
            at = slice((j * 4 + k) * rows, (j * 4 + k + 1) * rows)
            part = None
            for r in range(4):
                term = dot_cols(cap[place[0] ^ r], grads[r][at, :])
                part = term if part is None else part + term
            blocks[(place[1] + k) % 4 * 2 + (place[2] ^ j)] = part
    for s in range(8):
        for p in range(2):
            weight_out[:, (p * 8 + s) * cols : (p * 8 + s + 1) * cols] = blocks[
                s, :, p * cols : (p + 1) * cols
            ]
    for s in range(8):
        blocks[s] = caption_slice(weight, s).astype(f32)
    for r in range(4):
        clip = place[0] ^ r
        total = None
        for j in range(2):
            for k in range(4):
                at = slice((j * 4 + k) * rows, (j * 4 + k + 1) * rows)
                own = blocks[(place[1] + k) % 4 * 2 + (place[2] ^ j)].astype(bf16)
                term = dot_rows(grads[r][at, :], own)
                total = term if total is None else total + term
        for s in range(8):
            piece_out[clip * 8 + s, :own_rows] = total[s * own_rows : (s + 1) * own_rows]
            piece_out[clip * 8 + s, own_rows:] = cond[clip]


def attend_back_body(
    heads,
    grad,
    query,
    key,
    value,
    self_out,
    sums,
    text_query,
    text_stats,
    proj,
    stats,
    gains,
    cosine,
    sine,
    query_in_out,
    key_in_out,
    value_grad_out,
    stats_out,
    gain_out,
):
    cols, total = query.shape
    dim = cols // heads
    width = cols * 8
    step = total // 2
    score_scale = dim ** (-0.5)
    scales = rms_scale(stats[0:2, :] / width)
    stats_out[0] = jnp.zeros(stats_out.shape[1:], f32)
    gain_out[...] = jnp.zeros(gain_out.shape, f32)
    query_total = jnp.zeros((1, total), f32)
    key_total = jnp.zeros((1, total), f32)
    for h in range(heads):
        at = slice(h * dim, (h + 1) * dim)
        key_rows, value_rows = key[at].T, value[at].T
        delta = jnp.sum(grad[at].astype(f32) * self_out[at], axis=0, keepdims=True)
        key_grad = jnp.zeros((dim, total), f32)
        value_grad = jnp.zeros((dim, total), f32)
        query_parts = []
        for b in range(2):
            to = slice(b * step, (b + 1) * step)
            block, back = query[at, to], grad[at, to]
            weights = jnp.exp(dot(key_rows, block) * score_scale - sums[h : h + 1, to])
            value_grad = value_grad + dot_rows(back, weights.astype(bf16))
            score_grad = (weights * (dot(value_rows, back) - delta[:, to])).astype(bf16)
            key_grad = key_grad + dot_rows(block, score_grad)
            query_parts.append(dot(key[at], score_grad))
        value_grad_out[at] = value_grad.astype(bf16)
        query_grad = (jnp.concatenate(query_parts, axis=1) + text_query[at]) * score_scale
        query_grad = turn(query_grad, cosine[...], -sine[...])
        key_grad = turn(key_grad * score_scale, cosine[...], -sine[...])
        query_normed = proj[at] * scales[0:1]
        key_normed = proj[cols + h * dim : cols + (h + 1) * dim] * scales[1:2]
        gain_out[at, 0:1] = jnp.sum(query_grad * query_normed, axis=1, keepdims=True)
        gain_out[at, 1:2] = jnp.sum(key_grad * key_normed, axis=1, keepdims=True)
        query_grad = query_grad * gains[at, 0:1]
        key_grad = key_grad * gains[at, 1:2]
        query_in_out[at] = query_grad
        key_in_out[at] = key_grad
        query_total = query_total + jnp.sum(query_grad * query_normed, axis=0, keepdims=True)
        key_total = key_total + jnp.sum(key_grad * key_normed, axis=0, keepdims=True)
    stats_out[0, 0:1, :] = query_total
    stats_out[0, 1:2, :] = key_total
    stats_out[0, 2:3, : text_stats.shape[1]] = text_stats[0:1]
    spread(stats_out)


def project_back_body(place, *refs):
    tokens, weights = refs[0], refs[1:5]
    query_in, key_in, value_grad, proj, stats = refs[5:10]
    mean_parts, normed, vector = refs[10:13]
    middle_sums, residual_sums, own_gains, text_gains, gate_sums = refs[13:18]
    part_out, near_out, far_out, sums_out = refs[18:22]
    low, turned, unit, sum_out = refs[22:]
    cols, total = query_in.shape
    width = normed.shape[1]
    block = width // 4
    rows = total // 8
    scales = rms_scale(stats[0:2, :] / width)
    means = eight_sum(mean_parts) / width
    low[...] = jnp.zeros(low.shape, bf16)
    low[:cols] = (
        (query_in[...] - proj[:cols] * scales[0:1] * means[0:1, :]) * scales[0:1]
    ).astype(bf16)
    low[cols : 2 * cols] = (
        (key_in[...] - proj[cols : 2 * cols] * scales[1:2] * means[1:2, :]) * scales[1:2]
    ).astype(bf16)
    low[2 * cols : 3 * cols] = value_grad[...]
    turned[...] = low[...].T
    sum_out[...] = jnp.zeros(sum_out.shape, f32)
    for b in range(4):
        at = slice(b * 2 * rows, (b + 1) * 2 * rows)
        value = tokens[at].astype(f32)
        unit[...] = value * rms_scale(jnp.mean(value * value, axis=1, keepdims=True))
        for r in range(4):
            to_col = pl.ds(pl.multiple_of((place[0] ^ r) * block, 128), block)
            part = dot_rows(turned[at], weights[r][...])
            sum_out[0:1, to_col] = sum_out[0:1, to_col] + jnp.sum(
                part * unit[:, to_col], axis=0, keepdims=True
            )
            part_out[at, to_col] = part.astype(bf16)
    for r in range(4):
        from_col = pl.ds(pl.multiple_of((place[0] ^ r) * block, 128), block)
        part = dot(low[...], normed[:, from_col]).T.astype(bf16)
        if r % 2:
            far_out[r // 2] = part
        else:
            near_out[r // 2] = part
    sum_out[1:3] = residual_sums[0:2]
    sum_out[3:4] = middle_sums[0:1]
    lane = lax.broadcasted_iota(jnp.int32, (1, width), 1)
    mine = lane // cols == place[5]
    own_rows, text_row = own_gains[...].T, text_gains[...].T
    for at, row in ((4, own_rows[0:1]), (5, own_rows[1:2]), (6, text_row[0:1])):
        wide = jnp.concatenate([row[:, :cols]] * 8, axis=1)
        sum_out[at : at + 1] = jnp.where(mine, wide, 0.0)
    heads = 3
    gates = jnp.zeros((1, width), f32)
    for h in range(heads):
        gates = jnp.where(lane == place[5] * heads + h, gate_sums[h : h + 1, 0:1], gates)
    sum_out[7:8] = gates
    for s in range(8):
        sums_out[s] = sum_out[...]


def add_body(a, b, out):
    out[...] = (a[...].astype(f32) + b[...].astype(f32)).astype(bf16)


def add_pair_body(keep, got, keep_out, send_out):
    keep_out[...] = (keep[0].astype(f32) + got[0].astype(f32)).astype(bf16)
    send_out[...] = (keep[1].astype(f32) + got[1].astype(f32)).astype(bf16)


def final_body(grad_normed, residual_grad, token, vector, out):
    grad = grad_normed[...].astype(f32)
    value = token[...].astype(f32)
    inverse = rms_scale(jnp.mean(value * value, axis=1, keepdims=True))
    out[...] = residual_grad[...] + rms_pull(
        value * inverse, inverse, grad * vector[4:5] * (1.0 + vector[0:1])
    )


def modulation_back_body(parts, vector, shared_out):
    sums = eight_sum(parts)
    width = sums.shape[1]
    scale_attn, gate_attn, scale_ffn, gate_ffn = [vector[i : i + 1] for i in range(4)]
    gains = [vector[4 + i : 5 + i] for i in range(4)]
    zero, one, two, three = [sums[i : i + 1] for i in range(4)]
    rows = [
        gains[0] * zero,
        gains[1] * one * (1.0 - gate_attn * gate_attn),
        gains[2] * two,
        gains[3] * three * (1.0 - gate_ffn * gate_ffn),
    ]
    shared_out[...] = jnp.zeros(shared_out.shape, f32)
    for i in range(4):
        shared_out[i : i + 1] = rows[i]
    shared_out[4:5] = (1.0 + scale_attn) * zero
    shared_out[5:6] = gate_attn * one
    shared_out[6:7] = (1.0 + scale_ffn) * two
    shared_out[7:8] = gate_ffn * three
    shared_out[8:12] = sums[4:8]


def modulation_weight_body(
    place, t0, t1, t2, t3, p0, p1, p2, p3, weight_out, total_out, cond_out, square
):
    width = t0.shape[1]
    rows = weight_out.shape[0]
    span = 4 * width
    owner = owner_of(place, 0)
    total_out[...] = (t0[...] + t1[...]) + (t2[...] + t3[...])
    lane = lax.broadcasted_iota(jnp.int32, (rows, square.shape[0]), 1)
    columns = []
    for piece in (p0, p1, p2, p3):
        cond = piece[:, span + 256 : span + 384].astype(f32)
        cond = (cond / (1.0 + jnp.exp(-cond))).astype(bf16).astype(f32)
        square[...] = jnp.zeros(square.shape, f32)
        square[:rows] = cond
        turned = square[...].T[:rows]
        columns.append(jnp.sum(jnp.where(lane == owner, turned, 0.0), axis=1, keepdims=True))
    for i in range(4):
        part = None
        for column, shared in zip(columns, (t0, t1, t2, t3)):
            term = column * shared[i : i + 1, :]
            part = term if part is None else part + term
        weight_out[:, i * width : (i + 1) * width] = part
    lanes = cond_out.shape[2]
    for r, shared in enumerate((t0, t1, t2, t3)):
        back = jnp.zeros((8, rows), f32)
        for i in range(4):
            back = back + lax.dot_general(
                jnp.broadcast_to(shared[i : i + 1, :], (8, width)),
                p0[:, i * width : (i + 1) * width].astype(f32),
                (((1,), (1,)), ((), ())),
                precision=highest,
                preferred_element_type=f32,
            )
        cond_out[place[0] ^ r] = jnp.concatenate(
            [back, jnp.zeros((8, lanes - rows), f32)], axis=1
        )


def attention_grad_body(pieces, grad_out):
    cols = grad_out.shape[1] // 24
    for s in range(8):
        for p in range(3):
            grad_out[:, (p * 8 + s) * cols : (p * 8 + s + 1) * cols] = pieces[
                s, :, p * cols : (p + 1) * cols
            ].astype(f32)


def gateup_grad_body(pieces, grad_out):
    own = grad_out.shape[1] // 64
    for g in range(8):
        for part in range(2):
            for z in range(4):
                target = (part * 32 + (g // 2) * 8 + z * 2 + g % 2) * own
                source = (part * 4 + z) * own
                grad_out[:, target : target + own] = pieces[g, :, source : source + own].astype(f32)


def caption_grad_body(pieces, grad_out, cond_out):
    own = pieces.shape[2]
    rows = grad_out.shape[0]
    for o in range(32):
        grad_out[:, o * own : (o + 1) * own] = pieces[o, :rows]
        cond_out[o : o + 1] = pieces[o, rows : rows + 1]


def output_grad_body(place, mixed, *refs):
    grads, weight_outs, held, done = refs[:8], refs[8:12], refs[12], refs[13]
    rows = mixed.shape[2]
    copies = [
        pltpu.make_async_copy(grads[r], held.at[pl.ds(r * rows, rows)], done.at[r])
        for r in range(8)
    ]
    for copy in copies:
        copy.start()
    total = None
    for r in range(8):
        copies[r].wait()
        core, y, x = r // 4, (r // 2) % 2, r % 2
        source = ((place[3] ^ y) * 2 + (place[4] ^ core)) * 2 + (place[2] ^ x)
        part = dot(mixed[source], held[r * rows : (r + 1) * rows])
        total = part if total is None else total + part
    own = total.shape[0] // 4
    held[: total.shape[0]] = total.astype(bf16)
    for k in range(4):
        source = pl.multiple_of((place[1] + k) % 4 * own, 16)
        weight_outs[k][...] = held[pl.ds(source, own), :]


def output_sum_body(a, b, c, d, out):
    out[...] = four_sum([v[: out.shape[0]].astype(f32) for v in (a, b, c, d)])


def local_fast(
    tokens,
    caption,
    condition,
    caption_len,
    frame_shape,
    rope_shift,
    w_modulation,
    mod_bias,
    w_attention,
    w_output,
    w_caption,
    norm_gains,
    head_gate,
    w_gateup,
    w_down,
    cotangent,
):
    seq_axes = ("z", "x")
    all_axes = ("y", "core") + seq_axes
    plane_axes = ("y", "core", "x")
    rows, width = tokens.shape[1:]
    total = rows * 8
    heads = head_gate.shape[0]
    head_dim = width // heads
    own_heads = heads // 8
    cols = own_heads * head_dim
    wide_cols = round_up(3 * cols)
    text_rows = caption.shape[1]
    text_total = text_rows * 8
    attn_rows = w_attention.shape[0]
    z_at, x_at = lax.axis_index("z"), lax.axis_index("x")
    y_at, core_at = lax.axis_index("y"), lax.axis_index("core")
    seq_at = z_at * 2 + x_at
    clip_at = y_at * 2 + core_at
    owner = clip_at * 8 + seq_at
    place = jnp.stack([clip_at, z_at, x_at, y_at, core_at, seq_at]).astype(jnp.int32)

    line = Line()
    own_tokens = tokens[0]
    token_all = lax.all_gather(own_tokens, seq_axes, axis=0, tiled=True)

    cap_cols = w_caption.shape[0]
    hidden_own = w_down.shape[0]
    hidden = 4 * hidden_own
    cond_rows, span = w_modulation.shape
    bias_len = mod_bias.shape[0]
    gain_cols = norm_gains.shape[1]
    cond_square = condition.reshape(32, cond_rows)
    extra = jnp.concatenate(
        [
            jnp.pad(mod_bias[None], ((0, 31), (0, 256 - bias_len)))
            + jnp.pad(norm_gains, ((8, 17), (0, 256 - gain_cols))),
            jnp.pad(cond_square, ((0, 0), (0, 128 - cond_rows))),
        ],
        axis=1,
    )
    attn_piece, ffn_piece, cap_piece, mod_piece = alone(
        prep_body,
        [
            ((8, attn_rows, wide_cols), bf16),
            ((8, w_gateup.shape[0], 8 * hidden_own), bf16),
            ((32, text_rows, cap_cols), bf16),
            ((cond_rows, span + 384), bf16),
        ],
        w_attention,
        w_gateup,
        caption[0],
        w_modulation,
        extra,
    )
    mod_y, mod_core = flip(mod_piece, "y"), flip(mod_piece, "core")
    attn_0 = lax.all_to_all(attn_piece, seq_axes, 0, 0, tiled=True).reshape(-1, wide_cols)
    mod_piece, mod_y, mod_core, attn_0, cap_piece, ffn_piece = together(
        mod_piece, mod_y, mod_core, attn_0, cap_piece, ffn_piece
    )

    mod_parts = [mod_piece, mod_core, mod_y, flip(mod_y, "core")]
    attn_2, attn_1 = flip(attn_0, "y"), flip(attn_0, "core")
    cap_all = lax.all_to_all(cap_piece, all_axes, 0, 0, tiled=True)
    (small,) = line(
        modulate_body,
        [((32, 640), f32)],
        place,
        cond_square.astype(f32),
        *mod_parts,
        scalars=1,
    )
    vector, own_gains = line(
        vector_body,
        [((16, width), f32), ((256, 128), f32)],
        place,
        *seq_terms(small),
        scalars=1,
        scratch=[pltpu.VMEM((32, 640), f32), pltpu.VMEM((128, 256), f32)],
    )
    vector, attn_0, attn_1, attn_2, cap_all, ffn_piece, own_out, w_down = together(
        vector, attn_0, attn_1, attn_2, cap_all, ffn_piece, w_output, w_down
    )

    cap_all = cap_all.reshape(4, text_total, cap_cols)
    attn_3 = flip(attn_2, "core")
    four_text = (4, text_total, 2 * cols)
    cap_keep, cap_send = line(
        caption_body,
        [((2, 2) + four_text, bf16)] * 2,
        place,
        cap_all,
        w_caption,
        scalars=1,
    )
    out_near = swap_z(own_out, 1)
    own_down = lax.all_gather(w_down, "z", axis=0, tiled=True)
    ffn_piece = lax.all_to_all(ffn_piece, plane_axes, 0, 0, tiled=True)
    block = 2 * ffn_piece.shape[1]
    cap_keep, cap_send = line(
        add_pair_body, [((2,) + four_text, bf16)] * 2, cap_keep, flip(cap_send, "core")
    )
    attn_3, cap_send, cap_keep = together(attn_3, cap_send, cap_keep)

    attn_parts = (attn_0, attn_1, attn_2, attn_3)
    cap_send = flip(cap_send, "y")
    normed_all, projected, squares = line(
        qkv_body,
        [((total, width), bf16), ((wide_cols, total), f32), ((8, total), f32)],
        place,
        token_all,
        *attn_parts,
        vector,
        scalars=1,
    )
    squares = seq_terms(squares)
    (out_pair,) = line(
        stack_body, [((2 * attn_rows, width), bf16)], own_out, out_near, after=(squares[0],)
    )
    out_far = swap_z(out_pair, 2)
    cap_keep, cap_send = line(add_pair_body, [(four_text, bf16)] * 2, cap_keep, cap_send)
    cap_send = flip(cap_send, "x")
    text_parts = line(
        add_four_body, [(four_text[1:], bf16)] * 4, cap_keep, cap_send, after=tuple(squares[1:])
    )
    out_far, squares, text_parts, ffn_piece, own_down = together(
        out_far, squares, text_parts, ffn_piece, own_down
    )

    text_parts = [text_parts[0]] + [from_ahead(text_parts[4 - k], "z", k) for k in (1, 2, 3)]
    (out_z,) = line(stack_body, [((4 * attn_rows, width), bf16)], out_pair, out_far)
    out_x = flip(out_z, "x")

    head_low = lax.dynamic_slice_in_dim(head_gate, seq_at * own_heads, own_heads)
    tanh_gate = jnp.tanh(head_low.astype(f32))
    position = jnp.arange(total, dtype=jnp.int32)
    angles = rope_angles(frame_shape[0], rope_shift[0], position, head_dim // 2).T
    cosine = jnp.cos(angles)
    sine = jnp.sin(angles)
    flat = (cols, total)
    queries, key_rows, values, self_out, log_sum, squares = line(
        functools.partial(attend_body, own_heads),
        [
            (flat, bf16),
            (flat, bf16),
            (flat, bf16),
            (flat, f32),
            ((8, total), f32),
            ((8, total), f32),
        ],
        projected,
        *squares,
        own_gains,
        cosine,
        sine,
    )
    self_out, out_x, text_parts, ffn_piece = together(self_out, out_x, text_parts, ffn_piece)
    own_gateup = lax.all_gather(ffn_piece.reshape(4, block, -1), "z", axis=0)
    own_gateup = jnp.transpose(own_gateup, (1, 0, 2, 3)).reshape(width, -1)
    (out_0,) = line(stack_body, [((8 * attn_rows, width), bf16)], out_z, out_x)
    out_2 = flip(out_0, "y")

    text_proj, text_squares = line(
        text_body, [((2 * cols, text_total), f32), ((8, text_total), f32)], *text_parts
    )
    text_squares = seq_terms(text_squares)
    mixed_pieces, cross_out, text_keys, text_values, squares = line(
        functools.partial(cross_body, own_heads),
        [
            ((8, cols, rows), bf16),
            (flat, f32),
            ((cols, text_total), bf16),
            ((cols, text_total), bf16),
            ((8, total), f32),
        ],
        tanh_gate,
        caption_len,
        queries,
        self_out,
        text_proj,
        *text_squares,
        squares,
        own_gains,
        scalars=2,
    )
    mixed_pieces, out_2, out_0 = together(mixed_pieces, out_2, out_0)
    mixed_own = lax.all_to_all(mixed_pieces, seq_axes, 0, 0, tiled=True).reshape(width, rows)
    out_1, out_3 = flip(out_0, "core"), flip(out_2, "core")
    (full_out,) = line(
        output_weight_body,
        [((width, width), bf16)],
        place,
        out_0,
        out_1,
        out_2,
        out_3,
        scalars=1,
    )
    mixed_own, full_out = together(mixed_own, full_out)
    own_shape = (rows, width)
    attn_proj, residual, normed_ffn, mixed_plane = line(
        output_body,
        [
            (own_shape, f32),
            (own_shape, f32),
            (own_shape, bf16),
            ((8, 4 * attn_rows, rows), bf16),
        ],
        mixed_own,
        full_out,
        own_tokens,
        vector,
    )

    chip_shape = (4 * rows, width)
    on_way = [(own_shape, f32), (own_shape, f32), (own_shape, bf16), (own_shape, bf16)]
    normed_parts = gather_chips(normed_ffn)
    own_gateup = together(own_gateup, normed_parts[1], normed_parts[2])[0]
    gateups = (own_gateup, flip(own_gateup, "core"))
    own_down = together(own_down, normed_ffn)[0]
    downs = (own_down, flip(own_down, "core"))
    normed_ffn_all, gate_up, activated, *parts = line(
        feed_body,
        [
            (chip_shape, bf16),
            ((2, 4 * rows, 2 * hidden), f32),
            ((2, 4 * rows, hidden), bf16),
        ]
        + on_way,
        *normed_parts,
        *gateups,
        *downs,
    )
    block_out, grad_down, middle_sums = line(
        middle_body,
        [(own_shape, f32), (own_shape, bf16), ((8, width), f32)],
        *scatter_chips(line, *parts),
        residual,
        cotangent[0],
        vector,
    )

    grad_down_all, grad_gate_up, *parts = line(
        feed_back_body,
        [(chip_shape, bf16), ((2, 4 * rows, 2 * hidden), bf16)] + on_way,
        *gather_chips(grad_down),
        *gateups,
        *downs,
        gate_up,
    )

    def feed_weights():
        return line(
            down_weight_body, [((hidden, width), bf16)] * 2, activated, grad_down_all
        ) + line(
            gateup_weight_body,
            [((4, 4 * block, 2 * hidden), bf16)] * 2,
            normed_ffn_all,
            grad_gate_up,
        )

    ffn_parts = scatter_chips(line, *parts, feed_weights)
    down_own, down_other, gateup_own, gateup_other = feed_weights.grads
    (wgrad_down,) = line(
        add_body, [((hidden, width), bf16)], down_own, flip(down_other, "core")
    )
    wgrad_down = lax.psum_scatter(wgrad_down, "z", scatter_dimension=0, tiled=True)
    gateup_got = flip(gateup_other, "core")

    grad_residual, grad_attn, grad_mixed, residual_sums = line(
        residual_back_body,
        [(own_shape, f32), (own_shape, bf16), ((width, rows), bf16), ((8, width), f32)],
        *ffn_parts,
        residual,
        attn_proj,
        cotangent[0],
        vector,
        full_out,
    )
    grad_pieces = lax.all_to_all(grad_mixed.reshape(8, cols, rows), seq_axes, 0, 0, tiled=True)
    grad_by_x, grad_by_y = flip(grad_attn, "x"), flip(grad_attn, "y")
    (wgrad_gateup,) = line(
        add_body, [((4, 4 * block, 2 * hidden), bf16)], gateup_own, gateup_got
    )
    grad_pieces, grad_by_x, grad_by_y, mixed_plane, wgrad_down, wgrad_gateup = together(
        grad_pieces, grad_by_x, grad_by_y, mixed_plane, wgrad_down, wgrad_gateup
    )
    wgrad_gateup = lax.psum_scatter(wgrad_gateup, "z", scatter_dimension=0, tiled=False)
    mixed_plane = lax.all_to_all(mixed_plane, plane_axes, 0, 0, tiled=True)
    grad_far = flip(grad_by_y, "x")

    (
        grad_mixed,
        text_query,
        text_key_in,
        text_value_grad,
        text_stats,
        text_gain,
        gate_sum,
    ) = line(
        functools.partial(text_back_body, own_heads),
        [
            (flat, bf16),
            (flat, f32),
            ((cols, text_total), f32),
            ((cols, text_total), f32),
            ((8, text_total), f32),
            ((256, 128), f32),
            ((8, 128), f32),
        ],
        tanh_gate,
        caption_len,
        grad_pieces,
        queries,
        text_keys,
        text_values,
        cross_out,
        text_proj,
        squares,
        own_gains,
        scalars=2,
    )
    query_in, key_in, value_grad, means, own_gain_sums = line(
        functools.partial(attend_back_body, own_heads),
        [
            (flat, f32),
            (flat, f32),
            (flat, bf16),
            ((8, 8, total), f32),
            ((256, 128), f32),
        ],
        grad_mixed,
        queries,
        key_rows,
        values,
        self_out,
        log_sum,
        text_query,
        text_stats,
        projected,
        squares,
        own_gains,
        cosine,
        sine,
    )
    means, mixed_plane, grad_attn, grad_by_x, grad_by_y, grad_far = together(
        means, mixed_plane, grad_attn, grad_by_x, grad_by_y, grad_far
    )
    means = share(means)
    grad_attn_parts = [grad_attn, grad_by_x, grad_by_y, grad_far]
    grad_attn_parts = grad_attn_parts + [flip(piece, "core") for piece in grad_attn_parts]
    wgrad_parts = line(
        output_grad_body,
        [((attn_rows, width), bf16)] * 4,
        place,
        mixed_plane,
        *grad_attn_parts,
        scalars=1,
        far=8,
        scratch=[pltpu.VMEM((total, width), bf16), pltpu.SemaphoreType.DMA((8,))],
    )
    pack = (attn_rows + text_total * 2 * cols // width, width)
    packs = line(
        text_proj_back_body,
        [(pack, bf16)] * 4,
        text_key_in,
        text_value_grad,
        text_proj,
        squares,
        means,
        *wgrad_parts,
    )
    means, packs, wgrad_gateup = together(means, packs, wgrad_gateup)

    packs = [packs[0]] + [from_ahead(packs[4 - k], "z", k) for k in (1, 2, 3)]
    wgrad_gateup = lax.all_to_all(
        wgrad_gateup.reshape(8, block // 2, -1), plane_axes, 0, 0, tiled=True
    )
    quarter = width // 4
    grad_normed, near_part, far_part, sums = line(
        project_back_body,
        [((total, width), bf16)]
        + [((2, quarter, wide_cols), bf16)] * 2
        + [((8, 8, width), f32)],
        place,
        token_all,
        *attn_parts,
        query_in,
        key_in,
        value_grad,
        projected,
        squares,
        means,
        normed_all,
        vector,
        middle_sums,
        residual_sums,
        own_gain_sums,
        text_gain,
        gate_sum,
        scalars=1,
        scratch=[
            pltpu.VMEM((wide_cols, total), bf16),
            pltpu.VMEM((total, wide_cols), bf16),
            pltpu.VMEM((2 * rows, width), f32),
            pltpu.VMEM((8, width), f32),
        ],
    )
    grad_normed, far_part, sums, packs, wgrad_gateup = together(
        grad_normed, far_part, sums, packs, wgrad_gateup
    )

    grad_normed = lax.psum_scatter(grad_normed, seq_axes, scatter_dimension=0, tiled=True)
    (text_z,) = line(text_stack_body, [((4 * text_total, 2 * cols), bf16)], *packs)
    text_x = flip(text_z, "x")
    far_part = flip(far_part, "core")
    wide = (quarter, wide_cols)
    near_part, far_part = line(add_pair_body, [(wide, bf16)] * 2, near_part, far_part)
    far_part, text_x, sums = together(far_part, text_x, sums)

    far_part = flip(far_part, "y")
    sums = share(sums)
    (text_seq,) = line(stack_body, [((8 * text_total, 2 * cols), bf16)], text_z, text_x)
    (wgrad_gateup,) = line(gateup_grad_body, [(w_gateup.shape, f32)], wgrad_gateup)
    far_part, text_seq = together(far_part, text_seq)

    text_y, text_core = flip(text_seq, "y"), flip(text_seq, "core")
    (wgrad_attention,) = line(add_body, [(wide, bf16)], near_part, far_part)
    (shared,) = line(modulation_back_body, [((16, width), f32)], sums, vector)
    shared_y, shared_core = flip(shared, "y"), flip(shared, "core")
    wgrad_attention = together(wgrad_attention, sums)[0]
    wgrad_attention = lax.all_to_all(
        wgrad_attention.reshape(8, attn_rows, wide_cols), seq_axes, 0, 0, tiled=True
    )
    shared_y, shared_core, text_core, text_y = together(shared_y, shared_core, text_core, text_y)

    wgrad_modulation, shared, cond_back = line(
        modulation_weight_body,
        [(w_modulation.shape, f32), ((16, width), f32), ((4, 8, cap_cols), f32)],
        place,
        shared,
        shared_core,
        shared_y,
        flip(shared_y, "core"),
        *mod_parts,
        scalars=1,
        scratch=[pltpu.VMEM((128, 128), f32)],
    )
    wgrad_caption, cap_pieces = line(
        caption_back_body,
        [(w_caption.shape, f32), ((32, text_rows + 8, cap_cols), f32)],
        place,
        cap_all,
        text_seq,
        text_core,
        text_y,
        flip(text_y, "core"),
        w_caption,
        cond_back,
        scalars=1,
        scratch=[pltpu.VMEM((8, cap_cols, 2 * cols), f32)],
    )
    cap_pieces, wgrad_attention = together(cap_pieces, wgrad_attention)

    cap_pieces = lax.all_to_all(cap_pieces, all_axes, 0, 0, tiled=True)
    (wgrad_attention,) = line(attention_grad_body, [(w_attention.shape, f32)], wgrad_attention)
    (wgrad_output,) = line(output_sum_body, [((attn_rows, width), f32)], *packs)

    grad_caption, cond_back = line(
        caption_grad_body, [((text_rows, 32 * cap_cols), f32), ((32, cap_cols), f32)], cap_pieces
    )
    (grad_tokens,) = line(
        final_body, [(own_shape, f32)], grad_normed, grad_residual, own_tokens, vector
    )
    bias_grad = lax.dynamic_slice(shared, (clip_at, seq_at * bias_len), (1, bias_len))[0]
    gain_grads = lax.dynamic_slice(shared, (4, owner * gain_cols), (7, gain_cols))
    grad_gate_total = shared[11, :heads]
    cond_back = cond_back[:, :cond_rows].reshape(1, -1)
    cond_float = condition.astype(f32)
    cond_sigmoid = jax.nn.sigmoid(cond_float)
    grad_condition = cond_back * cond_sigmoid * (1.0 + cond_float * (1.0 - cond_sigmoid))

    return (
        block_out[None],
        grad_tokens[None],
        grad_caption[None],
        grad_condition,
        wgrad_modulation,
        bias_grad,
        wgrad_attention,
        wgrad_output,
        wgrad_caption,
        gain_grads,
        grad_gate_total,
        wgrad_gateup,
        wgrad_down.astype(f32),
    )


def specs(clip, seq):
    both = clip + seq
    placed = (
        P(clip, seq, None),
        P(clip, seq, None),
        P(clip, None),
        P(clip),
        P(clip, None),
        P(clip, None),
        P(both, None),
        P(both),
        P(both, None),
        P(both, None),
        P(both, None),
        P(None, both),
        P(),
        P(both, None),
        P(both, None),
        P(clip, seq, None),
    )
    given = (
        P(clip, seq, None),
        P(clip, seq, None),
        P(clip, seq, None),
        P(clip, None),
        P(both, None),
        P(both),
        P(both, None),
        P(both, None),
        P(both, None),
        P(None, both),
        P(),
        P(both, None),
        P(both, None),
    )
    return placed, given


def solution(mesh):
    if dict(mesh.shape) == {"clip": 4, "seq": 8}:
        grid = Mesh(mesh.devices.reshape(2, 2, 4, 2), ("y", "core", "z", "x"))
        placed, given = specs(("y", "core"), ("z", "x"))
        return jax.shard_map(
            local_fast, mesh=grid, in_specs=placed, out_specs=given, check_vma=False
        )
    placed, given = specs(("clip",), ("seq",))
    return jax.shard_map(local, mesh=mesh, in_specs=placed, out_specs=given, check_vma=False)
```
